32 devices in a mesh: row: 4 (over x, core), col: 8 (over z, y).
Axes of the slice: x: 2, y: 2, z: 4, core: 2. Of those that a mesh axis runs over, the one named last changes fastest.
Arguments:
- hidden: bfloat16 [2048, 8192], P('row', 'col'), may hold values from -600 to 600
- norm_gain: float32 [8192], replicated, may hold values from 0.5 to 2
- wq: bfloat16 [8192, 8192], P('row', 'col'), may hold values from -1 to 1
- wk: bfloat16 [8192, 1024], P('row', 'col'), may hold values from -1 to 1
- wv: bfloat16 [8192, 1024], P('row', 'col'), may hold values from -0.0625 to 0.0625
- wo: bfloat16 [8192, 8192], P('row', 'col'), may hold values from -0.25 to 0.25
Outputs:
- attn_out: bfloat16 [2048, 8192], P('row', 'col')
The draws below stay inside these ranges and needn't reach their ends.
All inputs are finite; a program needn't handle non-finite values.
Results may differ from the reference program's by a relative error of at most 0.011.
Values may be sent and summed in bfloat16 or wider, within the bound.
No kernel may reach another device: no remote copies, remote signals or barrier semaphores. Data moves between devices by JAX's collectives and lax.ppermute only.
A program may use at most 128 MiB of HBM per device.

```python
import math
import jax
import jax.numpy as jnp
from jax import lax

D = 8192
H = 64
KVH = 8
HD = 128
TOKENS = 2048


def draw_hidden(key, part):
    first, second = jax.random.split(jax.random.fold_in(key, 11), 2)
    normal = jax.random.truncated_normal(first, -6.0, 6.0, (TOKENS, D), jnp.float32)
    col_scale = jnp.exp(jax.random.uniform(second, (D,), jnp.float32, 0.0, math.log(10.0)))
    field = normal * col_scale[None, :]
    return field.astype(jnp.bfloat16)


def drawn_weight(key, salt, heads):
    normal = jax.random.truncated_normal(jax.random.fold_in(key, salt), -6.0, 6.0, (D, heads * HD), jnp.float32)
    weight = normal * D ** (-0.5)
    return weight


def draw_wq(key, part):
    return drawn_weight(key, 21, H).astype(jnp.bfloat16)


def draw_wk(key, part):
    return drawn_weight(key, 31, KVH).astype(jnp.bfloat16)


def level_of(key, dims, shards, least, high):
    loudness, own = 1.0, jax.random.fold_in(key, 6)
    for axis_at, parts in shards:
        draws = jnp.exp(jax.random.uniform(jax.random.fold_in(own, axis_at), (parts,), jnp.float32, least / len(shards), high / len(shards)))
        loudness = loudness * jnp.repeat(draws, dims[axis_at] // parts).reshape([-1 if axis == axis_at else 1 for axis in range(len(dims))])
    return loudness


def noise(stream_key, shape, spread, reach, pieces=(), kind=jnp.bfloat16):
    drawn = jax.random.normal(stream_key, shape, jnp.float32) * spread
    if len(pieces) > 0:
        drawn = level_of(stream_key, shape, pieces, -0.22, 0.18) * drawn
    return jnp.clip(drawn, min=-reach, max=reach).astype(kind)


def setup_inputs(seed: int = 0) -> dict:
    key_of = jax.random.split(jax.random.key(seed), 7)
    return {
        "hidden": draw_hidden(jax.random.fold_in(key_of[6], 71), 0),
        "norm_gain": jnp.clip(jnp.exp(jax.random.uniform(key_of[1], (D,), jnp.float32, math.log(0.5), math.log(2.0))), 0.5, 2.0),
        "wq": draw_wq(jax.random.fold_in(key_of[6], 71), 0),
        "wk": draw_wk(jax.random.fold_in(key_of[6], 71), 0),
        "wv": noise(key_of[4], (D, KVH * HD), D ** -0.5, 0.0625, ((0, 4), (1, 8))),
        "wo": noise(key_of[5], (H * HD, D), 0.035, 0.25, ((0, 4), (1, 8))),
    }


def rotary(field, positions):
    half = field.shape[-1] // 2
    steps = jnp.arange(half).astype(jnp.float32)
    freqs = 10000.0 ** (-steps / half)
    angles = positions.astype(jnp.float32)[:, None] * freqs[None, :]
    cosine = jnp.cos(angles)[:, None, :]
    sine = jnp.sin(angles)[:, None, :]
    first = field[..., :half]
    second = field[..., half:]
    return jnp.concatenate([first * cosine - second * sine, second * cosine + first * sine], axis=-1)

def reference(hidden, norm_gain, wq, wk, wv, wo):
    values_in = hidden.astype(jnp.float32)
    meansq = lax.optimization_barrier(jnp.mean(values_in * values_in, axis=1, keepdims=True))
    normed = (values_in * lax.rsqrt(meansq + 1e-05) * norm_gain).astype(jnp.bfloat16)
    qraw = jnp.dot(normed, wq, preferred_element_type=jnp.float32)
    kraw = jnp.dot(normed, wk, preferred_element_type=jnp.float32)
    vraw = jnp.dot(normed, wv, preferred_element_type=jnp.float32)
    positions = jnp.arange(TOKENS).astype(jnp.int32)
    queries = rotary(qraw.reshape(TOKENS, H, HD), positions).astype(jnp.bfloat16)
    keys = rotary(kraw.reshape(TOKENS, KVH, HD), positions).astype(jnp.bfloat16)
    values = vraw.reshape(TOKENS, KVH, HD).astype(jnp.bfloat16)
    per_kv = H // KVH
    query_groups = queries.reshape(TOKENS, KVH, per_kv, HD).transpose(1, 2, 0, 3)
    key_groups = keys.transpose(1, 0, 2)
    value_groups = values.transpose(1, 0, 2)
    visible = positions[:, None] >= positions[None, :]
    scale = HD ** (-0.5)

    def one_group(operands):
        query_block, key_block, value_block = operands
        scores = jnp.einsum('gtd,nd->gtn', query_block.astype(jnp.float32), key_block.astype(jnp.float32)) * scale
        scores = jnp.where(visible[None], scores, -jnp.inf)
        top = lax.optimization_barrier(jnp.max(scores, axis=2, keepdims=True))
        probs = jnp.exp(scores - top)
        total = lax.optimization_barrier(jnp.sum(probs, axis=2, keepdims=True))
        rounded = lax.optimization_barrier(probs.astype(jnp.bfloat16)).astype(jnp.float32)
        numer = jnp.einsum('gtn,nd->gtd', rounded, value_block.astype(jnp.float32))
        return (numer / total).astype(jnp.bfloat16)
    outputs = lax.map(one_group, (query_groups, key_groups, value_groups))
    heads = outputs.transpose(2, 0, 1, 3).reshape(TOKENS, H * HD)
    return jnp.dot(heads, wo, preferred_element_type=jnp.float32).astype(jnp.bfloat16)
```

```python
import functools
import math

import jax
import jax.numpy as jnp
from jax import lax
from jax.experimental import pallas as pl
from jax.experimental.pallas import tpu as pltpu
from jax.sharding import PartitionSpec as P

HD = 128
CHUNKS = 2
MIB = 1 << 20


def after(array, *earlier):
    return lax.optimization_barrier((array, *earlier))[0]


def swap(array, axis, mask):
    return lax.ppermute(array, axis, [(i, i ^ mask) for i in range(lax.axis_size(axis))])


def row_bits():
    return [1 << b for b in reversed(range((lax.axis_size("row")).bit_length() - 1))]


def gather_row(array):
    pieces = {0: array}
    for bit in row_bits():
        pieces.update({j ^ bit: swap(p, "row", bit) for j, p in list(pieces.items())})
    return [pieces[j] for j in range(len(pieces))]


def order_pair(mine, other, col_index, bit, axis_dim):
    upper = col_index // 2**bit % 2 == 1
    lower_part = jnp.where(upper, other, mine)
    upper_part = jnp.where(upper, mine, other)
    return jnp.concatenate([lower_part, upper_part], axis=axis_dim)


def ring_order(n):
    return list(range(0, n, 2)) + list(range(1, n, 2))[::-1]


def ring_source(c, hops, n):
    at = jnp.where(c % 2 == 0, c // 2, n - 1 - c // 2)
    at = (at - hops) % n
    return jnp.where(at < n // 2, 2 * at, 2 * (n - 1 - at) + 1)


def ring_gather(block):
    n = lax.axis_size("col")
    c = lax.axis_index("col")
    order = ring_order(n)
    up = [(order[i], order[(i + 1) % n]) for i in range(n)]
    down = [(b, a) for a, b in up]
    rows = block.shape[0] // 2
    halves = [block[:rows], block[rows:]]
    found = [(c, 0, halves[0]), (c, 1, halves[1])]
    chains = [[halves[0], halves[1]], [halves[0], halves[1]]]
    for hop in range(1, n // 2 + 1):
        for half in (0, 1):
            for way, perm in ((0, up), (1, down)):
                if hop == n // 2 and way != half:
                    continue
                got = lax.ppermute(chains[way][half], "col", perm)
                chains[way][half] = got
                found.append((ring_source(c, hop if way == 0 else -hop, n), half, got))
    return found


def project_kernel(parts, heads, tiles, a_ref, *refs):
    weights = refs[:parts]
    scale_ref, cos_ref, sin_ref, o_ref, acc = refs[parts:]
    step = pl.program_id(0)

    @pl.when(step == 0)
    def _():
        acc[...] = jnp.zeros_like(acc)

    for p in range(parts):

        @pl.when(step // tiles == p)
        def _():
            acc[...] += jnp.dot(a_ref[...], weights[p][...], preferred_element_type=jnp.float32)

    @pl.when(step == parts * tiles - 1)
    def _():
        for h in range(acc.shape[1] // HD):
            at = pl.ds(h * HD, HD)
            x = acc[:, at] * scale_ref[...]
            if h < heads:
                x = x * cos_ref[...] + pltpu.roll(x, HD // 2, 1) * sin_ref[...]
            o_ref[:, at] = x.astype(o_ref.dtype)


def project(panel, weights, scale, cos, sin, heads):
    tok, depth = panel.shape
    parts = len(weights)
    rows, cols = weights[0].shape
    tile = min(1024, rows)
    tiles = rows // tile
    full = lambda a: pl.BlockSpec(a.shape, lambda k: (0, 0))
    part = lambda p: pl.BlockSpec((tile, cols), lambda k: (jnp.clip(k - p * tiles, 0, tiles - 1), 0))
    return pl.pallas_call(
        functools.partial(project_kernel, parts, heads, tiles),
        grid=(parts * tiles,),
        in_specs=[pl.BlockSpec((tok, tile), lambda k: (0, k))]
        + [part(p) for p in range(parts)]
        + [full(scale), full(cos), full(sin)],
        out_specs=pl.BlockSpec((tok, cols), lambda k: (0, 0)),
        out_shape=jax.ShapeDtypeStruct((tok, cols), jnp.bfloat16),
        scratch_shapes=[pltpu.VMEM((tok, cols), jnp.float32)],
        compiler_params=pltpu.CompilerParams(
            dimension_semantics=("arbitrary",), vmem_limit_bytes=40 * MIB
        ),
        cost_estimate=pl.CostEstimate(
            flops=2 * tok * depth * cols,
            bytes_accessed=2 * (tok * depth + depth * cols + tok * cols),
            transcendentals=0,
        ),
    )(panel, *weights, scale, cos, sin)


def attend_kernel(parts, r_ref, q_ref, *refs):
    pieces = refs[:parts]
    o_ref, top, total, acc = refs[parts:]
    r = r_ref[0]
    q = q_ref[...]
    tok = q.shape[0]
    dims = (((1,), (1,)), ((), ()))

    s = lax.dot_general(q, pieces[0][:, :HD], dims, preferred_element_type=jnp.float32)
    row = lax.broadcasted_iota(jnp.int32, (tok, tok), 0)
    col = lax.broadcasted_iota(jnp.int32, (tok, tok), 1)
    s = jnp.where(row >= col, s, -jnp.inf)
    m = jnp.max(s, axis=1, keepdims=True)
    p = jnp.exp2(s - m)
    top[...] = m
    total[...] = jnp.sum(p, axis=1, keepdims=True)
    acc[...] = jnp.dot(p.astype(jnp.bfloat16), pieces[0][:, HD:], preferred_element_type=jnp.float32)
    for j in range(1, parts):

        @pl.when(jnp.bitwise_xor(r, j) < r)
        def _():
            s = lax.dot_general(q, pieces[j][:, :HD], dims, preferred_element_type=jnp.float32)
            m = jnp.maximum(top[...], jnp.max(s, axis=1, keepdims=True))
            keep = jnp.exp2(top[...] - m)
            p = jnp.exp2(s - m)
            top[...] = m
            total[...] = total[...] * keep + jnp.sum(p, axis=1, keepdims=True)
            acc[...] = acc[...] * keep + jnp.dot(
                p.astype(jnp.bfloat16), pieces[j][:, HD:], preferred_element_type=jnp.float32
            )

    o_ref[...] = (acc[...] / total[...]).astype(o_ref.dtype)


def attend(r, queries, pieces):
    tok, cols = queries.shape
    heads = cols // HD
    parts = len(pieces)
    return pl.pallas_call(
        functools.partial(attend_kernel, parts),
        grid_spec=pltpu.PrefetchScalarGridSpec(
            num_scalar_prefetch=1,
            grid=(heads,),
            in_specs=[pl.BlockSpec((tok, HD), lambda h, r: (0, h))]
            + [pl.BlockSpec((tok, 2 * HD), lambda h, r: (0, 0)) for _ in pieces],
            out_specs=pl.BlockSpec((tok, HD), lambda h, r: (0, h)),
            scratch_shapes=[
                pltpu.VMEM((tok, 1), jnp.float32),
                pltpu.VMEM((tok, 1), jnp.float32),
                pltpu.VMEM((tok, HD), jnp.float32),
            ],
        ),
        out_shape=jax.ShapeDtypeStruct((tok, cols), jnp.bfloat16),
        compiler_params=pltpu.CompilerParams(
            dimension_semantics=("arbitrary",), vmem_limit_bytes=32 * MIB
        ),
        cost_estimate=pl.CostEstimate(
            flops=4 * heads * tok * tok * parts * HD,
            bytes_accessed=4 * tok * cols + parts * 4 * tok * HD,
            transcendentals=heads * tok * tok * parts,
        ),
    )(r.reshape(1), queries, *pieces)


def finish_kernel(parts, chunks, *refs):
    panels = refs[:chunks]
    weights = refs[chunks : chunks + parts]
    o_ref, acc = refs[chunks + parts :]
    step = pl.program_id(0)
    steps = pl.num_programs(0)

    @pl.when(step == 0)
    def _():
        acc[...] = jnp.zeros_like(acc)

    for j in range(chunks):
        for p in range(parts):

            @pl.when(step // (steps // (chunks * parts)) == j * parts + p)
            def _():
                acc[...] += jnp.dot(
                    panels[j][...], weights[p][...], preferred_element_type=jnp.float32
                )

    @pl.when(step == steps - 1)
    def _():
        o_ref[...] = acc[...].astype(o_ref.dtype)


def finish(panels, weights, width):
    chunks, parts = len(panels), len(weights)
    tok, depth = panels[0].shape
    rows, cols = weights[0].shape
    per = rows // (width * chunks)
    span = per * parts

    def panel_spec(j):
        return pl.BlockSpec((tok, width), lambda k: (0, jnp.clip(k - j * span, 0, span - 1)))

    def weight_spec(p):
        def index(k):
            j, rest = k // span, k % span
            s = jnp.clip(rest - p * per, 0, per - 1)
            return (s * chunks + j, 0)

        return pl.BlockSpec((width, cols), index)

    return pl.pallas_call(
        functools.partial(finish_kernel, parts, chunks),
        grid=(chunks * span,),
        in_specs=[panel_spec(j) for j in range(chunks)] + [weight_spec(p) for p in range(parts)],
        out_specs=pl.BlockSpec((tok, cols), lambda k: (0, 0)),
        out_shape=jax.ShapeDtypeStruct((tok, cols), jnp.bfloat16),
        scratch_shapes=[pltpu.VMEM((tok, cols), jnp.float32)],
        compiler_params=pltpu.CompilerParams(
            dimension_semantics=("arbitrary",), vmem_limit_bytes=40 * MIB
        ),
        cost_estimate=pl.CostEstimate(
            flops=2 * tok * depth * chunks * cols,
            bytes_accessed=2 * (tok * depth * chunks + rows * parts * cols + tok * cols),
            transcendentals=0,
        ),
    )(*panels, *weights)


def per_device(hidden, norm_gain, wq, wk, wv, wo):
    tok, feat = hidden.shape
    n_row, n_col = lax.axis_size("row"), lax.axis_size("col")
    r, c = lax.axis_index("row"), lax.axis_index("col")
    depth = feat * n_col
    rows = wq.shape[0]
    cols = wq.shape[1]

    kv_cols = wk.shape[1]
    group = max(1, HD // kv_cols)
    stacked = jnp.stack((wk, wv), axis=1)
    for bit in range(group.bit_length() - 1):
        other = swap(stacked, "col", 1 << bit)
        stacked = order_pair(stacked, other, c, bit, 2)
    stacked = stacked.reshape(rows, 2 * HD)

    kv_weights = gather_row(stacked)
    wide = cols // CHUNKS
    q_weights = []
    last = kv_weights
    for j in range(CHUNKS):
        mine = wq[:, j * wide : (j + 1) * wide]
        if j > 0:
            mine = after(mine, *last)
        last = gather_row(mine)
        q_weights.append(last)
    o_weights = gather_row(after(wo, *last))

    panel = jnp.zeros((tok, depth), jnp.bfloat16)
    squares = [jnp.zeros((tok // 2, 1), jnp.float32) for _ in range(2)]
    for source, half, piece in ring_gather(hidden):
        wider = piece.astype(jnp.float32)
        squares[half] += jnp.sum(wider * wider, axis=1, keepdims=True)
        gain = lax.dynamic_slice(norm_gain, (source * feat,), (feat,))
        scaled = (wider * gain).astype(jnp.bfloat16)
        at = source * feat
        at = (at // rows ^ r) * rows + at % rows
        panel = lax.dynamic_update_slice(panel, scaled, (half * (tok // 2), at))
    meansq = jnp.concatenate(squares, axis=0) / depth
    scale = lax.rsqrt(meansq + 1e-05)

    half = HD // 2
    positions = r * tok + jnp.arange(tok)
    freqs = 10000.0 ** (-jnp.arange(half).astype(jnp.float32) / half)
    angles = positions.astype(jnp.float32)[:, None] * freqs[None, :]
    cosine, sine = jnp.cos(angles), jnp.sin(angles)
    cosine = jnp.concatenate([cosine, cosine], axis=1)
    sine = jnp.concatenate([-sine, sine], axis=1)
    factor = HD ** (-0.5) * math.log2(math.e)

    kv = project(panel, kv_weights, scale, cosine, sine, 1)
    kv_pieces = gather_row(kv)
    panels = []
    for j in range(CHUNKS):
        queries = project(panel, q_weights[j], scale, cosine * factor, sine * factor, wide // HD)
        heads = attend(r, queries, kv_pieces)
        gathered = jnp.zeros((tok, wide * n_col), jnp.bfloat16)
        for source, half, piece in ring_gather(heads):
            at = source * cols
            at = ((at // rows ^ r) * rows + at % rows) // CHUNKS
            gathered = lax.dynamic_update_slice(gathered, piece, (half * (tok // 2), at))
        panels.append(gathered)
    return finish(panels, o_weights, wide)


def solution(mesh):
    in_specs = (
        P("row", "col"),
        P(),
        P("row", "col"),
        P("row", "col"),
        P("row", "col"),
        P("row", "col"),
    )
    out_specs = P("row", "col")
    return jax.shard_map(
        per_device, mesh=mesh, in_specs=in_specs, out_specs=out_specs, check_vma=False
    )
```

```python
import functools
import math

import jax
import jax.numpy as jnp
from jax import lax
from jax.experimental import pallas as pl
from jax.experimental.pallas import tpu as pltpu
from jax.sharding import PartitionSpec as P

HD = 128
CHUNKS = 2
MIB = 1 << 20


def after(array, *earlier):
    if not earlier:
        return array
    return lax.optimization_barrier((array, *earlier))[0]


def swap(array, axis, mask):
    return lax.ppermute(array, axis, [(i, i ^ mask) for i in range(lax.axis_size(axis))])


def row_bits():
    return [1 << b for b in reversed(range((lax.axis_size("row")).bit_length() - 1))]


def exchange_row(array, *earlier):
    bit = row_bits()[0]
    return {0: array, bit: swap(after(array, *earlier), "row", bit)}


def gather_row(pieces, *earlier):
    pieces = dict(pieces)
    for bit in row_bits()[1:]:
        sent = {j: after(p, *earlier) if j > 0 else p for j, p in pieces.items()}
        pieces.update({j ^ bit: swap(p, "row", bit) for j, p in sent.items()})
    return [pieces[j] for j in range(len(pieces))]


def far(pieces):
    return pieces[row_bits()[0]]


def order_pair(mine, other, col_index, bit, axis_dim):
    upper = col_index // 2**bit % 2 == 1
    lower_part = jnp.where(upper, other, mine)
    upper_part = jnp.where(upper, mine, other)
    return jnp.concatenate([lower_part, upper_part], axis=axis_dim)


def ring_order(n):
    return list(range(0, n, 2)) + list(range(1, n, 2))[::-1]


def ring_source(c, hops, n):
    at = jnp.where(c % 2 == 0, c // 2, n - 1 - c // 2)
    at = (at - hops) % n
    return jnp.where(at < n // 2, 2 * at, 2 * (n - 1 - at) + 1)


def ring_gather(block, place, into, starts):
    n = lax.axis_size("col")
    c = lax.axis_index("col")
    order = ring_order(n)
    up = [(order[i], order[(i + 1) % n]) for i in range(n)]
    down = [(b, a) for a, b in up]
    rows = block.shape[0] // 2
    below = above = block
    into = place(into, c, 0, block)
    for hop in range(1, n // 2 + 1):
        if hop in starts:
            below, above = lax.optimization_barrier((below, above, *starts[hop]))[:2]
        if hop == n // 2:
            below, above = below[:rows], above[rows:]
        below = lax.ppermute(below, "col", up)
        above = lax.ppermute(above, "col", down)
        below, above = lax.optimization_barrier((below, above))
        into = place(into, ring_source(c, hop, n), 0, below)
        into = place(into, ring_source(c, -hop, n), rows if hop == n // 2 else 0, above)
    return into


def project_kernel(parts, heads, panel_ref, *refs):
    weights = refs[:parts]
    scale_ref, cos_ref, sin_ref, o_ref, a_buf, w_buf, acc, a_sem, w_sem = refs[parts:]
    slots, _, depth = panel_ref.shape
    per = slots // parts

    def a_copy(k):
        return pltpu.make_async_copy(panel_ref.at[k], a_buf.at[k], a_sem.at[k])

    def w_copy(k, p, s):
        return pltpu.make_async_copy(
            weights[p].at[pl.ds(s * depth, depth), :], w_buf.at[k], w_sem.at[k]
        )

    for p in range(parts):
        for s in range(per):
            a_copy(p * per + s).start()
            w_copy(p * per + s, p, s).start()
    acc[...] = jnp.zeros_like(acc)

    def body(k, carry):
        a_copy(k).wait()
        w_copy(k, 0, 0).wait()
        acc[...] += jnp.dot(a_buf[k], w_buf[k], preferred_element_type=jnp.float32)
        return carry

    lax.fori_loop(0, slots, body, 0)
    for h in range(acc.shape[1] // HD):
        at = pl.ds(h * HD, HD)
        x = acc[:, at] * scale_ref[...]
        if h < heads:
            x = x * cos_ref[...] + pltpu.roll(x, HD // 2, 1) * sin_ref[...]
        o_ref[:, at] = x.astype(o_ref.dtype)


def project(panel, weights, scale, cos, sin, heads):
    slots, tok, depth = panel.shape
    parts = len(weights)
    cols = weights[0].shape[1]
    hbm = pl.BlockSpec(memory_space=pl.ANY)
    vmem = pl.BlockSpec(memory_space=pltpu.VMEM)
    return pl.pallas_call(
        functools.partial(project_kernel, parts, heads),
        in_specs=[hbm] * (1 + parts) + [vmem] * 3,
        out_specs=vmem,
        out_shape=jax.ShapeDtypeStruct((tok, cols), jnp.bfloat16),
        scratch_shapes=[
            pltpu.VMEM((slots, tok, depth), jnp.bfloat16),
            pltpu.VMEM((slots, depth, cols), jnp.bfloat16),
            pltpu.VMEM((tok, cols), jnp.float32),
            pltpu.SemaphoreType.DMA((slots,)),
            pltpu.SemaphoreType.DMA((slots,)),
        ],
        compiler_params=pltpu.CompilerParams(vmem_limit_bytes=60 * MIB),
        cost_estimate=pl.CostEstimate(
            flops=2 * slots * tok * depth * cols,
            bytes_accessed=2 * (slots * depth * (tok + cols) + tok * cols),
            transcendentals=0,
        ),
    )(panel, *weights, scale, cos, sin)


def attend_kernel(parts, chunks, pair, r_ref, *refs):
    chunk_refs, pieces = refs[:chunks], refs[chunks : chunks + parts]
    o_ref, q_ref, turned, top, total, acc = refs[chunks + parts :]
    r = r_ref[0]
    tok = q_ref.shape[0]
    step = pl.program_id(0)
    per = pl.num_programs(0) // chunks
    for i in range(chunks):

        @pl.when(step // per == i)
        def _():
            q_ref[...] = chunk_refs[i][...]

    dims = (((1,), (1,)), ((), ()))

    @pl.when(step == 0)
    def _():
        for j in range(parts):
            turned[j] = pieces[j][:, HD:].T

    def scores(j, g):
        return lax.dot_general(
            pieces[j][:, :HD],
            q_ref[:, g * HD : (g + 1) * HD],
            dims,
            preferred_element_type=jnp.float32,
        )

    key = lax.broadcasted_iota(jnp.int32, (tok, tok), 0)
    query = lax.broadcasted_iota(jnp.int32, (tok, tok), 1)
    for g in range(pair):
        s = jnp.where(key <= query, scores(0, g), -jnp.inf)
        m = jnp.max(s, axis=0, keepdims=True)
        p = jnp.exp2(s - m)
        top[g] = m
        total[g] = jnp.sum(p, axis=0, keepdims=True)
        acc[g] = jnp.dot(turned[0], p.astype(jnp.bfloat16), preferred_element_type=jnp.float32)
    for j in range(1, parts):

        @pl.when(jnp.bitwise_xor(r, j) < r)
        def _():
            for g in range(pair):
                s = scores(j, g)
                m = jnp.maximum(top[g], jnp.max(s, axis=0, keepdims=True))
                keep = jnp.exp2(top[g] - m)
                p = jnp.exp2(s - m)
                top[g] = m
                total[g] = total[g] * keep + jnp.sum(p, axis=0, keepdims=True)
                acc[g] = acc[g] * keep + jnp.dot(
                    turned[j], p.astype(jnp.bfloat16), preferred_element_type=jnp.float32
                )

    for g in range(pair):
        o_ref[:, g * HD : (g + 1) * HD] = (acc[g] / total[g]).T.astype(o_ref.dtype)


def attend(r, queries, pieces):
    tok, cols = queries[0].shape
    chunks, parts = len(queries), len(pieces)
    pair = 2 if cols // HD % 2 == 0 else 1
    per = cols // (HD * pair)
    heads = chunks * cols // HD

    def query_spec(i):
        return pl.BlockSpec((tok, pair * HD), lambda h, r: (0, jnp.clip(h - i * per, 0, per - 1)))

    return pl.pallas_call(
        functools.partial(attend_kernel, parts, chunks, pair),
        grid_spec=pltpu.PrefetchScalarGridSpec(
            num_scalar_prefetch=1,
            grid=(chunks * per,),
            in_specs=[query_spec(i) for i in range(chunks)]
            + [pl.BlockSpec((tok, 2 * HD), lambda h, r: (0, 0)) for _ in pieces],
            out_specs=pl.BlockSpec((tok, pair * HD), lambda h, r: (0, h)),
            scratch_shapes=[
                pltpu.VMEM((tok, pair * HD), jnp.bfloat16),
                pltpu.VMEM((parts, HD, tok), jnp.bfloat16),
                pltpu.VMEM((pair, 1, tok), jnp.float32),
                pltpu.VMEM((pair, 1, tok), jnp.float32),
                pltpu.VMEM((pair, HD, tok), jnp.float32),
            ],
        ),
        out_shape=jax.ShapeDtypeStruct((tok, chunks * cols), jnp.bfloat16),
        compiler_params=pltpu.CompilerParams(
            dimension_semantics=("arbitrary",), vmem_limit_bytes=32 * MIB
        ),
        cost_estimate=pl.CostEstimate(
            flops=4 * heads * tok * tok * parts * HD,
            bytes_accessed=4 * tok * heads * HD + parts * 4 * tok * HD,
            transcendentals=heads * tok * tok * parts,
        ),
    )(r.reshape(1), *queries, *pieces)


def finish_kernel(parts, panel_ref, *refs):
    weights = refs[:parts]
    o_ref, a_buf, w_buf, acc, a_sem, w_sem = refs[-6:]
    slots, _, depth = panel_ref.shape
    per = slots // parts

    def a_copy(k):
        return pltpu.make_async_copy(panel_ref.at[k], a_buf.at[k], a_sem.at[k])

    def w_copy(k, p, s):
        return pltpu.make_async_copy(
            weights[p].at[pl.ds(s * depth, depth), :], w_buf.at[k], w_sem.at[k]
        )

    for p in range(parts):
        for s in range(per):
            a_copy(p * per + s).start()
            w_copy(p * per + s, p, s).start()
    acc[...] = jnp.zeros_like(acc)

    def body(k, carry):
        a_copy(k).wait()
        w_copy(k, 0, 0).wait()
        acc[...] += jnp.dot(a_buf[k], w_buf[k], preferred_element_type=jnp.float32)
        return carry

    lax.fori_loop(0, slots, body, 0)
    o_ref[...] = acc[...].astype(o_ref.dtype)


def finish(panel, weights, chunk, result=None):
    slots, tok, depth = panel.shape
    parts = len(weights)
    cols = weights[0].shape[1]
    hbm = pl.BlockSpec(memory_space=pl.ANY)
    old = [] if result is None else [result]
    return pl.pallas_call(
        functools.partial(finish_kernel, parts),
        grid=(1,),
        in_specs=[hbm] * (1 + parts + len(old)),
        out_specs=pl.BlockSpec((tok, cols), lambda i: (0, chunk)),
        out_shape=jax.ShapeDtypeStruct((tok, CHUNKS * cols), jnp.bfloat16),
        input_output_aliases={1 + parts: 0} if old else {},
        scratch_shapes=[
            pltpu.VMEM((slots, tok, depth), jnp.bfloat16),
            pltpu.VMEM((slots, depth, cols), jnp.bfloat16),
            pltpu.VMEM((tok, cols), jnp.float32),
            pltpu.SemaphoreType.DMA((slots,)),
            pltpu.SemaphoreType.DMA((slots,)),
        ],
        compiler_params=pltpu.CompilerParams(vmem_limit_bytes=60 * MIB),
        cost_estimate=pl.CostEstimate(
            flops=2 * slots * tok * depth * cols,
            bytes_accessed=2 * (slots * depth * (tok + cols) + tok * cols),
            transcendentals=0,
        ),
    )(panel, *weights, *old)


def per_device(hidden, norm_gain, wq, wk, wv, wo):
    tok, feat = hidden.shape
    n_row, n_col = lax.axis_size("row"), lax.axis_size("col")
    r, c = lax.axis_index("row"), lax.axis_index("col")
    depth = feat * n_col
    rows = wq.shape[0]
    cols = wq.shape[1]

    kv_cols = wk.shape[1]
    group = max(1, HD // kv_cols)
    stacked = jnp.stack((wk, wv), axis=1)
    for bit in range(group.bit_length() - 1):
        other = swap(stacked, "col", 1 << bit)
        stacked = order_pair(stacked, other, c, bit, 2)
    stacked = stacked.reshape(rows, 2 * HD)

    wide = cols // CHUNKS
    kv_parts = exchange_row(stacked)
    q_parts = []
    earlier = far(kv_parts)
    for j in range(CHUNKS):
        q_parts.append(exchange_row(wq[:, j * wide : (j + 1) * wide], earlier))
        earlier = far(q_parts[-1])

    per = rows // feat

    def slot_of(source):
        return (source // per ^ r) * per + source % per

    def put(into, source, first, piece):
        return lax.dynamic_update_slice(into, piece[None], (slot_of(source), first, 0))

    wider = hidden.astype(jnp.float32)
    squares = lax.psum(jnp.sum(wider * wider, axis=1, keepdims=True), "col")
    scale = lax.rsqrt(squares / depth + 1e-05)
    gain = lax.dynamic_slice(norm_gain, (c * feat,), (feat,))
    scaled = (wider * gain).astype(jnp.bfloat16)
    panel = jnp.zeros((n_col, tok, feat), jnp.bfloat16)
    panel = ring_gather(scaled, put, panel, {2: [far(kv_parts)]})

    half = HD // 2
    positions = r * tok + jnp.arange(tok)
    freqs = 10000.0 ** (-jnp.arange(half).astype(jnp.float32) / half)
    angles = positions.astype(jnp.float32)[:, None] * freqs[None, :]
    cosine, sine = jnp.cos(angles), jnp.sin(angles)
    cosine = jnp.concatenate([cosine, cosine], axis=1)
    sine = jnp.concatenate([-sine, sine], axis=1)
    factor = HD ** (-0.5) * math.log2(math.e)

    kv = project(panel, gather_row(kv_parts), scale, cosine, sine, 1)
    kv_own = exchange_row(kv)
    kv_pieces = gather_row(kv_own)
    scale = after(scale, kv)
    queries = []
    for j in range(CHUNKS):
        weights = gather_row(q_parts[j], *queries)
        queries.append(
            project(panel, weights, scale, cosine * factor, sine * factor, wide // HD)
        )
    heads = attend(r, queries, kv_pieces)

    o_parts = []
    earlier = far(kv_own)
    for j in range(CHUNKS):
        o_parts.append(exchange_row(wo[:, j * wide : (j + 1) * wide], earlier))
        earlier = far(o_parts[-1])
    gathered = jnp.zeros((n_col, tok, cols), jnp.bfloat16)
    gathered = ring_gather(heads, put, gathered, {})
    result = None
    for j in range(CHUNKS):
        weights = gather_row(o_parts[j], *([gathered] if j > 0 else []))
        result = finish(gathered, weights, j, result)
    return result


def solution(mesh):
    in_specs = (
        P("row", "col"),
        P(),
        P("row", "col"),
        P("row", "col"),
        P("row", "col"),
        P("row", "col"),
    )
    out_specs = P("row", "col")
    return jax.shard_map(
        per_device, mesh=mesh, in_specs=in_specs, out_specs=out_specs, check_vma=False
    )
```

```python
import functools
import math

import jax
import jax.numpy as jnp
from jax import lax
from jax.experimental import pallas as pl
from jax.experimental.pallas import tpu as pltpu
from jax.sharding import PartitionSpec as P

HD = 128
MIB = 1 << 20


def after(array, *earlier):
    if not earlier:
        return array
    return lax.optimization_barrier((array, *earlier))[0]


def swap(array, axis, mask):
    return lax.ppermute(array, axis, [(i, i ^ mask) for i in range(lax.axis_size(axis))])


def row_bits():
    return [1 << b for b in reversed(range((lax.axis_size("row")).bit_length() - 1))]


def exchange(array, *earlier):
    return swap(after(array, *earlier), "row", row_bits()[0])


def gather_near(array, *earlier):
    pieces = {0: after(array, *earlier)}
    for bit in row_bits()[1:]:
        pieces.update({j ^ bit: swap(p, "row", bit) for j, p in pieces.items()})
    return [pieces[j] for j in range(len(pieces))]


def order_pair(mine, other, col_index, bit, axis_dim):
    upper = col_index // 2**bit % 2 == 1
    lower_part = jnp.where(upper, other, mine)
    upper_part = jnp.where(upper, mine, other)
    return jnp.concatenate([lower_part, upper_part], axis=axis_dim)


def ring_order(n):
    return list(range(0, n, 2)) + list(range(1, n, 2))[::-1]


def ring_source(c, hops, n):
    at = jnp.where(c % 2 == 0, c // 2, n - 1 - c // 2)
    at = (at - hops) % n
    return jnp.where(at < n // 2, 2 * at, 2 * (n - 1 - at) + 1)


class Ring:
    def __init__(self, block):
        n = lax.axis_size("col")
        order = ring_order(n)
        self.n, self.hops = n, 0
        self.up = [(order[i], order[(i + 1) % n]) for i in range(n)]
        self.down = [(b, a) for a, b in self.up]
        self.found = [(lax.axis_index("col"), 0, block)]
        self.last = [block, block]

    def hop(self, *earlier, beside=()):
        if self.hops == self.n // 2:
            return beside
        c, own = self.found[0][0], self.found[0][2]
        rows = own.shape[0] // 2
        self.hops += 1
        end = self.hops == self.n // 2
        below, above = self.last
        if end:
            below, above = below[:rows], above[rows:]
        if earlier:
            below, above = lax.optimization_barrier((below, above, *earlier))[:2]
        below = lax.ppermute(below, "col", self.up)
        above = lax.ppermute(above, "col", self.down)
        below, above, *beside = lax.optimization_barrier((below, above, *beside))
        self.last = [below, above]
        self.found.append((ring_source(c, self.hops, self.n), 0, self.last[0]))
        self.found.append((ring_source(c, -self.hops, self.n), rows if end else 0, self.last[1]))
        return beside


class Panel:
    def __init__(self, slots_ref, rings, buffer, sems):
        self.slots_ref, self.rings, self.buffer, self.sems = slots_ref, rings, buffer, sems
        widths = [blocks[0].shape[1] for blocks in rings]
        self.firsts = [sum(widths[:i]) for i in range(len(rings))]

    def copy(self, ring, i):
        ref = self.rings[ring][i]
        rows, cols = ref.shape
        n = len(self.rings[ring])
        slot = self.slots_ref[i]
        first = rows if i == n - 1 else 0
        sem = n - 1 if i == n - 1 else slot
        into = self.buffer.at[slot, pl.ds(first, rows), pl.ds(self.firsts[ring], cols)]
        return pltpu.make_async_copy(ref, into, self.sems.at[ring, sem])

    def start(self):
        for ring, blocks in enumerate(self.rings):
            for i in reversed(range(len(blocks))):
                self.copy(ring, i).start()

    def wait_far(self):
        for ring, blocks in enumerate(self.rings):
            for i in (len(blocks) - 2, len(blocks) - 1):
                self.copy(ring, i).wait()

    def wait(self, k):
        for ring, blocks in enumerate(self.rings):
            rows, cols = blocks[0].shape
            into = self.buffer.at[k, :, pl.ds(self.firsts[ring], cols)]

            @pl.when(k != self.slots_ref[len(blocks) - 1])
            def _():
                pltpu.make_async_copy(blocks[0], into, self.sems.at[ring, k]).wait()


class Weights:
    def __init__(self, near, far, first, buffer, sems):
        self.near, self.far, self.first = near, far, first
        self.buffer, self.sems = buffer, sems

    def start(self, k):
        slots, depth, cols = self.buffer.shape
        per = slots // (len(self.near) + len(self.far))
        p, rows = k // per, pl.ds(k % per * depth, depth)
        if p < len(self.near):
            sources = [self.near[p].at[rows, pl.ds(self.first, cols)]]
        else:
            sources = [ref.at[rows, :] for ref in self.far[p - len(self.near)]]
        at = 0
        for source in sources:
            wide = source.shape[1]
            into = self.buffer.at[k, :, pl.ds(at, wide)]
            pltpu.make_async_copy(source, into, self.sems.at[k]).start()
            at += wide

    def wait(self, k):
        into = self.buffer.at[k]
        pltpu.make_async_copy(into, into, self.sems.at[k]).wait()


def multiply(panel, weights, acc):
    slots = weights.buffer.shape[0]
    panel.start()
    for k in range(slots):
        weights.start(k)
    acc[...] = jnp.zeros_like(acc)
    panel.wait_far()

    def body(k, carry):
        panel.wait(k)
        weights.wait(k)
        acc[...] += jnp.dot(
            panel.buffer[k], weights.buffer[k], preferred_element_type=jnp.float32
        )
        return carry

    lax.fori_loop(0, slots, body, 0)


def take(refs, *counts):
    out, at = [], 0
    for n in counts:
        out.append(refs[at : at + n])
        at += n
    return *out, refs[at:]


def stacked_weights(refs, near, far, first, buffer, sems):
    chunks = (len(refs) - near) // far
    return Weights(
        refs[:near],
        [refs[near + i * chunks : near + (i + 1) * chunks] for i in range(far)],
        first,
        buffer,
        sems,
    )


def project_kernel(n_blocks, near, far, count, first, heads, factor, slots_ref, *refs):
    blocks, weights, (scale_ref, cos_ref, sin_ref), rest = take(refs, n_blocks, count, 3)
    o_ref, w_buf, acc, panel_buf, panel_sem, sems = rest
    panel = Panel(slots_ref, [blocks], panel_buf, panel_sem)
    multiply(panel, stacked_weights(weights, near, far, first, w_buf, sems), acc)
    scale = scale_ref[...] * factor
    for h in range(acc.shape[1] // HD):
        at = pl.ds(h * HD, HD)
        x = acc[:, at] * scale
        if h < heads:
            x = x * cos_ref[...] + pltpu.roll(x, HD // 2, 1) * sin_ref[...]
        o_ref[:, at] = x.astype(o_ref.dtype)


def project(found, slots, near, far, first, heads, factor, scale, cos, sin):
    blocks = [piece for _, _, piece in found]
    tok, depth = blocks[0].shape
    count = len(blocks) - 1
    weights = [*near, *[w for chunks in far for w in chunks]]
    cols = sum(w.shape[1] for w in far[0])
    hbm = pl.BlockSpec(memory_space=pl.ANY)
    vmem = pl.BlockSpec(memory_space=pltpu.VMEM)
    return pl.pallas_call(
        functools.partial(
            project_kernel, len(blocks), len(near), len(far), len(weights), first, heads, factor
        ),
        in_specs=[pl.BlockSpec(memory_space=pltpu.SMEM)]
        + [hbm] * (len(blocks) + len(weights))
        + [vmem] * 3,
        out_specs=vmem,
        out_shape=jax.ShapeDtypeStruct((tok, cols), jnp.bfloat16),
        scratch_shapes=[
            pltpu.VMEM((count, depth, cols), jnp.bfloat16),
            pltpu.VMEM((tok, cols), jnp.float32),
            pltpu.VMEM((count, tok, depth), jnp.bfloat16),
            pltpu.SemaphoreType.DMA((1, count + 1)),
            pltpu.SemaphoreType.DMA((count,)),
        ],
        compiler_params=pltpu.CompilerParams(vmem_limit_bytes=60 * MIB),
        cost_estimate=pl.CostEstimate(
            flops=2 * count * tok * depth * cols,
            bytes_accessed=2 * (count * depth * (tok + cols) + tok * cols),
            transcendentals=0,
        ),
    )(slots, *blocks, *weights, scale, cos, sin)


def attend_kernel(parts, chunks, pair, r_ref, *refs):
    chunk_refs, pieces = refs[:chunks], refs[chunks : chunks + parts]
    o_ref, q_ref, turned, top, total, acc = refs[chunks + parts :]
    r = r_ref[0]
    tok = q_ref.shape[0]
    step = pl.program_id(0)
    per = pl.num_programs(0) // chunks
    for i in range(chunks):

        @pl.when(step // per == i)
        def _():
            q_ref[...] = chunk_refs[i][...]

    dims = (((1,), (1,)), ((), ()))

    @pl.when(step == 0)
    def _():
        for j in range(parts):
            turned[j] = pieces[j][:, HD:].T

    def scores(j, g):
        return lax.dot_general(
            pieces[j][:, :HD],
            q_ref[:, g * HD : (g + 1) * HD],
            dims,
            preferred_element_type=jnp.float32,
        )

    key = lax.broadcasted_iota(jnp.int32, (tok, tok), 0)
    query = lax.broadcasted_iota(jnp.int32, (tok, tok), 1)
    for g in range(pair):
        s = jnp.where(key <= query, scores(0, g), -jnp.inf)
        m = jnp.max(s, axis=0, keepdims=True)
        p = jnp.exp2(s - m)
        top[g] = m
        total[g] = jnp.sum(p, axis=0, keepdims=True)
        acc[g] = jnp.dot(turned[0], p.astype(jnp.bfloat16), preferred_element_type=jnp.float32)
    for j in range(1, parts):

        @pl.when(jnp.bitwise_xor(r, j) < r)
        def _():
            for g in range(pair):
                s = scores(j, g)
                m = jnp.maximum(top[g], jnp.max(s, axis=0, keepdims=True))
                keep = jnp.exp2(top[g] - m)
                p = jnp.exp2(s - m)
                top[g] = m
                total[g] = total[g] * keep + jnp.sum(p, axis=0, keepdims=True)
                acc[g] = acc[g] * keep + jnp.dot(
                    turned[j], p.astype(jnp.bfloat16), preferred_element_type=jnp.float32
                )

    for g in range(pair):
        o_ref[:, g * HD : (g + 1) * HD] = (acc[g] / total[g]).T.astype(o_ref.dtype)


def attend(r, queries, pieces):
    tok, cols = queries[0].shape
    chunks, parts = len(queries), len(pieces)
    pair = 2 if cols // HD % 2 == 0 else 1
    per = cols // (HD * pair)
    heads = chunks * cols // HD

    def query_spec(i):
        return pl.BlockSpec((tok, pair * HD), lambda h, r: (0, jnp.clip(h - i * per, 0, per - 1)))

    return pl.pallas_call(
        functools.partial(attend_kernel, parts, chunks, pair),
        grid_spec=pltpu.PrefetchScalarGridSpec(
            num_scalar_prefetch=1,
            grid=(chunks * per,),
            in_specs=[query_spec(i) for i in range(chunks)]
            + [pl.BlockSpec((tok, 2 * HD), lambda h, r: (0, 0)) for _ in pieces],
            out_specs=pl.BlockSpec((tok, pair * HD), lambda h, r: (0, h)),
            scratch_shapes=[
                pltpu.VMEM((tok, pair * HD), jnp.bfloat16),
                pltpu.VMEM((parts, HD, tok), jnp.bfloat16),
                pltpu.VMEM((pair, 1, tok), jnp.float32),
                pltpu.VMEM((pair, 1, tok), jnp.float32),
                pltpu.VMEM((pair, HD, tok), jnp.float32),
            ],
        ),
        out_shape=jax.ShapeDtypeStruct((tok, chunks * cols), jnp.bfloat16),
        compiler_params=pltpu.CompilerParams(
            dimension_semantics=("arbitrary",), vmem_limit_bytes=32 * MIB
        ),
        cost_estimate=pl.CostEstimate(
            flops=4 * heads * tok * tok * parts * HD,
            bytes_accessed=4 * tok * heads * HD + parts * 4 * tok * HD,
            transcendentals=heads * tok * tok * parts,
        ),
    )(r.reshape(1), *queries, *pieces)


def finish_kernel(n_blocks, rings, near, far, count, first, slots_ref, *refs):
    blocks, weights, rest = take(refs, n_blocks * rings, count)
    o_ref, w_buf, acc, panel_buf, panel_sem, sems = rest[-6:]
    by_ring = [blocks[i * n_blocks : (i + 1) * n_blocks] for i in range(rings)]
    panel = Panel(slots_ref, by_ring, panel_buf, panel_sem)
    multiply(panel, stacked_weights(weights, near, far, first, w_buf, sems), acc)
    o_ref[...] = acc[...].astype(o_ref.dtype)


def finish(rings, slots, near, far, first, total, result=None):
    blocks = [piece for found in rings for _, _, piece in found]
    n_blocks = len(rings[0])
    tok = blocks[0].shape[0]
    depth = sum(found[0][2].shape[1] for found in rings)
    count = n_blocks - 1
    weights = [*near, *[w for chunks in far for w in chunks]]
    cols = sum(w.shape[1] for w in far[0])
    hbm = pl.BlockSpec(memory_space=pl.ANY)
    old = [] if result is None else [result]
    return pl.pallas_call(
        functools.partial(
            finish_kernel, n_blocks, len(rings), len(near), len(far), len(weights), first
        ),
        grid=(1,),
        in_specs=[pl.BlockSpec(memory_space=pltpu.SMEM)]
        + [hbm] * (len(blocks) + len(weights) + len(old)),
        out_specs=pl.BlockSpec((tok, cols), lambda i: (0, first // cols)),
        out_shape=jax.ShapeDtypeStruct((tok, total), jnp.bfloat16),
        input_output_aliases={1 + len(blocks) + len(weights): 0} if old else {},
        scratch_shapes=[
            pltpu.VMEM((count, depth, cols), jnp.bfloat16),
            pltpu.VMEM((tok, cols), jnp.float32),
            pltpu.VMEM((count, tok, depth), jnp.bfloat16),
            pltpu.SemaphoreType.DMA((len(rings), count + 1)),
            pltpu.SemaphoreType.DMA((count,)),
        ],
        compiler_params=pltpu.CompilerParams(vmem_limit_bytes=60 * MIB),
        cost_estimate=pl.CostEstimate(
            flops=2 * count * tok * depth * cols,
            bytes_accessed=2 * (count * depth * (tok + cols) + tok * cols),
            transcendentals=0,
        ),
    )(slots, *blocks, *weights, *old)


def per_device(hidden, norm_gain, wq, wk, wv, wo):
    tok, feat = hidden.shape
    n_row, n_col = lax.axis_size("row"), lax.axis_size("col")
    r, c = lax.axis_index("row"), lax.axis_index("col")
    depth = feat * n_col
    rows = wq.shape[0]
    cols = wq.shape[1]

    kv_cols = wk.shape[1]
    group = max(1, HD // kv_cols)
    stacked = jnp.stack((wk, wv), axis=1)
    for bit in range(group.bit_length() - 1):
        other = swap(stacked, "col", 1 << bit)
        stacked = order_pair(stacked, other, c, bit, 2)
    stacked = stacked.reshape(rows, 2 * HD)

    unit = cols // HD // 4
    late = max(1, unit) * HD
    early = cols - late
    sizes = [n * HD for n in (unit, unit, unit // 2, unit - unit // 2) if n > 0] or [early]

    def early_chunk(i):
        return wq[:, sum(sizes[:i]) : sum(sizes[: i + 1])]

    per = rows // feat
    wider = hidden.astype(jnp.float32)
    gain = lax.dynamic_slice(norm_gain, (c * feat,), (feat,))
    squares = jnp.sum(wider * wider, axis=1)
    for bit in range(n_col.bit_length() - 1):
        squares += swap(squares, "col", 1 << bit)
    kv_near, q_near = gather_near(stacked), gather_near(wq)
    ring = Ring((wider * gain).astype(jnp.bfloat16))
    kv_other, squares = ring.hop(beside=[exchange(stacked), squares])
    q_other = []
    last = kv_other
    ties = [[*kv_near, *q_near], gather_near(kv_other)]
    for i in range(n_col // 2 - 1):
        beside = [exchange(early_chunk(i), last)] if i < len(sizes) else []
        beside = ring.hop(*(ties[i] if i < len(ties) else []), beside=beside)
        q_other += beside
        last = q_other[-1]
        if i == 0:
            o_near = gather_near(wo, *ring.last)
            ties.append(o_near)
    for i in range(len(q_other), len(sizes)):
        q_other.append(exchange(early_chunk(i), q_other[-1]))
    kv_far = ties[1]
    found = ring.found
    slots = jnp.stack([(source // per ^ r) * per + source % per for source, _, _ in found])
    scale = lax.rsqrt(squares / depth + 1e-05)[:, None]

    half = HD // 2
    positions = r * tok + jnp.arange(tok)
    freqs = 10000.0 ** (-jnp.arange(half).astype(jnp.float32) / half)
    angles = positions.astype(jnp.float32)[:, None] * freqs[None, :]
    cosine, sine = jnp.cos(angles), jnp.sin(angles)
    cosine = jnp.concatenate([cosine, cosine], axis=1)
    sine = jnp.concatenate([-sine, sine], axis=1)
    factor = HD ** (-0.5) * math.log2(math.e)

    kv_far = [[w] for w in kv_far]
    kv = project(found, slots, kv_near, kv_far, 0, 1, 1.0, scale, cosine, sine)
    kv_other = exchange(kv)
    last_other = exchange(wq[:, early:], kv_other)
    kv_pieces = [*gather_near(kv), *gather_near(kv_other)]
    scale = after(scale, kv)
    ended = len(q_other) - 1
    q_far = [gather_near(w, *([kv] if i == ended else [])) for i, w in enumerate(q_other)]
    q_far = list(zip(*q_far))
    queries = project(
        found, slots, q_near, q_far, 0, early // HD, factor, scale, cosine, sine
    )
    heads = attend(r, [queries], kv_pieces)

    o_other = exchange(wo[:, :early], last_other, heads)
    o_last_other = exchange(wo[:, early:], o_other)
    ring = Ring(heads)
    ring.hop()
    q_far = [[w] for w in gather_near(last_other, heads)]
    scale = after(scale, *ring.last)
    ring.hop()
    queries = project(
        found, slots, q_near, q_far, early, late // HD, factor, scale, cosine, sine
    )
    last_ring = Ring(attend(r, [queries], kv_pieces))
    for _ in range(n_col // 2):
        arrived = ring.last
        ring.hop(*last_ring.last)
        last_ring.hop(*arrived)

    rings = [ring.found, last_ring.found]
    o_far = [[w] for w in gather_near(o_other, ring.last[1])]
    result = finish(rings, slots, o_near, o_far, 0, cols)
    o_far = [[w] for w in gather_near(o_last_other, result)]
    return finish(rings, slots, o_near, o_far, early, cols, result)


def solution(mesh):
    in_specs = (
        P("row", "col"),
        P(),
        P("row", "col"),
        P("row", "col"),
        P("row", "col"),
        P("row", "col"),
    )
    out_specs = P("row", "col")
    return jax.shard_map(
        per_device, mesh=mesh, in_specs=in_specs, out_specs=out_specs, check_vma=False
    )
```

```python
import functools
import math

import jax
import jax.numpy as jnp
from jax import lax
from jax.experimental import pallas as pl
from jax.experimental.pallas import tpu as pltpu
from jax.sharding import PartitionSpec as P

HD = 128
MIB = 1 << 20


def after(array, *earlier):
    if not earlier:
        return array
    return lax.optimization_barrier((array, *earlier))[0]


def swap(array, axis, mask):
    return lax.ppermute(array, axis, [(i, i ^ mask) for i in range(lax.axis_size(axis))])


def row_bits():
    return [1 << b for b in reversed(range((lax.axis_size("row")).bit_length() - 1))]


def exchange(array, *earlier):
    return swap(after(array, *earlier), "row", row_bits()[0])


def gather_near(array, *earlier):
    pieces = {0: after(array, *earlier)}
    for bit in row_bits()[1:]:
        pieces.update({j ^ bit: swap(p, "row", bit) for j, p in pieces.items()})
    return [pieces[j] for j in range(len(pieces))]


def order_pair(mine, other, col_index, bit, axis_dim):
    upper = col_index // 2**bit % 2 == 1
    lower_part = jnp.where(upper, other, mine)
    upper_part = jnp.where(upper, mine, other)
    return jnp.concatenate([lower_part, upper_part], axis=axis_dim)


def ring_order(n):
    return list(range(0, n, 2)) + list(range(1, n, 2))[::-1]


def ring_source(c, hops, n):
    at = jnp.where(c % 2 == 0, c // 2, n - 1 - c // 2)
    at = (at - hops) % n
    return jnp.where(at < n // 2, 2 * at, 2 * (n - 1 - at) + 1)


class Ring:
    def __init__(self, block):
        n = lax.axis_size("col")
        order = ring_order(n)
        self.n, self.hops = n, 0
        self.up = [(order[i], order[(i + 1) % n]) for i in range(n)]
        self.down = [(b, a) for a, b in self.up]
        self.found = [(lax.axis_index("col"), 0, block)]
        self.last = [block, block]

    def hop(self, *earlier, beside=()):
        if self.hops == self.n // 2:
            return beside
        c, own = self.found[0][0], self.found[0][2]
        rows = own.shape[0] // 2
        self.hops += 1
        end = self.hops == self.n // 2
        below, above = self.last
        if end:
            below, above = below[:rows], above[rows:]
        if earlier:
            below, above = lax.optimization_barrier((below, above, *earlier))[:2]
        below = lax.ppermute(below, "col", self.up)
        above = lax.ppermute(above, "col", self.down)
        below, above, *beside = lax.optimization_barrier((below, above, *beside))
        self.last = [below, above]
        self.found.append((ring_source(c, self.hops, self.n), 0, self.last[0]))
        self.found.append((ring_source(c, -self.hops, self.n), rows if end else 0, self.last[1]))
        return beside


class Panel:
    def __init__(self, blocks, first, buffer, sems):
        self.blocks, self.first, self.buffer, self.sems = blocks, first, buffer, sems

    def start(self, i):
        n, tok, cols = self.buffer.shape
        sources = [(0, self.blocks[i])] if i < n - 1 else [(0, self.blocks[i]), (tok // 2, self.blocks[n])]
        for at, ref in sources:
            rows = ref.shape[0]
            into = self.buffer.at[i, pl.ds(at, rows), :]
            pltpu.make_async_copy(ref.at[:, pl.ds(self.first, cols)], into, self.sems.at[i]).start()

    def wait(self, i):
        into = self.buffer.at[i]
        pltpu.make_async_copy(into, into, self.sems.at[i]).wait()


class Weights:
    def __init__(self, refs, near, far, stride, first_row, first, buffer, sems):
        chunks = (len(refs) - near) // far
        self.near = refs[:near]
        self.far = [refs[near + i * chunks : near + (i + 1) * chunks] for i in range(far)]
        self.stride, self.first_row, self.first = stride, first_row, first
        self.buffer, self.sems = buffer, sems

    def start(self, i, slot):
        blocks, depth, cols = self.buffer.shape
        parts = len(self.near) + len(self.far)
        per = blocks // parts
        s = slot % per
        for p in range(parts):

            @pl.when(slot // per == p)
            def _():
                if p < len(self.near):
                    row = pl.multiple_of(s * self.stride + self.first_row, HD)
                    sources = [self.near[p].at[pl.ds(row, depth), pl.ds(self.first, cols)]]
                else:
                    row = pl.multiple_of(s * depth, HD)
                    sources = [ref.at[pl.ds(row, depth), :] for ref in self.far[p - len(self.near)]]
                at = 0
                for source in sources:
                    wide = source.shape[1]
                    into = self.buffer.at[i, :, pl.ds(at, wide)]
                    pltpu.make_async_copy(source, into, self.sems.at[i]).start()
                    at += wide

    def wait(self, i):
        into = self.buffer.at[i]
        pltpu.make_async_copy(into, into, self.sems.at[i]).wait()


def multiply(slots_ref, panel, groups):
    blocks = panel.buffer.shape[0]
    for i in range(blocks):
        panel.start(i)
        for weights, _ in groups:
            weights.start(i, slots_ref[i])

    def body(i, carry):
        panel.wait(i)
        for weights, acc in groups:
            weights.wait(i)
            acc[...] += jnp.dot(
                panel.buffer[i], weights.buffer[i], preferred_element_type=jnp.float32
            )
        return carry

    lax.fori_loop(0, blocks, body, 0)


def take(refs, *counts):
    out, at = [], 0
    for n in counts:
        out.append(refs[at : at + n])
        at += n
    return *out, refs[at:]


def project_kernel(n_blocks, plan, slots_ref, *refs):
    n = len(plan)
    blocks, weights, (scale_ref, cos_ref, sin_ref), outs, w_bufs, accs, rest = take(
        refs, n_blocks, sum(p[0] for p in plan), 3, n, n, n
    )
    panel_buf, panel_sem, sems = rest
    depth = panel_buf.shape[2]
    groups, at = [], 0
    for g, (count, near, far, first, _, _) in enumerate(plan):
        stack = Weights(
            weights[at : at + count], near, far, depth, 0, first, w_bufs[g], sems.at[g]
        )
        accs[g][...] = jnp.zeros_like(accs[g])
        groups.append((stack, accs[g]))
        at += count
    multiply(slots_ref, Panel(blocks, 0, panel_buf, panel_sem), groups)
    for acc, o_ref, (*_, heads, factor) in zip(accs, outs, plan):
        scale = scale_ref[...] * factor
        for h in range(acc.shape[1] // HD):
            at = pl.ds(h * HD, HD)
            x = acc[:, at] * scale
            if h < heads:
                x = x * cos_ref[...] + pltpu.roll(x, HD // 2, 1) * sin_ref[...]
            o_ref[:, at] = x.astype(o_ref.dtype)


def project(blocks, slots, groups, scale, cos, sin):
    tok, depth = blocks[0].shape
    count = len(blocks) - 1
    stacks = [[*near, *[w for chunks in far for w in chunks]] for near, far, *_ in groups]
    widths = [sum(w.shape[1] for w in far[0]) for _, far, *_ in groups]
    plan = [
        (len(stack), len(near), len(far), *rest)
        for stack, (near, far, *rest) in zip(stacks, groups)
    ]
    weights = [w for stack in stacks for w in stack]
    hbm = pl.BlockSpec(memory_space=pl.ANY)
    vmem = pl.BlockSpec(memory_space=pltpu.VMEM)
    return pl.pallas_call(
        functools.partial(project_kernel, len(blocks), plan),
        in_specs=[pl.BlockSpec(memory_space=pltpu.SMEM)]
        + [hbm] * (len(blocks) + len(weights))
        + [vmem] * 3,
        out_specs=[vmem] * len(groups),
        out_shape=[jax.ShapeDtypeStruct((tok, w), jnp.bfloat16) for w in widths],
        scratch_shapes=[pltpu.VMEM((count, depth, w), jnp.bfloat16) for w in widths]
        + [pltpu.VMEM((tok, w), jnp.float32) for w in widths]
        + [
            pltpu.VMEM((count, tok, depth), jnp.bfloat16),
            pltpu.SemaphoreType.DMA((count,)),
            pltpu.SemaphoreType.DMA((len(groups), count)),
        ],
        compiler_params=pltpu.CompilerParams(vmem_limit_bytes=60 * MIB),
        cost_estimate=pl.CostEstimate(
            flops=2 * count * tok * depth * sum(widths),
            bytes_accessed=2 * (count * depth * (tok + sum(widths)) + tok * sum(widths)),
            transcendentals=0,
        ),
    )(slots, *blocks, *weights, scale, cos, sin)


def attend_kernel(parts, chunks, pair, r_ref, *refs):
    chunk_refs, pieces = refs[:chunks], refs[chunks : chunks + parts]
    o_ref, q_ref, turned, top, total, acc = refs[chunks + parts :]
    r = r_ref[0]
    tok = q_ref.shape[0]
    step = pl.program_id(0)
    per = pl.num_programs(0) // chunks
    for i in range(chunks):

        @pl.when(step // per == i)
        def _():
            q_ref[...] = chunk_refs[i][...]

    dims = (((1,), (1,)), ((), ()))

    @pl.when(step == 0)
    def _():
        for j in range(parts):
            turned[j] = pieces[j][:, HD:].T

    def scores(j, g):
        return lax.dot_general(
            pieces[j][:, :HD],
            q_ref[:, g * HD : (g + 1) * HD],
            dims,
            preferred_element_type=jnp.float32,
        )

    key = lax.broadcasted_iota(jnp.int32, (tok, tok), 0)
    query = lax.broadcasted_iota(jnp.int32, (tok, tok), 1)
    for g in range(pair):
        s = jnp.where(key <= query, scores(0, g), -jnp.inf)
        m = jnp.max(s, axis=0, keepdims=True)
        p = jnp.exp2(s - m)
        top[g] = m
        total[g] = jnp.sum(p, axis=0, keepdims=True)
        acc[g] = jnp.dot(turned[0], p.astype(jnp.bfloat16), preferred_element_type=jnp.float32)
    for j in range(1, parts):

        @pl.when(jnp.bitwise_xor(r, j) < r)
        def _():
            for g in range(pair):
                s = scores(j, g)
                m = jnp.maximum(top[g], jnp.max(s, axis=0, keepdims=True))
                keep = jnp.exp2(top[g] - m)
                p = jnp.exp2(s - m)
                top[g] = m
                total[g] = total[g] * keep + jnp.sum(p, axis=0, keepdims=True)
                acc[g] = acc[g] * keep + jnp.dot(
                    turned[j], p.astype(jnp.bfloat16), preferred_element_type=jnp.float32
                )

    for g in range(pair):
        o_ref[:, g * HD : (g + 1) * HD] = (acc[g] / total[g]).T.astype(o_ref.dtype)


def attend(r, queries, pieces):
    tok, cols = queries[0].shape
    chunks, parts = len(queries), len(pieces)
    pair = 2 if cols // HD % 2 == 0 else 1
    per = cols // (HD * pair)
    heads = chunks * cols // HD

    def query_spec(i):
        return pl.BlockSpec((tok, pair * HD), lambda h, r: (0, jnp.clip(h - i * per, 0, per - 1)))

    return pl.pallas_call(
        functools.partial(attend_kernel, parts, chunks, pair),
        grid_spec=pltpu.PrefetchScalarGridSpec(
            num_scalar_prefetch=1,
            grid=(chunks * per,),
            in_specs=[query_spec(i) for i in range(chunks)]
            + [pl.BlockSpec((tok, 2 * HD), lambda h, r: (0, 0)) for _ in pieces],
            out_specs=pl.BlockSpec((tok, pair * HD), lambda h, r: (0, h)),
            scratch_shapes=[
                pltpu.VMEM((tok, pair * HD), jnp.bfloat16),
                pltpu.VMEM((parts, HD, tok), jnp.bfloat16),
                pltpu.VMEM((pair, 1, tok), jnp.float32),
                pltpu.VMEM((pair, 1, tok), jnp.float32),
                pltpu.VMEM((pair, HD, tok), jnp.float32),
            ],
        ),
        out_shape=jax.ShapeDtypeStruct((tok, chunks * cols), jnp.bfloat16),
        compiler_params=pltpu.CompilerParams(
            dimension_semantics=("arbitrary",), vmem_limit_bytes=32 * MIB
        ),
        cost_estimate=pl.CostEstimate(
            flops=4 * heads * tok * tok * parts * HD,
            bytes_accessed=4 * tok * heads * HD + parts * 4 * tok * HD,
            transcendentals=heads * tok * tok * parts,
        ),
    )(r.reshape(1), *queries, *pieces)


def finish_kernel(n_blocks, near, far, count, stride, first, column, slots_ref, *refs):
    blocks, weights, rest = take(refs, n_blocks, count)
    *old, o_ref, w_buf, panel_buf, acc, panel_sem, sems = rest
    acc[...] = old[0][...] if old else jnp.zeros_like(acc)
    stack = Weights(weights, near, far, stride, first, 0, w_buf, sems)
    multiply(slots_ref, Panel(blocks, column, panel_buf, panel_sem), [(stack, acc)])
    o_ref[...] = acc[...].astype(o_ref.dtype)


def finish(blocks, slots, column, near, far, stride, first, wide, dtype, total=None):
    tok = blocks[0].shape[0]
    count = len(blocks) - 1
    weights = [*near, *far]
    cols = near[0].shape[1]
    hbm = pl.BlockSpec(memory_space=pl.ANY)
    vmem = pl.BlockSpec(memory_space=pltpu.VMEM)
    old = [] if total is None else [total]
    return pl.pallas_call(
        functools.partial(
            finish_kernel, len(blocks), len(near), len(far), len(weights), stride, first, column
        ),
        in_specs=[pl.BlockSpec(memory_space=pltpu.SMEM)]
        + [hbm] * (len(blocks) + len(weights))
        + [vmem] * len(old),
        out_specs=vmem,
        out_shape=jax.ShapeDtypeStruct((tok, cols), dtype),
        scratch_shapes=[
            pltpu.VMEM((count, wide, cols), jnp.bfloat16),
            pltpu.VMEM((count, tok, wide), jnp.bfloat16),
            pltpu.VMEM((tok, cols), jnp.float32),
            pltpu.SemaphoreType.DMA((count,)),
            pltpu.SemaphoreType.DMA((count,)),
        ],
        compiler_params=pltpu.CompilerParams(vmem_limit_bytes=60 * MIB),
        cost_estimate=pl.CostEstimate(
            flops=2 * count * tok * wide * cols,
            bytes_accessed=2 * count * wide * (tok + cols) + 8 * tok * cols,
            transcendentals=0,
        ),
    )(slots, *blocks, *weights, *old)


def per_device(hidden, norm_gain, wq, wk, wv, wo):
    tok, feat = hidden.shape
    n_row, n_col = lax.axis_size("row"), lax.axis_size("col")
    r, c = lax.axis_index("row"), lax.axis_index("col")
    depth = feat * n_col
    rows = wq.shape[0]
    cols = wq.shape[1]

    kv_cols = wk.shape[1]
    group = max(1, HD // kv_cols)
    stacked = jnp.stack((wk, wv), axis=1)
    for bit in range(group.bit_length() - 1):
        other = swap(stacked, "col", 1 << bit)
        stacked = order_pair(stacked, other, c, bit, 2)
    stacked = stacked.reshape(rows, 2 * HD)

    n_heads = cols // HD
    first_heads = n_heads // 2
    quarter, eighth = n_heads // 4, n_heads // 8
    if eighth > 0:
        sizes = [quarter, first_heads - quarter, eighth, eighth, n_heads - first_heads - 2 * eighth]
    else:
        sizes = [first_heads, n_heads - first_heads]
    early = 2 if eighth > 0 else 1
    wide = first_heads * HD

    def chunk(i):
        return wq[:, sum(sizes[:i]) * HD : sum(sizes[: i + 1]) * HD]

    def columns(far):
        return [list(chunks) for chunks in zip(*far)]

    per = rows // feat
    wider = hidden.astype(jnp.float32)
    gain = lax.dynamic_slice(norm_gain, (c * feat,), (feat,))
    squares = jnp.sum(wider * wider, axis=1)
    for bit in range(n_col.bit_length() - 1):
        squares += swap(squares, "col", 1 << bit)
    ring = Ring((wider * gain).astype(jnp.bfloat16))
    kv_other, squares, *kv_near = ring.hop(
        beside=[exchange(stacked), squares, *gather_near(stacked)]
    )
    near = len(kv_near)
    at, q_far, pending = 0, [], None
    for i in range(n_col // 2 - 1):
        beside = []
        if i == 0:
            beside += gather_near(kv_other) + gather_near(wq)
        if i == 1:
            beside += gather_near(wo)
        if pending is not None:
            beside += gather_near(pending)
        sent = at < len(sizes) - 1
        if sent:
            beside.append(exchange(chunk(at), ring.last[0]))
        beside = ring.hop(beside=beside)
        if i == 0:
            kv_far, q_near, beside = take(beside, near, near)
        if i == 1:
            o_near, beside = take(beside, near)
        if pending is not None:
            far, beside = take(beside, near)
            q_far.append(far)
        pending = beside[0] if sent else None
        at += sent
    blocks = [piece for _, _, piece in ring.found]
    slots = jnp.stack([(source // per ^ r) * per + source % per for source, _, _ in ring.found])
    scale = lax.rsqrt(squares / depth + 1e-05)[:, None]

    half = HD // 2
    positions = r * tok + jnp.arange(tok)
    freqs = 10000.0 ** (-jnp.arange(half).astype(jnp.float32) / half)
    angles = positions.astype(jnp.float32)[:, None] * freqs[None, :]
    cosine, sine = jnp.cos(angles), jnp.sin(angles)
    cosine = jnp.concatenate([cosine, cosine], axis=1)
    sine = jnp.concatenate([-sine, sine], axis=1)
    factor = HD ** (-0.5) * math.log2(math.e)

    beside = gather_near(pending) if pending is not None else []
    sent = at < len(sizes) - 1
    if sent:
        beside.append(exchange(chunk(at), blocks[-1]))
    kv_group = kv_near, columns([kv_far]), 0, 1, 1.0
    q_group = q_near, columns(q_far[:early]), 0, first_heads, factor
    out = project(blocks, slots, [kv_group, q_group], scale, cosine, sine)
    kv, queries, *beside = lax.optimization_barrier((*out, *beside))
    if pending is not None:
        far, beside = take(beside, near)
        q_far.append(far)
    kv_other = exchange(kv)
    beside = gather_near(kv) + (gather_near(beside[0]) if sent else [])
    kv_other, *beside = lax.optimization_barrier((kv_other, *beside))
    kv_pieces, far = take(beside, near)
    if sent:
        q_far.append(far)
    kv_pieces = [*kv_pieces, *gather_near(kv_other)]
    last_other = exchange(chunk(len(sizes) - 1), kv_other)
    heads = attend(r, [queries], kv_pieces)

    ring = Ring(heads)
    (last_other,) = ring.hop(beside=[last_other])

    def o_rows(first, wide):
        return wo.reshape(-1, cols, wo.shape[1])[:, first : first + wide].reshape(-1, wo.shape[1])

    o_first = exchange(o_rows(0, wide), last_other)
    q_far.append(gather_near(last_other))
    q_group = q_near, columns(q_far[early:]), wide, n_heads - first_heads, factor
    (queries,) = ring.hop(
        beside=project(blocks, slots, [q_group], scale, cosine, sine)
    )
    (heads,) = ring.hop(beside=[attend(r, [queries], kv_pieces)])
    second = Ring(heads)
    for _ in range(n_col // 2):
        arrived = ring.last
        ring.hop(*second.last)
        second.hop(*arrived)

    blocks = [piece for _, _, piece in ring.found]
    o_far = gather_near(o_first, *second.last)
    total = finish(blocks, slots, 0, o_near, o_far, cols, 0, wide, jnp.float32)
    blocks = [piece for _, _, piece in second.found]
    rest = cols - wide
    parts = [(0, rest // 2), (rest // 2, rest - rest // 2)] if rest >= 2 * HD else [(0, rest)]
    earlier = o_first
    others = []
    for first, part in parts:
        others.append(exchange(o_rows(wide + first, part), earlier))
        earlier = others[-1]
    for j, (first, part) in enumerate(parts):
        dtype = jnp.bfloat16 if j == len(parts) - 1 else jnp.float32
        o_far = gather_near(others[j], total)
        total = finish(
            blocks, slots, first, o_near, o_far, cols, wide + first, part, dtype, total
        )
    return total


def solution(mesh):
    in_specs = (
        P("row", "col"),
        P(),
        P("row", "col"),
        P("row", "col"),
        P("row", "col"),
        P("row", "col"),
    )
    out_specs = P("row", "col")
    return jax.shard_map(
        per_device, mesh=mesh, in_specs=in_specs, out_specs=out_specs, check_vma=False
    )
```

```python
import functools
import math

import jax
import jax.numpy as jnp
from jax import lax
from jax.experimental import pallas as pl
from jax.experimental.pallas import tpu as pltpu
from jax.sharding import PartitionSpec as P

HD = 128
MIB = 1 << 20
SHORT = pl.CostEstimate(flops=1, bytes_accessed=1, transcendentals=0)


def after(array, *earlier):
    if not earlier:
        return array
    return lax.optimization_barrier((array, *earlier))[0]


def swap(array, axis, mask):
    return lax.ppermute(array, axis, [(i, i ^ mask) for i in range(lax.axis_size(axis))])


def row_bits():
    return [1 << b for b in reversed(range((lax.axis_size("row")).bit_length() - 1))]


def exchange(array, *earlier):
    return swap(after(array, *earlier), "row", row_bits()[0])


def gather_near(array, *earlier):
    pieces = {0: after(array, *earlier)}
    for bit in row_bits()[1:]:
        pieces.update({j ^ bit: swap(p, "row", bit) for j, p in pieces.items()})
    return [pieces[j] for j in range(len(pieces))]


def order_pair(mine, other, col_index, bit, axis_dim):
    upper = col_index // 2**bit % 2 == 1
    lower_part = jnp.where(upper, other, mine)
    upper_part = jnp.where(upper, mine, other)
    return jnp.concatenate([lower_part, upper_part], axis=axis_dim)


def ring_order(n):
    return list(range(0, n, 2)) + list(range(1, n, 2))[::-1]


def ring_source(c, hops, n):
    at = jnp.where(c % 2 == 0, c // 2, n - 1 - c // 2)
    at = (at - hops) % n
    return jnp.where(at < n // 2, 2 * at, 2 * (n - 1 - at) + 1)


class Ring:
    def __init__(self, block):
        n = lax.axis_size("col")
        order = ring_order(n)
        self.n, self.hops = n, 0
        self.up = [(order[i], order[(i + 1) % n]) for i in range(n)]
        self.down = [(b, a) for a, b in self.up]
        self.found = [(lax.axis_index("col"), 0, block)]
        self.last = [block, block]

    def hop(self, *earlier, beside=()):
        if self.hops == self.n // 2:
            return beside
        c, own = self.found[0][0], self.found[0][2]
        rows = own.shape[0] // 2
        self.hops += 1
        end = self.hops == self.n // 2
        below, above = self.last
        if end:
            below, above = below[:rows], above[rows:]
        if earlier:
            below, above = lax.optimization_barrier((below, above, *earlier))[:2]
        below = lax.ppermute(below, "col", self.up)
        above = lax.ppermute(above, "col", self.down)
        below, above, *beside = lax.optimization_barrier((below, above, *beside))
        self.last = [below, above]
        self.found.append((ring_source(c, self.hops, self.n), 0, self.last[0]))
        self.found.append((ring_source(c, -self.hops, self.n), rows if end else 0, self.last[1]))
        return beside


def blank(shape):
    return pl.pallas_call(
        lambda o_ref: None,
        out_specs=pl.BlockSpec(memory_space=pl.ANY),
        out_shape=jax.ShapeDtypeStruct(shape, jnp.bfloat16),
    )()


def take(refs, *counts):
    out, at = [], 0
    for n in counts:
        out.append(refs[at : at + n])
        at += n
    return *out, refs[at:]


def multiply(steps, a_buf, w_bufs, accs, a_sem, w_sem):
    for i, (left, rights) in enumerate(steps):
        pltpu.make_async_copy(left, a_buf.at[i], a_sem.at[i]).start()
        for g, chunks in enumerate(rights):
            at = 0
            for chunk in chunks:
                wide = chunk.shape[1]
                into = w_bufs[g].at[i, :, pl.ds(at, wide)]
                pltpu.make_async_copy(chunk, into, w_sem.at[g, i]).start()
                at += wide

    def body(i, carry):
        pltpu.make_async_copy(a_buf.at[i], a_buf.at[i], a_sem.at[i]).wait()
        for g, acc in enumerate(accs):
            pltpu.make_async_copy(w_bufs[g].at[i], w_bufs[g].at[i], w_sem.at[g, i]).wait()
            acc[...] += jnp.dot(a_buf[i], w_bufs[g][i], preferred_element_type=jnp.float32)
        return carry

    lax.fori_loop(0, len(steps), body, 0)


def project_kernel(near, far, chunks, first, heads, factor, panel_ref, *refs):
    near_refs, far_refs, (scale_ref, cos_ref, sin_ref), rest = take(refs, near, far * chunks, 3)
    o_ref, a_buf, w_buf, acc, a_sem, w_sem = rest
    slots, _, depth = panel_ref.shape
    per = slots // (near + far)
    cols = acc.shape[1]
    steps = []
    for k in range(slots):
        p, rows = k // per, pl.ds(k % per * depth, depth)
        if p < near:
            right = [near_refs[p].at[rows, pl.ds(first, cols)]]
        else:
            at = (p - near) * chunks
            right = [ref.at[rows, :] for ref in far_refs[at : at + chunks]]
        steps.append((panel_ref.at[k], [right]))
    acc[...] = jnp.zeros_like(acc)
    multiply(steps, a_buf, [w_buf], [acc], a_sem, w_sem)
    scale = scale_ref[...] * factor
    for h in range(cols // HD):
        at = pl.ds(h * HD, HD)
        x = acc[:, at] * scale
        if h < heads:
            x = x * cos_ref[...] + pltpu.roll(x, HD // 2, 1) * sin_ref[...]
        o_ref[:, at] = x.astype(o_ref.dtype)


def project(panel, near, far, first, heads, factor, scale, cos, sin):
    slots, tok, depth = panel.shape
    chunks = len(far[0])
    cols = sum(w.shape[1] for w in far[0])
    hbm = pl.BlockSpec(memory_space=pl.ANY)
    vmem = pl.BlockSpec(memory_space=pltpu.VMEM)
    return pl.pallas_call(
        functools.partial(project_kernel, len(near), len(far), chunks, first, heads, factor),
        in_specs=[hbm] * (1 + len(near) + len(far) * chunks) + [vmem] * 3,
        out_specs=vmem,
        out_shape=jax.ShapeDtypeStruct((tok, cols), jnp.bfloat16),
        scratch_shapes=[
            pltpu.VMEM((slots, tok, depth), jnp.bfloat16),
            pltpu.VMEM((slots, depth, cols), jnp.bfloat16),
            pltpu.VMEM((tok, cols), jnp.float32),
            pltpu.SemaphoreType.DMA((slots,)),
            pltpu.SemaphoreType.DMA((1, slots)),
        ],
        compiler_params=pltpu.CompilerParams(vmem_limit_bytes=60 * MIB),
        cost_estimate=SHORT,
    )(panel, *near, *[w for pieces in far for w in pieces], scale, cos, sin)


def attend_kernel(parts, chunks, pair, r_ref, *refs):
    chunk_refs, pieces = refs[:chunks], refs[chunks : chunks + parts]
    o_ref, q_ref, turned, top, total, acc = refs[chunks + parts :]
    r = r_ref[0]
    tok = q_ref.shape[0]
    step = pl.program_id(0)
    per = pl.num_programs(0) // chunks
    for i in range(chunks):

        @pl.when(step // per == i)
        def _():
            q_ref[...] = chunk_refs[i][...]

    dims = (((1,), (1,)), ((), ()))

    @pl.when(step == 0)
    def _():
        for j in range(parts):
            turned[j] = pieces[j][:, HD:].T

    def scores(j, g):
        return lax.dot_general(
            pieces[j][:, :HD],
            q_ref[:, g * HD : (g + 1) * HD],
            dims,
            preferred_element_type=jnp.float32,
        )

    key = lax.broadcasted_iota(jnp.int32, (tok, tok), 0)
    query = lax.broadcasted_iota(jnp.int32, (tok, tok), 1)
    for g in range(pair):
        s = jnp.where(key <= query, scores(0, g), -jnp.inf)
        m = jnp.max(s, axis=0, keepdims=True)
        p = jnp.exp2(s - m)
        top[g] = m
        total[g] = jnp.sum(p, axis=0, keepdims=True)
        acc[g] = jnp.dot(turned[0], p.astype(jnp.bfloat16), preferred_element_type=jnp.float32)
    for j in range(1, parts):

        @pl.when(jnp.bitwise_xor(r, j) < r)
        def _():
            for g in range(pair):
                s = scores(j, g)
                m = jnp.maximum(top[g], jnp.max(s, axis=0, keepdims=True))
                keep = jnp.exp2(top[g] - m)
                p = jnp.exp2(s - m)
                top[g] = m
                total[g] = total[g] * keep + jnp.sum(p, axis=0, keepdims=True)
                acc[g] = acc[g] * keep + jnp.dot(
                    turned[j], p.astype(jnp.bfloat16), preferred_element_type=jnp.float32
                )

    for g in range(pair):
        o_ref[:, g * HD : (g + 1) * HD] = (acc[g] / total[g]).T.astype(o_ref.dtype)


def attend(r, queries, pieces):
    tok, cols = queries[0].shape
    chunks, parts = len(queries), len(pieces)
    pair = 2 if cols // HD % 2 == 0 else 1
    per = cols // (HD * pair)
    heads = chunks * cols // HD

    def query_spec(i):
        return pl.BlockSpec((tok, pair * HD), lambda h, r: (0, jnp.clip(h - i * per, 0, per - 1)))

    return pl.pallas_call(
        functools.partial(attend_kernel, parts, chunks, pair),
        grid_spec=pltpu.PrefetchScalarGridSpec(
            num_scalar_prefetch=1,
            grid=(chunks * per,),
            in_specs=[query_spec(i) for i in range(chunks)]
            + [pl.BlockSpec((tok, 2 * HD), lambda h, r: (0, 0)) for _ in pieces],
            out_specs=pl.BlockSpec((tok, pair * HD), lambda h, r: (0, h)),
            scratch_shapes=[
                pltpu.VMEM((tok, pair * HD), jnp.bfloat16),
                pltpu.VMEM((parts, HD, tok), jnp.bfloat16),
                pltpu.VMEM((pair, 1, tok), jnp.float32),
                pltpu.VMEM((pair, 1, tok), jnp.float32),
                pltpu.VMEM((pair, HD, tok), jnp.float32),
            ],
        ),
        out_shape=jax.ShapeDtypeStruct((tok, chunks * cols), jnp.bfloat16),
        compiler_params=pltpu.CompilerParams(
            dimension_semantics=("arbitrary",), vmem_limit_bytes=32 * MIB
        ),
        cost_estimate=SHORT,
    )(r.reshape(1), *queries, *pieces)


def finish_kernel(plan, n_refs, *refs):
    arrays, (*old, o_ref, a_buf, w_buf, acc, a_sem, w_sem) = take(refs, n_refs)
    depth = a_buf.shape[2]
    steps = []
    for panel, slot, column, weights, row in plan:
        left = arrays[panel].at[slot, :, pl.ds(column, depth)]
        steps.append((left, [[arrays[weights].at[pl.ds(row, depth), :]]]))
    acc[...] = old[0][...] if old else jnp.zeros_like(acc)
    multiply(steps, a_buf, [w_buf], [acc], a_sem, w_sem)
    o_ref[...] = acc[...].astype(o_ref.dtype)


def finish(arrays, plan, depth, dtype, total=None):
    tok = arrays[plan[0][0]].shape[1]
    cols = arrays[plan[0][3]].shape[1]
    n = len(plan)
    hbm = pl.BlockSpec(memory_space=pl.ANY)
    vmem = pl.BlockSpec(memory_space=pltpu.VMEM)
    old = [] if total is None else [total]
    return pl.pallas_call(
        functools.partial(finish_kernel, plan, len(arrays)),
        in_specs=[hbm] * len(arrays) + [vmem] * len(old),
        out_specs=vmem,
        out_shape=jax.ShapeDtypeStruct((tok, cols), dtype),
        scratch_shapes=[
            pltpu.VMEM((n, tok, depth), jnp.bfloat16),
            pltpu.VMEM((n, depth, cols), jnp.bfloat16),
            pltpu.VMEM((tok, cols), jnp.float32),
            pltpu.SemaphoreType.DMA((n,)),
            pltpu.SemaphoreType.DMA((1, n)),
        ],
        compiler_params=pltpu.CompilerParams(vmem_limit_bytes=60 * MIB),
        cost_estimate=SHORT,
    )(*arrays, *old)


def per_device(hidden, norm_gain, wq, wk, wv, wo):
    tok, feat = hidden.shape
    n_row, n_col = lax.axis_size("row"), lax.axis_size("col")
    r, c = lax.axis_index("row"), lax.axis_index("col")
    depth = feat * n_col
    rows = wq.shape[0]
    cols = wq.shape[1]

    kv_cols = wk.shape[1]
    group = max(1, HD // kv_cols)
    stacked = jnp.stack((wk, wv), axis=1)
    for bit in range(group.bit_length() - 1):
        other = swap(stacked, "col", 1 << bit)
        stacked = order_pair(stacked, other, c, bit, 2)
    stacked = stacked.reshape(rows, 2 * HD)

    n_heads = cols // HD
    first_heads = n_heads // 2
    late_heads = n_heads - first_heads
    if n_heads >= 4:
        sizes = [first_heads // 2, first_heads - first_heads // 2, late_heads // 2]
        sizes.append(late_heads - late_heads // 2)
    else:
        sizes = [first_heads, late_heads]
    early = 2 if n_heads >= 4 else 1
    wide, rest = first_heads * HD, late_heads * HD
    chunks = [
        wq[:, sum(sizes[:i]) * HD : sum(sizes[: i + 1]) * HD] for i in range(len(sizes))
    ]

    def by_block(far):
        return [list(pieces) for pieces in zip(*far)]

    half = HD // 2
    positions = r * tok + jnp.arange(tok)
    freqs = 10000.0 ** (-jnp.arange(half).astype(jnp.float32) / half)
    angles = positions.astype(jnp.float32)[:, None] * freqs[None, :]
    cosine, sine = jnp.cos(angles), jnp.sin(angles)
    cosine = jnp.concatenate([cosine, cosine], axis=1)
    sine = jnp.concatenate([-sine, sine], axis=1)
    factor = HD ** (-0.5) * math.log2(math.e)

    per = rows // feat

    def put(panel, found):
        for source, first, piece in found:
            slot = (source // per ^ r) * per + source % per
            panel = lax.dynamic_update_slice(panel, piece[None], (slot, first, 0))
        return panel

    wider = hidden.astype(jnp.float32)
    gain = lax.dynamic_slice(norm_gain, (c * feat,), (feat,))
    squares = jnp.sum(wider * wider, axis=1)
    ring = Ring((wider * gain).astype(jnp.bfloat16))
    hops = n_col // 2
    sq_bits = n_col.bit_length() - 1
    x_sent = exchange(stacked)
    gathering = gather_near(stacked)
    got_near = []
    panel = put(blank((n_col, tok, feat)), ring.found)
    for i in range(hops):
        last_hop = i == hops - 1
        beside = [panel, cosine, sine, *gathering]
        if i < sq_bits:
            beside.append(swap(squares, "col", 1 << i))
        ahead = chunks[i : i + 1] if i < len(sizes) - 1 else []
        if not last_hop and x_sent is not None:
            beside.append(x_sent)
        beside = ring.hop(beside=[*beside, *ahead])
        (panel, cosine, sine), near, beside = take(beside, 3, len(gathering))
        panel = put(panel, ring.found[-2:])
        got_near.append(near)
        if i < sq_bits:
            squares, beside = squares + beside[0], beside[1:]
        if last_hop:
            break
        gathering = []
        if x_sent is not None:
            gathering = gather_near(beside[0])
            beside = beside[1:]
        x_sent = exchange(beside[0]) if ahead else None
        if i == hops - 2:
            gathering = [*gathering, *gather_near(after(wq, ring.last[0]))]
    blocks_near = len(got_near[0])
    kv_near, kv_far = got_near[0], got_near[1]
    q_near = got_near[-1][-blocks_near:]
    q_far = [near[:blocks_near] for near in got_near[2:] if len(near) > 0]
    scale = lax.rsqrt(squares / depth + 1e-05)[:, None]

    kv = project(panel, kv_near, by_block([kv_far]), 0, 1, 1.0, scale, cosine, sine)
    kv, *arrived = lax.optimization_barrier((kv, *([x_sent] if x_sent is not None else [])))
    scale = after(scale, kv)
    queries = project(
        panel, q_near, by_block(q_far[:early]), 0, first_heads, factor, scale, cosine, sine
    )
    beside = [exchange(kv), queries, *gather_near(kv)]
    for piece in arrived:
        beside += gather_near(piece)
    kv_other, queries, *beside = lax.optimization_barrier(tuple(beside))
    kv_pieces, far = take(beside, blocks_near)
    late_far = [far] if arrived else []
    kv_pieces = [*kv_pieces, *gather_near(kv_other)]
    last_other = exchange(after(chunks[-1], kv_other))
    heads = attend(r, [queries], kv_pieces)

    def o_rows(first, wide):
        return wo.reshape(-1, cols, wo.shape[1])[:, first : first + wide].reshape(-1, wo.shape[1])

    o_first = o_rows(0, wide)
    ring = Ring(heads)
    first_panel = put(blank((n_col, tok, wide)), ring.found)
    second_panel = blank((n_col, tok, rest))
    last_other, o_first, first_panel, second_panel = ring.hop(
        beside=[last_other, o_first, first_panel, second_panel]
    )
    first_panel = put(first_panel, ring.found[-2:])
    o_first = exchange(o_first)
    far = gather_near(last_other)
    late_far = by_block([*late_far, far])
    parts = [(0, rest // 2), (rest // 2, rest - rest // 2)] if rest >= 2 * HD else [(0, rest)]
    o_parts = [o_rows(wide + first, part) for first, part in parts]
    queries = project(
        panel, q_near, late_far, wide, late_heads, factor, scale, cosine, sine
    )
    queries, first_panel, *o_parts = ring.hop(beside=[queries, first_panel, *o_parts])
    first_panel = put(first_panel, ring.found[-2:])
    o_near = gather_near(after(wo, queries))
    beside = ring.hop(beside=[attend(r, [queries], kv_pieces), first_panel, *o_near])
    (heads, first_panel), o_near = take(beside, 2)
    first_panel = put(first_panel, ring.found[-2:])
    second = Ring(heads)
    second_panel = put(second_panel, second.found)
    others, gathered, sent = [], [], o_first
    for i in range(hops):
        arrived, hop = ring.last, ring.hops
        ring.hop(*second.last)
        beside = [first_panel, second_panel]
        if gathered and i in (1, 3):
            beside += gathered[-1]
        if i in (0, 2) and len(others) < len(parts):
            beside.append(sent)
        (first_panel, second_panel), beside = take(second.hop(*arrived, beside=beside), 2)
        if ring.hops > hop:
            first_panel = put(first_panel, ring.found[-2:])
        second_panel = put(second_panel, second.found[-2:])
        if gathered and i in (1, 3):
            gathered[-1], beside = take(beside, blocks_near)
        if i in (0, 2) and len(others) < len(parts):
            gathered.append(gather_near(beside[0]))
            sent = exchange(after(o_parts[len(others)], beside[0]))
            others.append(sent)

    while len(gathered) < len(parts):
        gathered.append(gather_near(others[len(gathered) - 1]))
    half = n_col // 2
    unit = math.gcd(wide, rest)
    arrays = [first_panel, second_panel, *o_near, *gathered[0]]
    plan = []
    for k in range(n_col):
        p, s = k // per, k % per
        for at in range(0, wide, unit):
            row = s * cols + at if p < blocks_near else s * wide + at
            plan.append((0, k, at, 2 + p, row))
        for at in range(0, rest, unit):
            if p < blocks_near:
                plan.append((1, k, at, 2 + p, s * cols + wide + at))
    total = finish(arrays, plan, unit, jnp.float32)
    for j, (first, part) in enumerate(parts):
        if j + 1 < len(gathered):
            far = gathered[j + 1]
        else:
            far = gather_near(after(others[j], total))
        plan = [
            (0, k, first, 1 + k // per - blocks_near, k % per * part) for k in range(half, n_col)
        ]
        dtype = jnp.bfloat16 if j == len(parts) - 1 else jnp.float32
        total = finish([second_panel, *far], plan, part, dtype, total)
    return total


def solution(mesh):
    in_specs = (
        P("row", "col"),
        P(),
        P("row", "col"),
        P("row", "col"),
        P("row", "col"),
        P("row", "col"),
    )
    out_specs = P("row", "col")
    return jax.shard_map(
        per_device, mesh=mesh, in_specs=in_specs, out_specs=out_specs, check_vma=False
    )
```

```python
import functools
import math

import jax
import jax.numpy as jnp
from jax import lax
from jax.experimental import pallas as pl
from jax.experimental.pallas import tpu as pltpu
from jax.sharding import PartitionSpec as P

HD = 128
MIB = 1 << 20
SHORT = pl.CostEstimate(flops=1, bytes_accessed=1, transcendentals=0)


def after(array, *earlier):
    if not earlier:
        return array
    return lax.optimization_barrier((array, *earlier))[0]


def swap(array, axis, mask):
    return lax.ppermute(array, axis, [(i, i ^ mask) for i in range(lax.axis_size(axis))])


def row_bits():
    return [1 << b for b in reversed(range((lax.axis_size("row")).bit_length() - 1))]


def exchange(array, *earlier):
    return swap(after(array, *earlier), "row", row_bits()[0])


def gather_near(array, *earlier):
    pieces = {0: after(array, *earlier)}
    for bit in row_bits()[1:]:
        pieces.update({j ^ bit: swap(p, "row", bit) for j, p in pieces.items()})
    return [pieces[j] for j in range(len(pieces))]


def order_pair(mine, other, col_index, bit, axis_dim):
    upper = col_index // 2**bit % 2 == 1
    lower_part = jnp.where(upper, other, mine)
    upper_part = jnp.where(upper, mine, other)
    return jnp.concatenate([lower_part, upper_part], axis=axis_dim)


def ring_order(n):
    return list(range(0, n, 2)) + list(range(1, n, 2))[::-1]


def ring_source(c, hops, n):
    at = jnp.where(c % 2 == 0, c // 2, n - 1 - c // 2)
    at = (at - hops) % n
    return jnp.where(at < n // 2, 2 * at, 2 * (n - 1 - at) + 1)


class Ring:
    def __init__(self, block):
        n = lax.axis_size("col")
        order = ring_order(n)
        self.n, self.hops = n, 0
        self.up = [(order[i], order[(i + 1) % n]) for i in range(n)]
        self.down = [(b, a) for a, b in self.up]
        self.found = [(lax.axis_index("col"), 0, block)]
        self.last = [block, block]

    def hop(self, *earlier, beside=()):
        if self.hops == self.n // 2:
            return beside
        c, own = self.found[0][0], self.found[0][2]
        rows = own.shape[0] // 2
        self.hops += 1
        end = self.hops == self.n // 2
        below, above = self.last
        if end:
            below, above = below[:rows], above[rows:]
        if earlier:
            below, above = lax.optimization_barrier((below, above, *earlier))[:2]
        below = lax.ppermute(below, "col", self.up)
        above = lax.ppermute(above, "col", self.down)
        below, above, *beside = lax.optimization_barrier((below, above, *beside))
        self.last = [below, above]
        self.found.append((ring_source(c, self.hops, self.n), 0, self.last[0]))
        self.found.append((ring_source(c, -self.hops, self.n), rows if end else 0, self.last[1]))
        return beside


def blank(shape):
    return pl.pallas_call(
        lambda o_ref: None,
        out_specs=pl.BlockSpec(memory_space=pl.ANY),
        out_shape=jax.ShapeDtypeStruct(shape, jnp.bfloat16),
    )()


def take(refs, *counts):
    out, at = [], 0
    for n in counts:
        out.append(refs[at : at + n])
        at += n
    return *out, refs[at:]


def multiply(steps, a_buf, w_bufs, accs, a_sem, w_sem):
    for i, (left, rights) in enumerate(steps):
        pltpu.make_async_copy(left, a_buf.at[i], a_sem.at[i]).start()
        for g, chunks in enumerate(rights):
            at = 0
            for chunk in chunks:
                wide = chunk.shape[1]
                into = w_bufs[g].at[i, :, pl.ds(at, wide)]
                pltpu.make_async_copy(chunk, into, w_sem.at[g, i]).start()
                at += wide

    def body(i, carry):
        pltpu.make_async_copy(a_buf.at[i], a_buf.at[i], a_sem.at[i]).wait()
        for g, acc in enumerate(accs):
            pltpu.make_async_copy(w_bufs[g].at[i], w_bufs[g].at[i], w_sem.at[g, i]).wait()
            acc[...] += jnp.dot(a_buf[i], w_bufs[g][i], preferred_element_type=jnp.float32)
        return carry

    lax.fori_loop(0, len(steps), body, 0)


def project_kernel(near, far, chunks, first, heads, factor, panel_ref, *refs):
    near_refs, far_refs, (scale_ref, cos_ref, sin_ref), rest = take(refs, near, far * chunks, 3)
    o_ref, a_buf, w_buf, acc, a_sem, w_sem = rest
    slots, _, depth = panel_ref.shape
    per = slots // (near + far)
    cols = acc.shape[1]
    steps = []
    for k in range(slots):
        p, rows = k // per, pl.ds(k % per * depth, depth)
        if p < near:
            right = [near_refs[p].at[rows, pl.ds(first, cols)]]
        else:
            at = (p - near) * chunks
            right = [ref.at[rows, :] for ref in far_refs[at : at + chunks]]
        steps.append((panel_ref.at[k], [right]))
    acc[...] = jnp.zeros_like(acc)
    multiply(steps, a_buf, [w_buf], [acc], a_sem, w_sem)
    scale = scale_ref[...] * factor
    for h in range(cols // HD):
        at = pl.ds(h * HD, HD)
        x = acc[:, at] * scale
        if h < heads:
            x = x * cos_ref[...] + pltpu.roll(x, HD // 2, 1) * sin_ref[...]
        o_ref[:, at] = x.astype(o_ref.dtype)


def project(panel, near, far, first, heads, factor, scale, cos, sin):
    slots, tok, depth = panel.shape
    chunks = len(far[0])
    cols = sum(w.shape[1] for w in far[0])
    hbm = pl.BlockSpec(memory_space=pl.ANY)
    vmem = pl.BlockSpec(memory_space=pltpu.VMEM)
    return pl.pallas_call(
        functools.partial(project_kernel, len(near), len(far), chunks, first, heads, factor),
        in_specs=[hbm] * (1 + len(near) + len(far) * chunks) + [vmem] * 3,
        out_specs=vmem,
        out_shape=jax.ShapeDtypeStruct((tok, cols), jnp.bfloat16),
        scratch_shapes=[
            pltpu.VMEM((slots, tok, depth), jnp.bfloat16),
            pltpu.VMEM((slots, depth, cols), jnp.bfloat16),
            pltpu.VMEM((tok, cols), jnp.float32),
            pltpu.SemaphoreType.DMA((slots,)),
            pltpu.SemaphoreType.DMA((1, slots)),
        ],
        compiler_params=pltpu.CompilerParams(vmem_limit_bytes=60 * MIB),
        cost_estimate=SHORT,
    )(panel, *near, *[w for pieces in far for w in pieces], scale, cos, sin)


def attend_kernel(parts, chunks, pair, r_ref, *refs):
    chunk_refs, pieces = refs[:chunks], refs[chunks : chunks + parts]
    o_ref, q_ref, turned, top, total, acc = refs[chunks + parts :]
    r = r_ref[0]
    tok = q_ref.shape[0]
    step = pl.program_id(0)
    per = pl.num_programs(0) // chunks
    for i in range(chunks):

        @pl.when(step // per == i)
        def _():
            q_ref[...] = chunk_refs[i][...]

    dims = (((1,), (1,)), ((), ()))

    @pl.when(step == 0)
    def _():
        for j in range(parts):
            turned[j] = pieces[j][:, HD:].T

    def scores(j, g):
        return lax.dot_general(
            pieces[j][:, :HD],
            q_ref[:, g * HD : (g + 1) * HD],
            dims,
            preferred_element_type=jnp.float32,
        )

    key = lax.broadcasted_iota(jnp.int32, (tok, tok), 0)
    query = lax.broadcasted_iota(jnp.int32, (tok, tok), 1)
    for g in range(pair):
        s = jnp.where(key <= query, scores(0, g), -jnp.inf)
        m = jnp.max(s, axis=0, keepdims=True)
        p = jnp.exp2(s - m)
        top[g] = m
        total[g] = jnp.sum(p, axis=0, keepdims=True)
        acc[g] = jnp.dot(turned[0], p.astype(jnp.bfloat16), preferred_element_type=jnp.float32)
    for j in range(1, parts):

        @pl.when(jnp.bitwise_xor(r, j) < r)
        def _():
            for g in range(pair):
                s = scores(j, g)
                m = jnp.maximum(top[g], jnp.max(s, axis=0, keepdims=True))
                keep = jnp.exp2(top[g] - m)
                p = jnp.exp2(s - m)
                top[g] = m
                total[g] = total[g] * keep + jnp.sum(p, axis=0, keepdims=True)
                acc[g] = acc[g] * keep + jnp.dot(
                    turned[j], p.astype(jnp.bfloat16), preferred_element_type=jnp.float32
                )

    for g in range(pair):
        o_ref[:, g * HD : (g + 1) * HD] = (acc[g] / total[g]).T.astype(o_ref.dtype)


def attend(r, queries, pieces):
    tok, cols = queries[0].shape
    chunks, parts = len(queries), len(pieces)
    pair = 2 if cols // HD % 2 == 0 else 1
    per = cols // (HD * pair)
    heads = chunks * cols // HD

    def query_spec(i):
        return pl.BlockSpec((tok, pair * HD), lambda h, r: (0, jnp.clip(h - i * per, 0, per - 1)))

    return pl.pallas_call(
        functools.partial(attend_kernel, parts, chunks, pair),
        grid_spec=pltpu.PrefetchScalarGridSpec(
            num_scalar_prefetch=1,
            grid=(chunks * per,),
            in_specs=[query_spec(i) for i in range(chunks)]
            + [pl.BlockSpec((tok, 2 * HD), lambda h, r: (0, 0)) for _ in pieces],
            out_specs=pl.BlockSpec((tok, pair * HD), lambda h, r: (0, h)),
            scratch_shapes=[
                pltpu.VMEM((tok, pair * HD), jnp.bfloat16),
                pltpu.VMEM((parts, HD, tok), jnp.bfloat16),
                pltpu.VMEM((pair, 1, tok), jnp.float32),
                pltpu.VMEM((pair, 1, tok), jnp.float32),
                pltpu.VMEM((pair, HD, tok), jnp.float32),
            ],
        ),
        out_shape=jax.ShapeDtypeStruct((tok, chunks * cols), jnp.bfloat16),
        compiler_params=pltpu.CompilerParams(
            dimension_semantics=("arbitrary",), vmem_limit_bytes=32 * MIB
        ),
        cost_estimate=SHORT,
    )(r.reshape(1), *queries, *pieces)


def finish_kernel(plan, n_refs, *refs):
    arrays, (*old, o_ref, a_buf, w_buf, acc, a_sem, w_sem) = take(refs, n_refs)
    depth = a_buf.shape[2]
    steps = []
    for panel, slot, column, weights, row in plan:
        left = arrays[panel].at[slot, :, pl.ds(column, depth)]
        steps.append((left, [[arrays[weights].at[pl.ds(row, depth), :]]]))
    acc[...] = old[0][...] if old else jnp.zeros_like(acc)
    multiply(steps, a_buf, [w_buf], [acc], a_sem, w_sem)
    o_ref[...] = acc[...].astype(o_ref.dtype)


def finish(arrays, plan, depth, dtype, total=None):
    tok = arrays[plan[0][0]].shape[1]
    cols = arrays[plan[0][3]].shape[1]
    n = len(plan)
    hbm = pl.BlockSpec(memory_space=pl.ANY)
    vmem = pl.BlockSpec(memory_space=pltpu.VMEM)
    old = [] if total is None else [total]
    return pl.pallas_call(
        functools.partial(finish_kernel, plan, len(arrays)),
        in_specs=[hbm] * len(arrays) + [vmem] * len(old),
        out_specs=vmem,
        out_shape=jax.ShapeDtypeStruct((tok, cols), dtype),
        scratch_shapes=[
            pltpu.VMEM((n, tok, depth), jnp.bfloat16),
            pltpu.VMEM((n, depth, cols), jnp.bfloat16),
            pltpu.VMEM((tok, cols), jnp.float32),
            pltpu.SemaphoreType.DMA((n,)),
            pltpu.SemaphoreType.DMA((1, n)),
        ],
        compiler_params=pltpu.CompilerParams(vmem_limit_bytes=60 * MIB),
        cost_estimate=SHORT,
    )(*arrays, *old)


def per_device(hidden, norm_gain, wq, wk, wv, wo):
    tok, feat = hidden.shape
    n_row, n_col = lax.axis_size("row"), lax.axis_size("col")
    r, c = lax.axis_index("row"), lax.axis_index("col")
    depth = feat * n_col
    rows = wq.shape[0]
    cols = wq.shape[1]

    kv_cols = wk.shape[1]
    group = max(1, HD // kv_cols)
    stacked = jnp.stack((wk, wv), axis=1)
    for bit in range(group.bit_length() - 1):
        other = swap(stacked, "col", 1 << bit)
        stacked = order_pair(stacked, other, c, bit, 2)
    stacked = stacked.reshape(rows, 2 * HD)

    n_heads = cols // HD
    first_heads = n_heads // 2
    late_heads = n_heads - first_heads
    if n_heads >= 4:
        last_heads = max(1, late_heads // 4)
        sizes = [first_heads // 2, first_heads - first_heads // 2, late_heads - last_heads]
        sizes.append(last_heads)
    else:
        sizes = [first_heads, late_heads]
    early = 2 if n_heads >= 4 else 1
    wide, rest = first_heads * HD, late_heads * HD
    chunks = [
        wq[:, sum(sizes[:i]) * HD : sum(sizes[: i + 1]) * HD] for i in range(len(sizes))
    ]

    def by_block(far):
        return [list(pieces) for pieces in zip(*far)]

    half = HD // 2
    positions = r * tok + jnp.arange(tok)
    freqs = 10000.0 ** (-jnp.arange(half).astype(jnp.float32) / half)
    angles = positions.astype(jnp.float32)[:, None] * freqs[None, :]
    cosine, sine = jnp.cos(angles), jnp.sin(angles)
    cosine = jnp.concatenate([cosine, cosine], axis=1)
    sine = jnp.concatenate([-sine, sine], axis=1)
    factor = HD ** (-0.5) * math.log2(math.e)

    per = rows // feat

    def put(panel, found):
        for source, first, piece in found:
            slot = (source // per ^ r) * per + source % per
            panel = lax.dynamic_update_slice(panel, piece[None], (slot, first, 0))
        return panel

    def put_hidden(panel, found):
        sums = []
        for source, first, piece in found:
            wider = piece.astype(jnp.float32)
            sums.append(jnp.sum(wider * wider, axis=1))
            gain = lax.dynamic_slice(norm_gain, (source * feat,), (feat,))
            panel = put(panel, [(source, first, (wider * gain).astype(jnp.bfloat16))])
        return panel, sums

    ring = Ring(hidden)
    hops = n_col // 2
    x_sent = exchange(stacked)
    gathering = gather_near(stacked)
    got_near = []
    panel, (squares,) = put_hidden(blank((n_col, tok, feat)), ring.found)
    for i in range(hops):
        last_hop = i == hops - 1
        beside = [panel, squares, cosine, sine, *gathering]
        ahead = chunks[i : i + 1] if i < len(sizes) - 1 else []
        if not last_hop and x_sent is not None:
            beside.append(x_sent)
        beside = ring.hop(beside=[*beside, *ahead])
        (panel, squares, cosine, sine), near, beside = take(beside, 4, len(gathering))
        panel, sums = put_hidden(panel, ring.found[-2:])
        squares += jnp.concatenate(sums) if last_hop else sums[0] + sums[1]
        got_near.append(near)
        if last_hop:
            break
        gathering = []
        if x_sent is not None:
            gathering = gather_near(beside[0])
            beside = beside[1:]
        x_sent = exchange(beside[0]) if ahead else None
        if i == hops - 2:
            gathering = [*gathering, *gather_near(after(wq, ring.last[0]))]
    blocks_near = len(got_near[0])
    kv_near, kv_far = got_near[0], got_near[1]
    q_near = got_near[-1][-blocks_near:]
    q_far = [near[:blocks_near] for near in got_near[2:] if len(near) > 0]
    scale = lax.rsqrt(squares / depth + 1e-05)[:, None]

    kv = project(panel, kv_near, by_block([kv_far]), 0, 1, 1.0, scale, cosine, sine)
    scale = after(scale, kv)
    queries = project(
        panel, q_near, by_block(q_far[:early]), 0, first_heads, factor, scale, cosine, sine
    )
    beside = [exchange(kv), queries, *gather_near(kv)]
    if x_sent is not None:
        beside.append(x_sent)
    kv_other, queries, *beside = lax.optimization_barrier(tuple(beside))
    kv_pieces, arrived = take(beside, blocks_near)
    kv_pieces = [*kv_pieces, *gather_near(kv_other)]
    late_far = [gather_near(piece) for piece in arrived]
    last_other = exchange(after(chunks[-1], kv_other))
    heads = attend(r, [queries], kv_pieces)

    def o_rows(first, wide):
        return wo.reshape(-1, cols, wo.shape[1])[:, first : first + wide].reshape(-1, wo.shape[1])

    split = cols - rest // 2 if rest >= 2 * HD else cols
    o_first = o_rows(0, split)
    ring = Ring(heads)
    first_panel = put(blank((n_col, tok, wide)), ring.found)
    second_panel = blank((n_col, tok, rest))
    last_other, o_first, first_panel, second_panel = ring.hop(
        beside=[last_other, o_first, first_panel, second_panel]
    )
    first_panel = put(first_panel, ring.found[-2:])
    o_first = exchange(o_first)
    far = gather_near(last_other)
    late_far = by_block([*late_far, far])
    queries = project(
        panel, q_near, late_far, wide, late_heads, factor, scale, cosine, sine
    )
    queries, first_panel = ring.hop(beside=[queries, first_panel])
    first_panel = put(first_panel, ring.found[-2:])
    o_near = gather_near(after(wo, queries))
    beside = ring.hop(beside=[attend(r, [queries], kv_pieces), first_panel, *o_near])
    (heads, first_panel), o_near = take(beside, 2)
    first_panel = put(first_panel, ring.found[-2:])
    second = Ring(heads)
    second_panel = put(second_panel, second.found)
    o_last = [o_rows(split, cols - split)] if split < cols else []
    plan = []
    for k in range(n_col):
        p, s = k // per, k % per
        plan.append((0, k, 0, 1 + p, s * (cols if p < blocks_near else split)))
    for i in range(hops):
        arrived, hop = ring.last, ring.hops
        ring.hop(*second.last)
        beside = [first_panel, second_panel, *o_last]
        if i == hops - 3:
            beside.append(o_first)
        if i == hops - 2:
            beside += gather_near(o_first)
        if i == hops - 1:
            beside.append(finish([first_panel, *o_near, *o_far], plan, wide, jnp.float32))
        beside = second.hop(*arrived, beside=beside)
        (first_panel, second_panel), o_last, beside = take(beside, 2, len(o_last))
        if ring.hops > hop:
            first_panel = put(first_panel, ring.found[-2:])
        second_panel = put(second_panel, second.found[-2:])
        if i == hops - 3:
            (o_first,) = beside
            o_other, o_last = [exchange(after(w, o_first)) for w in o_last], []
        if i == hops - 2:
            o_far = beside
    (total,) = beside

    part = math.gcd(rest, split - wide)
    plan = []
    for k in range(n_col):
        p, s = k // per, k % per
        near = p < blocks_near
        for at in range(0, rest if near else split - wide, part):
            plan.append((0, k, at, 1 + p, s * (cols if near else split) + wide + at))
    dtype = jnp.float32 if o_other else jnp.bfloat16
    total = finish([second_panel, *o_near, *o_far], plan, part, dtype, total)
    if o_other:
        far = gather_near(after(o_other[0], total))
        plan = [
            (0, k, split - wide, 1 + k // per - blocks_near, k % per * (cols - split))
            for k in range(n_col // 2, n_col)
        ]
        total = finish([second_panel, *far], plan, cols - split, jnp.bfloat16, total)
    return total


def solution(mesh):
    in_specs = (
        P("row", "col"),
        P(),
        P("row", "col"),
        P("row", "col"),
        P("row", "col"),
        P("row", "col"),
    )
    out_specs = P("row", "col")
    return jax.shard_map(
        per_device, mesh=mesh, in_specs=in_specs, out_specs=out_specs, check_vma=False
    )
```

```python
import functools
import math

import jax
import jax.numpy as jnp
from jax import lax
from jax.experimental import pallas as pl
from jax.experimental.pallas import tpu as pltpu
from jax.sharding import PartitionSpec as P

HD = 128
MIB = 1 << 20
SHORT = pl.CostEstimate(flops=1, bytes_accessed=1, transcendentals=0)


def after(array, *earlier):
    if not earlier:
        return array
    return lax.optimization_barrier((array, *earlier))[0]


def swap(array, axis, mask):
    return lax.ppermute(array, axis, [(i, i ^ mask) for i in range(lax.axis_size(axis))])


def row_bits():
    return [1 << b for b in reversed(range((lax.axis_size("row")).bit_length() - 1))]


def exchange(array, *earlier):
    return swap(after(array, *earlier), "row", row_bits()[0])


def gather_near(array, *earlier):
    pieces = {0: after(array, *earlier)}
    for bit in row_bits()[1:]:
        pieces.update({j ^ bit: swap(p, "row", bit) for j, p in pieces.items()})
    return [pieces[j] for j in range(len(pieces))]


def order_pair(mine, other, col_index, bit, axis_dim):
    upper = col_index // 2**bit % 2 == 1
    lower_part = jnp.where(upper, other, mine)
    upper_part = jnp.where(upper, mine, other)
    return jnp.concatenate([lower_part, upper_part], axis=axis_dim)


def ring_order(n):
    return list(range(0, n, 2)) + list(range(1, n, 2))[::-1]


def ring_source(c, hops, n):
    at = jnp.where(c % 2 == 0, c // 2, n - 1 - c // 2)
    at = (at - hops) % n
    return jnp.where(at < n // 2, 2 * at, 2 * (n - 1 - at) + 1)


class Ring:
    def __init__(self, block):
        n = lax.axis_size("col")
        order = ring_order(n)
        self.n, self.hops = n, 0
        self.up = [(order[i], order[(i + 1) % n]) for i in range(n)]
        self.down = [(b, a) for a, b in self.up]
        self.found = [(lax.axis_index("col"), 0, block)]
        self.last = [block, block]

    def hop(self, *earlier, beside=()):
        if self.hops == self.n // 2:
            return beside
        c, own = self.found[0][0], self.found[0][2]
        rows = own.shape[0] // 2
        self.hops += 1
        end = self.hops == self.n // 2
        below, above = self.last
        if end:
            below, above = below[:rows], above[rows:]
        if earlier:
            below, above = lax.optimization_barrier((below, above, *earlier))[:2]
        below = lax.ppermute(below, "col", self.up)
        above = lax.ppermute(above, "col", self.down)
        below, above, *beside = lax.optimization_barrier((below, above, *beside))
        self.last = [below, above]
        self.found.append((ring_source(c, self.hops, self.n), 0, self.last[0]))
        self.found.append((ring_source(c, -self.hops, self.n), rows if end else 0, self.last[1]))
        return beside


def blank(shape):
    return pl.pallas_call(
        lambda o_ref: None,
        out_specs=pl.BlockSpec(memory_space=pl.ANY),
        out_shape=jax.ShapeDtypeStruct(shape, jnp.bfloat16),
    )()


def take(refs, *counts):
    out, at = [], 0
    for n in counts:
        out.append(refs[at : at + n])
        at += n
    return *out, refs[at:]


def multiply(steps, a_buf, w_bufs, accs, a_sem, w_sem):
    for i, (left, rights) in enumerate(steps):
        pltpu.make_async_copy(left, a_buf.at[i], a_sem.at[i]).start()
        for g, chunks in enumerate(rights):
            at = 0
            for chunk in chunks:
                wide = chunk.shape[1]
                into = w_bufs[g].at[i, :, pl.ds(at, wide)]
                pltpu.make_async_copy(chunk, into, w_sem.at[g, i]).start()
                at += wide

    def body(i, carry):
        pltpu.make_async_copy(a_buf.at[i], a_buf.at[i], a_sem.at[i]).wait()
        for g, acc in enumerate(accs):
            pltpu.make_async_copy(w_bufs[g].at[i], w_bufs[g].at[i], w_sem.at[g, i]).wait()
            acc[...] += jnp.dot(a_buf[i], w_bufs[g][i], preferred_element_type=jnp.float32)
        return carry

    lax.fori_loop(0, len(steps), body, 0)


def project_kernel(near, far, chunks, first, heads, factor, panel_ref, *refs):
    near_refs, far_refs, (scale_ref, cos_ref, sin_ref), rest = take(refs, near, far * chunks, 3)
    o_ref, a_buf, w_buf, acc, a_sem, w_sem = rest
    slots, _, depth = panel_ref.shape
    per = slots // (near + far)
    cols = acc.shape[1]
    steps = []
    for k in range(slots):
        p, rows = k // per, pl.ds(k % per * depth, depth)
        if p < near:
            right = [near_refs[p].at[rows, pl.ds(first, cols)]]
        else:
            at = (p - near) * chunks
            right = [ref.at[rows, :] for ref in far_refs[at : at + chunks]]
        steps.append((panel_ref.at[k], [right]))
    acc[...] = jnp.zeros_like(acc)
    multiply(steps, a_buf, [w_buf], [acc], a_sem, w_sem)
    scale = scale_ref[...] * factor
    for h in range(cols // HD):
        at = pl.ds(h * HD, HD)
        x = acc[:, at] * scale
        if h < heads:
            x = x * cos_ref[...] + pltpu.roll(x, HD // 2, 1) * sin_ref[...]
        o_ref[:, at] = x.astype(o_ref.dtype)


def project(panel, near, far, first, heads, factor, scale, cos, sin):
    slots, tok, depth = panel.shape
    chunks = len(far[0])
    cols = sum(w.shape[1] for w in far[0])
    hbm = pl.BlockSpec(memory_space=pl.ANY)
    vmem = pl.BlockSpec(memory_space=pltpu.VMEM)
    return pl.pallas_call(
        functools.partial(project_kernel, len(near), len(far), chunks, first, heads, factor),
        in_specs=[hbm] * (1 + len(near) + len(far) * chunks) + [vmem] * 3,
        out_specs=vmem,
        out_shape=jax.ShapeDtypeStruct((tok, cols), jnp.bfloat16),
        scratch_shapes=[
            pltpu.VMEM((slots, tok, depth), jnp.bfloat16),
            pltpu.VMEM((slots, depth, cols), jnp.bfloat16),
            pltpu.VMEM((tok, cols), jnp.float32),
            pltpu.SemaphoreType.DMA((slots,)),
            pltpu.SemaphoreType.DMA((1, slots)),
        ],
        compiler_params=pltpu.CompilerParams(vmem_limit_bytes=60 * MIB),
        cost_estimate=SHORT,
    )(panel, *near, *[w for pieces in far for w in pieces], scale, cos, sin)


def attend_kernel(parts, chunks, pair, r_ref, *refs):
    chunk_refs, pieces = refs[:chunks], refs[chunks : chunks + parts]
    o_ref, q_ref, turned, top, total, acc = refs[chunks + parts :]
    r = r_ref[0]
    tok = q_ref.shape[0]
    step = pl.program_id(0)
    per = pl.num_programs(0) // chunks
    for i in range(chunks):

        @pl.when(step // per == i)
        def _():
            q_ref[...] = chunk_refs[i][...]

    dims = (((1,), (1,)), ((), ()))

    @pl.when(step == 0)
    def _():
        for j in range(parts):
            turned[j] = pieces[j][:, HD:].T

    def scores(j, g):
        return lax.dot_general(
            pieces[j][:, :HD],
            q_ref[:, g * HD : (g + 1) * HD],
            dims,
            preferred_element_type=jnp.float32,
        )

    key = lax.broadcasted_iota(jnp.int32, (tok, tok), 0)
    query = lax.broadcasted_iota(jnp.int32, (tok, tok), 1)
    for g in range(pair):
        s = jnp.where(key <= query, scores(0, g), -jnp.inf)
        m = jnp.max(s, axis=0, keepdims=True)
        p = jnp.exp2(s - m)
        top[g] = m
        total[g] = jnp.sum(p, axis=0, keepdims=True)
        acc[g] = jnp.dot(turned[0], p.astype(jnp.bfloat16), preferred_element_type=jnp.float32)
    for j in range(1, parts):

        @pl.when(jnp.bitwise_xor(r, j) < r)
        def _():
            for g in range(pair):
                s = scores(j, g)
                m = jnp.maximum(top[g], jnp.max(s, axis=0, keepdims=True))
                keep = jnp.exp2(top[g] - m)
                p = jnp.exp2(s - m)
                top[g] = m
                total[g] = total[g] * keep + jnp.sum(p, axis=0, keepdims=True)
                acc[g] = acc[g] * keep + jnp.dot(
                    turned[j], p.astype(jnp.bfloat16), preferred_element_type=jnp.float32
                )

    for g in range(pair):
        o_ref[:, g * HD : (g + 1) * HD] = (acc[g] / total[g]).T.astype(o_ref.dtype)


def attend(r, queries, pieces):
    tok, cols = queries[0].shape
    chunks, parts = len(queries), len(pieces)
    pair = 2 if cols // HD % 2 == 0 else 1
    per = cols // (HD * pair)
    heads = chunks * cols // HD

    def query_spec(i):
        return pl.BlockSpec((tok, pair * HD), lambda h, r: (0, jnp.clip(h - i * per, 0, per - 1)))

    return pl.pallas_call(
        functools.partial(attend_kernel, parts, chunks, pair),
        grid_spec=pltpu.PrefetchScalarGridSpec(
            num_scalar_prefetch=1,
            grid=(chunks * per,),
            in_specs=[query_spec(i) for i in range(chunks)]
            + [pl.BlockSpec((tok, 2 * HD), lambda h, r: (0, 0)) for _ in pieces],
            out_specs=pl.BlockSpec((tok, pair * HD), lambda h, r: (0, h)),
            scratch_shapes=[
                pltpu.VMEM((tok, pair * HD), jnp.bfloat16),
                pltpu.VMEM((parts, HD, tok), jnp.bfloat16),
                pltpu.VMEM((pair, 1, tok), jnp.float32),
                pltpu.VMEM((pair, 1, tok), jnp.float32),
                pltpu.VMEM((pair, HD, tok), jnp.float32),
            ],
        ),
        out_shape=jax.ShapeDtypeStruct((tok, chunks * cols), jnp.bfloat16),
        compiler_params=pltpu.CompilerParams(
            dimension_semantics=("arbitrary",), vmem_limit_bytes=32 * MIB
        ),
        cost_estimate=SHORT,
    )(r.reshape(1), *queries, *pieces)


def finish_kernel(column, depth, per, first, r_ref, panel_ref, gathered_ref, *refs):
    *old, o_ref, a_buf, w_buf, acc, a_sem, w_sem = refs
    steps = []
    stride = gathered_ref.shape[1] // per
    for k in range(panel_ref.shape[0]):
        block = jnp.bitwise_xor(r_ref[0], k // per)
        left = panel_ref.at[k, :, pl.ds(column, depth)]
        right = gathered_ref.at[block, pl.ds(k % per * stride + first, depth), :]
        steps.append((left, [[right]]))
    acc[...] = old[0][...] if old else jnp.zeros_like(acc)
    multiply(steps, a_buf, [w_buf], [acc], a_sem, w_sem)
    o_ref[...] = acc[...].astype(o_ref.dtype)


def finish(r, panel, column, gathered, per, first, depth, dtype, total=None):
    n, tok, _ = panel.shape
    cols = gathered.shape[2]
    hbm = pl.BlockSpec(memory_space=pl.ANY)
    vmem = pl.BlockSpec(memory_space=pltpu.VMEM)
    old = [] if total is None else [total]
    return pl.pallas_call(
        functools.partial(finish_kernel, column, depth, per, first),
        in_specs=[pl.BlockSpec(memory_space=pltpu.SMEM)] + [hbm] * 2 + [vmem] * len(old),
        out_specs=vmem,
        out_shape=jax.ShapeDtypeStruct((tok, cols), dtype),
        scratch_shapes=[
            pltpu.VMEM((n, tok, depth), jnp.bfloat16),
            pltpu.VMEM((n, depth, cols), jnp.bfloat16),
            pltpu.VMEM((tok, cols), jnp.float32),
            pltpu.SemaphoreType.DMA((n,)),
            pltpu.SemaphoreType.DMA((1, n)),
        ],
        compiler_params=pltpu.CompilerParams(vmem_limit_bytes=60 * MIB),
        cost_estimate=SHORT,
    )(r.reshape(1), panel, gathered, *old)


def per_device(hidden, norm_gain, wq, wk, wv, wo):
    tok, feat = hidden.shape
    n_row, n_col = lax.axis_size("row"), lax.axis_size("col")
    r, c = lax.axis_index("row"), lax.axis_index("col")
    depth = feat * n_col
    rows = wq.shape[0]
    cols = wq.shape[1]

    kv_cols = wk.shape[1]
    group = max(1, HD // kv_cols)
    stacked = jnp.stack((wk, wv), axis=1)
    for bit in range(group.bit_length() - 1):
        other = swap(stacked, "col", 1 << bit)
        stacked = order_pair(stacked, other, c, bit, 2)
    stacked = stacked.reshape(rows, 2 * HD)

    n_heads = cols // HD
    first_heads = n_heads // 2
    late_heads = n_heads - first_heads
    if n_heads >= 4:
        last_heads = max(1, late_heads // 4)
        sizes = [first_heads // 2, first_heads - first_heads // 2, late_heads - last_heads]
        sizes.append(last_heads)
    else:
        sizes = [first_heads, late_heads]
    early = 2 if n_heads >= 4 else 1
    wide, rest = first_heads * HD, late_heads * HD
    chunks = [
        wq[:, sum(sizes[:i]) * HD : sum(sizes[: i + 1]) * HD] for i in range(len(sizes))
    ]

    def by_block(far):
        return [list(pieces) for pieces in zip(*far)]

    half = HD // 2
    positions = r * tok + jnp.arange(tok)
    freqs = 10000.0 ** (-jnp.arange(half).astype(jnp.float32) / half)
    angles = positions.astype(jnp.float32)[:, None] * freqs[None, :]
    cosine, sine = jnp.cos(angles), jnp.sin(angles)
    cosine = jnp.concatenate([cosine, cosine], axis=1)
    sine = jnp.concatenate([-sine, sine], axis=1)
    factor = HD ** (-0.5) * math.log2(math.e)

    per = rows // feat

    def put(panel, found):
        for source, first, piece in found:
            slot = (source // per ^ r) * per + source % per
            panel = lax.dynamic_update_slice(panel, piece[None], (slot, first, 0))
        return panel

    def put_hidden(panel, found):
        sums = []
        for source, first, piece in found:
            wider = piece.astype(jnp.float32)
            sums.append(jnp.sum(wider * wider, axis=1))
            gain = lax.dynamic_slice(norm_gain, (source * feat,), (feat,))
            panel = put(panel, [(source, first, (wider * gain).astype(jnp.bfloat16))])
        return panel, sums

    ring = Ring(hidden)
    hops = n_col // 2
    x_sent = exchange(stacked)
    gathering = gather_near(stacked)
    got_near = []
    panel, (squares,) = put_hidden(blank((n_col, tok, feat)), ring.found)
    for i in range(hops):
        last_hop = i == hops - 1
        beside = [panel, squares, cosine, sine, *gathering]
        ahead = chunks[i : i + 1] if i < len(sizes) - 1 else []
        if not last_hop and x_sent is not None:
            beside.append(x_sent)
        beside = ring.hop(beside=[*beside, *ahead])
        (panel, squares, cosine, sine), near, beside = take(beside, 4, len(gathering))
        panel, sums = put_hidden(panel, ring.found[-2:])
        squares += jnp.concatenate(sums) if last_hop else sums[0] + sums[1]
        got_near.append(near)
        if last_hop:
            break
        gathering = []
        if x_sent is not None:
            gathering = gather_near(beside[0])
            beside = beside[1:]
        x_sent = exchange(beside[0]) if ahead else None
        if i == hops - 2:
            gathering = [*gathering, *gather_near(after(wq, ring.last[0]))]
    blocks_near = len(got_near[0])
    kv_near, kv_far = got_near[0], got_near[1]
    q_near = got_near[-1][-blocks_near:]
    q_far = [near[:blocks_near] for near in got_near[2:] if len(near) > 0]
    scale = lax.rsqrt(squares / depth + 1e-05)[:, None]

    kv = project(panel, kv_near, by_block([kv_far]), 0, 1, 1.0, scale, cosine, sine)
    scale = after(scale, kv)
    queries = project(
        panel, q_near, by_block(q_far[:early]), 0, first_heads, factor, scale, cosine, sine
    )
    beside = [exchange(kv), queries, chunks[-1], *gather_near(kv)]
    if x_sent is not None:
        beside.append(x_sent)
    kv_other, queries, last_chunk, *beside = lax.optimization_barrier(tuple(beside))
    kv_pieces, arrived = take(beside, blocks_near)
    kv_pieces = [*kv_pieces, *gather_near(kv_other)]
    late_far = [gather_near(piece) for piece in arrived]
    last_other = exchange(last_chunk)
    split = cols - rest // 2 if rest >= 2 * HD else cols

    def o_rows(first, last, *earlier):
        piece = wo.reshape(-1, cols, wo.shape[1])[:, first:last].reshape(-1, wo.shape[1])
        return lax.all_gather(after(piece, *earlier), "row")

    o_first = o_rows(0, split, kv_other)
    heads = attend(r, [queries], kv_pieces)

    ring = Ring(heads)
    first_panel = put(blank((n_col, tok, wide)), ring.found)
    second_panel = blank((n_col, tok, rest))
    last_other, first_panel, second_panel = ring.hop(
        beside=[last_other, first_panel, second_panel]
    )
    first_panel = put(first_panel, ring.found[-2:])
    far = gather_near(last_other)
    first_panel, *far = ring.hop(beside=[first_panel, *far])
    first_panel = put(first_panel, ring.found[-2:])
    late_far = by_block([*late_far, far])
    queries = project(
        panel, q_near, late_far, wide, late_heads, factor, scale, cosine, sine
    )
    queries, first_panel = ring.hop(beside=[queries, first_panel])
    first_panel = put(first_panel, ring.found[-2:])
    heads = attend(r, [queries], kv_pieces)
    for i in range(3, hops):
        heads, first_panel = ring.hop(beside=[heads, first_panel])
        first_panel = put(first_panel, ring.found[-2:])
    second = Ring(heads)
    second_panel = put(second_panel, second.found)
    o_last = None
    for i in range(hops):
        (second_panel,) = second.hop(beside=[second_panel])
        second_panel = put(second_panel, second.found[-2:])
        if i == hops - 3 and split < cols:
            o_last = o_rows(split, cols, o_first, *second.last)

    total = finish(r, first_panel, 0, o_first, per, 0, wide, jnp.float32)
    total = after(total, *second.last)
    dtype = jnp.bfloat16 if o_last is None else jnp.float32
    total = finish(r, second_panel, 0, o_first, per, wide, split - wide, dtype, total)
    if o_last is not None:
        total = finish(
            r, second_panel, split - wide, o_last, per, 0, cols - split, jnp.bfloat16, total
        )
    return total


def solution(mesh):
    in_specs = (
        P("row", "col"),
        P(),
        P("row", "col"),
        P("row", "col"),
        P("row", "col"),
        P("row", "col"),
    )
    out_specs = P("row", "col")
    return jax.shard_map(
        per_device, mesh=mesh, in_specs=in_specs, out_specs=out_specs, check_vma=False
    )
```

```python
import functools
import math

import jax
import jax.numpy as jnp
from jax import lax
from jax.experimental import pallas as pl
from jax.experimental.pallas import tpu as pltpu
from jax.sharding import PartitionSpec as P

HD = 128
MIB = 1 << 20
SHORT = pl.CostEstimate(flops=1, bytes_accessed=1, transcendentals=0)


def after(array, *earlier):
    if not earlier:
        return array
    return lax.optimization_barrier((array, *earlier))[0]


def swap(array, axis, mask):
    return lax.ppermute(array, axis, [(i, i ^ mask) for i in range(lax.axis_size(axis))])


def row_bits():
    return [1 << b for b in reversed(range((lax.axis_size("row")).bit_length() - 1))]


def exchange(array, *earlier):
    return swap(after(array, *earlier), "row", row_bits()[0])


def gather_near(array, *earlier):
    pieces = {0: after(array, *earlier)}
    for bit in row_bits()[1:]:
        pieces.update({j ^ bit: swap(p, "row", bit) for j, p in pieces.items()})
    return [pieces[j] for j in range(len(pieces))]


def order_pair(mine, other, col_index, bit, axis_dim):
    upper = col_index // 2**bit % 2 == 1
    lower_part = jnp.where(upper, other, mine)
    upper_part = jnp.where(upper, mine, other)
    return jnp.concatenate([lower_part, upper_part], axis=axis_dim)


def ring_order(n):
    return list(range(0, n, 2)) + list(range(1, n, 2))[::-1]


def ring_source(c, hops, n):
    at = jnp.where(c % 2 == 0, c // 2, n - 1 - c // 2)
    at = (at - hops) % n
    return jnp.where(at < n // 2, 2 * at, 2 * (n - 1 - at) + 1)


def take(refs, *counts):
    out, at = [], 0
    for n in counts:
        out.append(refs[at : at + n])
        at += n
    return *out, refs[at:]


class Ring:
    def __init__(self, block, pieces):
        n = lax.axis_size("col")
        order = ring_order(n)
        self.n, self.hops = n, 0
        self.up = [(order[i], order[(i + 1) % n]) for i in range(n)]
        self.down = [(b, a) for a, b in self.up]
        self.rows = block.shape[0]
        self.found = [(lax.axis_index("col"), 0, block)]
        self.height = self.rows // pieces
        parts = [block[i * self.height : (i + 1) * self.height] for i in range(pieces)]
        self.last = [(p, p) for p in parts]

    def hop(self, beside=()):
        if self.hops == self.n // 2:
            return [], list(beside)
        c, half = self.found[0][0], self.rows // 2
        self.hops += 1
        found = []
        for i, (below, above) in enumerate(self.last):
            top = i * self.height
            firsts = [top, top]
            sends = [(below, self.up), (above, self.down)]
            if self.hops == self.n // 2:
                if len(self.last) == 1:
                    sends = [(below[:half], self.up), (above[half:], self.down)]
                    firsts = [0, half]
                else:
                    sends = [sends[0], None] if top < half else [None, sends[1]]
            got = [None if s is None else lax.ppermute(s[0], "col", s[1]) for s in sends]
            more = list(beside) if i == len(self.last) - 1 else []
            here = [g for g in got if g is not None]
            here, more = take(lax.optimization_barrier((*here, *more)), len(here))
            here = list(here)
            got = [None if g is None else here.pop(0) for g in got]
            self.last[i] = tuple(got)
            for way, piece in enumerate(got):
                if piece is not None:
                    hops = self.hops if way == 0 else -self.hops
                    found.append((ring_source(c, hops, self.n), firsts[way], piece))
        self.found += found
        return found, list(more)


def blank(shape):
    return pl.pallas_call(
        lambda o_ref: None,
        out_specs=pl.BlockSpec(memory_space=pl.ANY),
        out_shape=jax.ShapeDtypeStruct(shape, jnp.bfloat16),
    )()


def multiply(steps, a_buf, w_bufs, accs, a_sem, w_sem):
    for i, (left, rights) in enumerate(steps):
        pltpu.make_async_copy(left, a_buf.at[i], a_sem.at[i]).start()
        for g, chunks in enumerate(rights):
            at = 0
            for chunk in chunks:
                wide = chunk.shape[1]
                into = w_bufs[g].at[i, :, pl.ds(at, wide)]
                pltpu.make_async_copy(chunk, into, w_sem.at[g, i]).start()
                at += wide

    def body(i, carry):
        pltpu.make_async_copy(a_buf.at[i], a_buf.at[i], a_sem.at[i]).wait()
        for g, acc in enumerate(accs):
            pltpu.make_async_copy(w_bufs[g].at[i], w_bufs[g].at[i], w_sem.at[g, i]).wait()
            acc[...] += jnp.dot(a_buf[i], w_bufs[g][i], preferred_element_type=jnp.float32)
        return carry

    lax.fori_loop(0, len(steps), body, 0)


def project_kernel(near, far, chunks, first, heads, factor, panel_ref, *refs):
    near_refs, far_refs, (scale_ref, cos_ref, sin_ref), rest = take(refs, near, far * chunks, 3)
    o_ref, a_buf, w_buf, acc, a_sem, w_sem = rest
    slots, _, depth = panel_ref.shape
    per = slots // (near + far)
    cols = acc.shape[1]
    steps = []
    for k in range(slots):
        p, rows = k // per, pl.ds(k % per * depth, depth)
        if p < near:
            right = [near_refs[p].at[rows, pl.ds(first, cols)]]
        else:
            at = (p - near) * chunks
            right = [ref.at[rows, :] for ref in far_refs[at : at + chunks]]
        steps.append((panel_ref.at[k], [right]))
    acc[...] = jnp.zeros_like(acc)
    multiply(steps, a_buf, [w_buf], [acc], a_sem, w_sem)
    scale = scale_ref[...] * factor
    for h in range(cols // HD):
        at = pl.ds(h * HD, HD)
        x = acc[:, at] * scale
        if h < heads:
            x = x * cos_ref[...] + pltpu.roll(x, HD // 2, 1) * sin_ref[...]
        o_ref[:, at] = x.astype(o_ref.dtype)


def project(panel, near, far, first, heads, factor, scale, cos, sin):
    slots, tok, depth = panel.shape
    chunks = len(far[0])
    cols = sum(w.shape[1] for w in far[0])
    hbm = pl.BlockSpec(memory_space=pl.ANY)
    vmem = pl.BlockSpec(memory_space=pltpu.VMEM)
    return pl.pallas_call(
        functools.partial(project_kernel, len(near), len(far), chunks, first, heads, factor),
        in_specs=[hbm] * (1 + len(near) + len(far) * chunks) + [vmem] * 3,
        out_specs=vmem,
        out_shape=jax.ShapeDtypeStruct((tok, cols), jnp.bfloat16),
        scratch_shapes=[
            pltpu.VMEM((slots, tok, depth), jnp.bfloat16),
            pltpu.VMEM((slots, depth, cols), jnp.bfloat16),
            pltpu.VMEM((tok, cols), jnp.float32),
            pltpu.SemaphoreType.DMA((slots,)),
            pltpu.SemaphoreType.DMA((1, slots)),
        ],
        compiler_params=pltpu.CompilerParams(vmem_limit_bytes=60 * MIB),
        cost_estimate=SHORT,
    )(panel, *near, *[w for pieces in far for w in pieces], scale, cos, sin)


def attend_kernel(parts, chunks, pair, r_ref, *refs):
    chunk_refs, pieces = refs[:chunks], refs[chunks : chunks + parts]
    o_ref, q_ref, turned, top, total, acc = refs[chunks + parts :]
    r = r_ref[0]
    tok = q_ref.shape[0]
    step = pl.program_id(0)
    per = pl.num_programs(0) // chunks
    for i in range(chunks):

        @pl.when(step // per == i)
        def _():
            q_ref[...] = chunk_refs[i][...]

    dims = (((1,), (1,)), ((), ()))

    @pl.when(step == 0)
    def _():
        for j in range(parts):
            turned[j] = pieces[j][:, HD:].T

    def scores(j, g):
        return lax.dot_general(
            pieces[j][:, :HD],
            q_ref[:, g * HD : (g + 1) * HD],
            dims,
            preferred_element_type=jnp.float32,
        )

    key = lax.broadcasted_iota(jnp.int32, (tok, tok), 0)
    query = lax.broadcasted_iota(jnp.int32, (tok, tok), 1)
    for g in range(pair):
        s = jnp.where(key <= query, scores(0, g), -jnp.inf)
        m = jnp.max(s, axis=0, keepdims=True)
        p = jnp.exp2(s - m)
        top[g] = m
        total[g] = jnp.sum(p, axis=0, keepdims=True)
        acc[g] = jnp.dot(turned[0], p.astype(jnp.bfloat16), preferred_element_type=jnp.float32)
    for j in range(1, parts):

        @pl.when(jnp.bitwise_xor(r, j) < r)
        def _():
            for g in range(pair):
                s = scores(j, g)
                m = jnp.maximum(top[g], jnp.max(s, axis=0, keepdims=True))
                keep = jnp.exp2(top[g] - m)
                p = jnp.exp2(s - m)
                top[g] = m
                total[g] = total[g] * keep + jnp.sum(p, axis=0, keepdims=True)
                acc[g] = acc[g] * keep + jnp.dot(
                    turned[j], p.astype(jnp.bfloat16), preferred_element_type=jnp.float32
                )

    for g in range(pair):
        o_ref[:, g * HD : (g + 1) * HD] = (acc[g] / total[g]).T.astype(o_ref.dtype)


def attend(r, queries, pieces):
    tok, cols = queries[0].shape
    chunks, parts = len(queries), len(pieces)
    pair = 2 if cols // HD % 2 == 0 else 1
    per = cols // (HD * pair)
    heads = chunks * cols // HD

    def query_spec(i):
        return pl.BlockSpec((tok, pair * HD), lambda h, r: (0, jnp.clip(h - i * per, 0, per - 1)))

    return pl.pallas_call(
        functools.partial(attend_kernel, parts, chunks, pair),
        grid_spec=pltpu.PrefetchScalarGridSpec(
            num_scalar_prefetch=1,
            grid=(chunks * per,),
            in_specs=[query_spec(i) for i in range(chunks)]
            + [pl.BlockSpec((tok, 2 * HD), lambda h, r: (0, 0)) for _ in pieces],
            out_specs=pl.BlockSpec((tok, pair * HD), lambda h, r: (0, h)),
            scratch_shapes=[
                pltpu.VMEM((tok, pair * HD), jnp.bfloat16),
                pltpu.VMEM((parts, HD, tok), jnp.bfloat16),
                pltpu.VMEM((pair, 1, tok), jnp.float32),
                pltpu.VMEM((pair, 1, tok), jnp.float32),
                pltpu.VMEM((pair, HD, tok), jnp.float32),
            ],
        ),
        out_shape=jax.ShapeDtypeStruct((tok, chunks * cols), jnp.bfloat16),
        compiler_params=pltpu.CompilerParams(
            dimension_semantics=("arbitrary",), vmem_limit_bytes=32 * MIB
        ),
        cost_estimate=SHORT,
    )(r.reshape(1), *queries, *pieces)


def finish_kernel(most, per, first, depth, count, r_ref, panel_ref, gathered_ref, *refs):
    pieces, (*old, o_ref, a_buf, w_buf, acc, a_sem, w_sem) = take(refs, count)
    steps = []
    slots, _, wide = panel_ref.shape
    stride = gathered_ref.shape[1] // per
    for k in range(slots):
        block = jnp.bitwise_xor(r_ref[0], k // per)
        for at in range(0, wide, depth):
            if at < most:
                row = k % per * stride + first + at
                right = gathered_ref.at[block, pl.ds(row, depth), :]
            else:
                row = k % per * (wide - most) + at - most
                right = pieces[k // per].at[pl.ds(row, depth), :]
            steps.append((panel_ref.at[k, :, pl.ds(at, depth)], [[right]]))
    acc[...] = old[0][...] if old else jnp.zeros_like(acc)
    multiply(steps, a_buf, [w_buf], [acc], a_sem, w_sem)
    o_ref[...] = acc[...].astype(o_ref.dtype)


def finish(r, panel, most, gathered, per, first, pieces, dtype, total=None):
    n, tok, wide = panel.shape
    cols = gathered.shape[2]
    most = most or wide
    depth = math.gcd(most, wide)
    count = n * wide // depth
    hbm = pl.BlockSpec(memory_space=pl.ANY)
    vmem = pl.BlockSpec(memory_space=pltpu.VMEM)
    old = [] if total is None else [total]
    return pl.pallas_call(
        functools.partial(finish_kernel, most, per, first, depth, len(pieces)),
        in_specs=[pl.BlockSpec(memory_space=pltpu.SMEM)]
        + [hbm] * (2 + len(pieces))
        + [vmem] * len(old),
        out_specs=vmem,
        out_shape=jax.ShapeDtypeStruct((tok, cols), dtype),
        scratch_shapes=[
            pltpu.VMEM((count, tok, depth), jnp.bfloat16),
            pltpu.VMEM((count, depth, cols), jnp.bfloat16),
            pltpu.VMEM((tok, cols), jnp.float32),
            pltpu.SemaphoreType.DMA((count,)),
            pltpu.SemaphoreType.DMA((1, count)),
        ],
        compiler_params=pltpu.CompilerParams(vmem_limit_bytes=60 * MIB),
        cost_estimate=SHORT,
    )(r.reshape(1), panel, gathered, *pieces, *old)


def per_device(hidden, norm_gain, wq, wk, wv, wo):
    tok, feat = hidden.shape
    n_row, n_col = lax.axis_size("row"), lax.axis_size("col")
    r, c = lax.axis_index("row"), lax.axis_index("col")
    depth = feat * n_col
    rows = wq.shape[0]
    cols = wq.shape[1]

    kv_cols = wk.shape[1]
    group = max(1, HD // kv_cols)
    stacked = jnp.stack((wk, wv), axis=1)
    for bit in range(group.bit_length() - 1):
        other = swap(stacked, "col", 1 << bit)
        stacked = order_pair(stacked, other, c, bit, 2)
    stacked = stacked.reshape(rows, 2 * HD)

    n_heads = cols // HD
    first_heads = n_heads // 2
    late_heads = n_heads - first_heads
    if n_heads >= 4:
        eighth = max(1, n_heads // 8)
        sizes = [first_heads // 2, first_heads - first_heads // 2, eighth]
        sizes += [n for n in (late_heads - 2 * eighth, eighth) if n > 0]
    else:
        sizes = [first_heads, late_heads]
    early = 2 if n_heads >= 4 else 1
    wide, rest = first_heads * HD, late_heads * HD
    chunks = [
        wq[:, sum(sizes[:i]) * HD : sum(sizes[: i + 1]) * HD] for i in range(len(sizes))
    ]

    def by_block(far):
        return [list(pieces) for pieces in zip(*far)]

    half = HD // 2
    positions = r * tok + jnp.arange(tok)
    freqs = 10000.0 ** (-jnp.arange(half).astype(jnp.float32) / half)
    angles = positions.astype(jnp.float32)[:, None] * freqs[None, :]
    cosine, sine = jnp.cos(angles), jnp.sin(angles)
    cosine = jnp.concatenate([cosine, cosine], axis=1)
    sine = jnp.concatenate([-sine, sine], axis=1)
    factor = HD ** (-0.5) * math.log2(math.e)

    per = rows // feat

    def put(panel, found):
        for source, first, piece in found:
            slot = (source // per ^ r) * per + source % per
            panel = lax.dynamic_update_slice(panel, piece[None], (slot, first, 0))
        return panel

    def put_hidden(panel, squares, found):
        for source, first, piece in found:
            wider = piece.astype(jnp.float32)
            sums = jnp.sum(wider * wider, axis=1)
            for h in range(2):
                if first <= h * tok // 2 < first + piece.shape[0]:
                    at = h * tok // 2 - first
                    squares[h] += sums[at : at + tok // 2]
            gain = lax.dynamic_slice(norm_gain, (source * feat,), (feat,))
            panel = put(panel, [(source, first, (wider * gain).astype(jnp.bfloat16))])
        return panel, squares

    ring = Ring(hidden, 1)
    hops = n_col // 2
    x_sent = exchange(stacked)
    got_x = []
    zeros = [jnp.zeros((tok // 2,), jnp.float32)] * 2
    panel, squares = put_hidden(blank((n_col, tok, feat)), zeros, ring.found)
    for i in range(hops):
        last_hop = i == hops - 1
        tie = ring.last[0][1]
        sent = [] if x_sent is None else [x_sent]
        ahead = chunks[i : i + 1] if i < len(sizes) - 1 else []
        beside = [panel, *squares, cosine, sine, *sent, *ahead]
        if last_hop:
            near = gather_near(after(stacked, tie))
            kv_weights = [*near, *gather_near(after(got_x[0], tie))]
            beside += kv_weights
        found, beside = ring.hop(beside)
        (panel, *squares, cosine, sine), beside = take(beside, 5)
        panel, squares = put_hidden(panel, squares, found)
        sent, ahead, kv_weights = take(beside, len(sent), len(ahead))
        got_x += sent
        x_sent = exchange(ahead[0]) if ahead else None
    blocks_near = len(kv_weights) // 2
    kv_near, kv_far = take(kv_weights, blocks_near)
    scale = lax.rsqrt(jnp.concatenate(squares) / depth + 1e-05)[:, None]

    kv = project(panel, kv_near, by_block([kv_far]), 0, 1, 1.0, scale, cosine, sine)
    scale = after(scale, kv)
    q_far = [gather_near(after(x, *kv_weights)) for x in got_x[1 : 1 + early]]
    q_near = gather_near(after(wq, *kv_weights))
    queries = project(
        panel, q_near, by_block(q_far[:early]), 0, first_heads, factor, scale, cosine, sine
    )
    beside = [exchange(kv), queries, chunks[-1], *gather_near(kv)]
    if x_sent is not None:
        beside.append(x_sent)
    kv_other, queries, last_chunk, *beside = lax.optimization_barrier(tuple(beside))
    kv_pieces, arrived = take(beside, blocks_near)
    kv_pieces = [*kv_pieces, *gather_near(kv_other)]
    late_far = [gather_near(piece) for piece in (*got_x[1 + early :], *arrived)]
    last_other = exchange(last_chunk)
    split = cols - rest // 2 if rest >= 2 * HD else cols

    def o_rows(first, last):
        return wo.reshape(-1, cols, wo.shape[1])[:, first:last].reshape(-1, wo.shape[1])

    o_most = lax.all_gather(after(o_rows(0, split), kv_other), "row")
    o_last = [o_rows(split, cols)] if split < cols else []
    heads = attend(r, [queries], kv_pieces)

    ring = Ring(heads, 1)
    panels = [put(blank((n_col, tok, wide)), ring.found), blank((n_col, tok, rest))]
    found, (last_other, *panels) = ring.hop([last_other, *panels])
    panels[0] = put(panels[0], found)
    late_far = by_block([*late_far, gather_near(last_other)])
    queries = project(
        panel, q_near, late_far, wide, late_heads, factor, scale, cosine, sine
    )
    found, (queries, panels[0]) = ring.hop([queries, panels[0]])
    panels[0] = put(panels[0], found)
    heads = attend(r, [queries], kv_pieces)
    found, (heads, panels[0]) = ring.hop([heads, panels[0]])
    panels[0] = put(panels[0], found)
    second = Ring(heads, 1)
    panels[1] = put(panels[1], second.found)
    for i in range(hops):
        found, (panels[0],) = ring.hop([panels[0]])
        panels[0] = put(panels[0], found)
        beside = [panels[1]]
        if i == hops - 3:
            beside += o_last
        if i == hops - 2:
            beside += [exchange(w) for w in o_last]
        if i == hops - 1:
            for w in o_last:
                beside += [*gather_near(w), *gather_near(o_other)]
            beside.append(finish(r, panels[0], 0, o_most, per, 0, [], jnp.float32))
        found, (panels[1], *beside) = second.hop(beside)
        panels[1] = put(panels[1], found)
        if i == hops - 3:
            o_last = beside
        if i == hops - 2 and o_last:
            (o_other,) = beside
    *pieces, total = beside

    return finish(r, panels[1], split - wide, o_most, per, wide, pieces, jnp.bfloat16, total)


def solution(mesh):
    in_specs = (
        P("row", "col"),
        P(),
        P("row", "col"),
        P("row", "col"),
        P("row", "col"),
        P("row", "col"),
    )
    out_specs = P("row", "col")
    return jax.shard_map(
        per_device, mesh=mesh, in_specs=in_specs, out_specs=out_specs, check_vma=False
    )
```

```python
import functools
import math

import jax
import jax.numpy as jnp
from jax import lax
from jax.experimental import pallas as pl
from jax.experimental.pallas import tpu as pltpu
from jax.sharding import PartitionSpec as P

HD = 128
MIB = 1 << 20
SHORT = pl.CostEstimate(flops=1, bytes_accessed=1, transcendentals=0)


def after(array, *earlier):
    if not earlier:
        return array
    return lax.optimization_barrier((array, *earlier))[0]


def swap(array, axis, mask):
    return lax.ppermute(array, axis, [(i, i ^ mask) for i in range(lax.axis_size(axis))])


def row_bits():
    return [1 << b for b in reversed(range((lax.axis_size("row")).bit_length() - 1))]


def exchange(array, *earlier):
    return swap(after(array, *earlier), "row", row_bits()[0])


def gather_near(array, *earlier):
    pieces = {0: after(array, *earlier)}
    for bit in row_bits()[1:]:
        pieces.update({j ^ bit: swap(p, "row", bit) for j, p in pieces.items()})
    return [pieces[j] for j in range(len(pieces))]


def order_pair(mine, other, col_index, bit, axis_dim):
    upper = col_index // 2**bit % 2 == 1
    lower_part = jnp.where(upper, other, mine)
    upper_part = jnp.where(upper, mine, other)
    return jnp.concatenate([lower_part, upper_part], axis=axis_dim)


def ring_order(n):
    return list(range(0, n, 2)) + list(range(1, n, 2))[::-1]


def ring_source(c, hops, n):
    at = jnp.where(c % 2 == 0, c // 2, n - 1 - c // 2)
    at = (at - hops) % n
    return jnp.where(at < n // 2, 2 * at, 2 * (n - 1 - at) + 1)


def take(refs, *counts):
    out, at = [], 0
    for n in counts:
        out.append(refs[at : at + n])
        at += n
    return *out, refs[at:]


class Ring:
    def __init__(self, block, pieces):
        n = lax.axis_size("col")
        order = ring_order(n)
        self.n, self.hops = n, 0
        self.up = [(order[i], order[(i + 1) % n]) for i in range(n)]
        self.down = [(b, a) for a, b in self.up]
        self.rows = block.shape[0]
        self.found = [(lax.axis_index("col"), 0, block)]
        self.height = self.rows // pieces
        parts = [block[i * self.height : (i + 1) * self.height] for i in range(pieces)]
        self.last = [(p, p) for p in parts]

    def hop(self, beside=()):
        if self.hops == self.n // 2:
            return [], list(beside)
        c, half = self.found[0][0], self.rows // 2
        self.hops += 1
        found = []
        for i, (below, above) in enumerate(self.last):
            top = i * self.height
            firsts = [top, top]
            sends = [(below, self.up), (above, self.down)]
            if self.hops == self.n // 2:
                if len(self.last) == 1:
                    sends = [(below[:half], self.up), (above[half:], self.down)]
                    firsts = [0, half]
                else:
                    sends = [sends[0], None] if top < half else [None, sends[1]]
            got = [None if s is None else lax.ppermute(s[0], "col", s[1]) for s in sends]
            more = list(beside) if i == len(self.last) - 1 else []
            here = [g for g in got if g is not None]
            here, more = take(lax.optimization_barrier((*here, *more)), len(here))
            here = list(here)
            got = [None if g is None else here.pop(0) for g in got]
            self.last[i] = tuple(got)
            for way, piece in enumerate(got):
                if piece is not None:
                    hops = self.hops if way == 0 else -self.hops
                    found.append((ring_source(c, hops, self.n), firsts[way], piece))
        self.found += found
        return found, list(more)


def blank(shape):
    return pl.pallas_call(
        lambda o_ref: None,
        out_specs=pl.BlockSpec(memory_space=pl.ANY),
        out_shape=jax.ShapeDtypeStruct(shape, jnp.bfloat16),
    )()


def multiply(steps, a_buf, w_bufs, accs, a_sem, w_sem):
    for i, (left, rights) in enumerate(steps):
        pltpu.make_async_copy(left, a_buf.at[i], a_sem.at[i]).start()
        for g, chunks in enumerate(rights):
            at = 0
            for chunk in chunks:
                wide = chunk.shape[1]
                into = w_bufs[g].at[i, :, pl.ds(at, wide)]
                pltpu.make_async_copy(chunk, into, w_sem.at[g, i]).start()
                at += wide

    def body(i, carry):
        pltpu.make_async_copy(a_buf.at[i], a_buf.at[i], a_sem.at[i]).wait()
        for g, acc in enumerate(accs):
            pltpu.make_async_copy(w_bufs[g].at[i], w_bufs[g].at[i], w_sem.at[g, i]).wait()
            acc[...] += jnp.dot(a_buf[i], w_bufs[g][i], preferred_element_type=jnp.float32)
        return carry

    lax.fori_loop(0, len(steps), body, 0)


def project_kernel(near, far, chunks, first, heads, factor, panel_ref, *refs):
    near_refs, far_refs, (scale_ref, cos_ref, sin_ref), rest = take(refs, near, far * chunks, 3)
    o_ref, a_buf, w_buf, acc, a_sem, w_sem = rest
    slots, _, depth = panel_ref.shape
    per = slots // (near + far)
    cols = acc.shape[1]
    steps = []
    for k in range(slots):
        p, rows = k // per, pl.ds(k % per * depth, depth)
        if p < near:
            right = [near_refs[p].at[rows, pl.ds(first, cols)]]
        else:
            at = (p - near) * chunks
            right = [ref.at[rows, :] for ref in far_refs[at : at + chunks]]
        steps.append((panel_ref.at[k], [right]))
    acc[...] = jnp.zeros_like(acc)
    multiply(steps, a_buf, [w_buf], [acc], a_sem, w_sem)
    scale = scale_ref[...] * factor
    for h in range(cols // HD):
        at = pl.ds(h * HD, HD)
        x = acc[:, at] * scale
        if heads < 0 or h < heads:
            x = x * cos_ref[...] + pltpu.roll(x, HD // 2, 1) * sin_ref[...]
        o_ref[:, at] = x.astype(o_ref.dtype)


def project(panel, near, far, first, heads, factor, scale, cos, sin):
    slots, tok, depth = panel.shape
    chunks = len(far[0])
    cols = sum(w.shape[1] for w in far[0])
    hbm = pl.BlockSpec(memory_space=pl.ANY)
    vmem = pl.BlockSpec(memory_space=pltpu.VMEM)
    return pl.pallas_call(
        functools.partial(project_kernel, len(near), len(far), chunks, first, heads, factor),
        in_specs=[hbm] * (1 + len(near) + len(far) * chunks) + [vmem] * 3,
        out_specs=vmem,
        out_shape=jax.ShapeDtypeStruct((tok, cols), jnp.bfloat16),
        scratch_shapes=[
            pltpu.VMEM((slots, tok, depth), jnp.bfloat16),
            pltpu.VMEM((slots, depth, cols), jnp.bfloat16),
            pltpu.VMEM((tok, cols), jnp.float32),
            pltpu.SemaphoreType.DMA((slots,)),
            pltpu.SemaphoreType.DMA((1, slots)),
        ],
        compiler_params=pltpu.CompilerParams(vmem_limit_bytes=60 * MIB),
        cost_estimate=SHORT,
    )(panel, *near, *[w for pieces in far for w in pieces], scale, cos, sin)


def attend_kernel(parts, chunks, pair, r_ref, *refs):
    chunk_refs, pieces = refs[:chunks], refs[chunks : chunks + parts]
    o_ref, q_ref, turned, top, total, acc = refs[chunks + parts :]
    r = r_ref[0]
    tok = q_ref.shape[0]
    step = pl.program_id(0)
    per = pl.num_programs(0) // chunks
    for i in range(chunks):

        @pl.when(step // per == i)
        def _():
            q_ref[...] = chunk_refs[i][...]

    dims = (((1,), (1,)), ((), ()))

    @pl.when(step == 0)
    def _():
        for j in range(parts):
            turned[j] = pieces[j][:, HD:].T

    def scores(j, g):
        return lax.dot_general(
            pieces[j][:, :HD],
            q_ref[:, g * HD : (g + 1) * HD],
            dims,
            preferred_element_type=jnp.float32,
        )

    key = lax.broadcasted_iota(jnp.int32, (tok, tok), 0)
    query = lax.broadcasted_iota(jnp.int32, (tok, tok), 1)
    for g in range(pair):
        s = jnp.where(key <= query, scores(0, g), -jnp.inf)
        m = jnp.max(s, axis=0, keepdims=True)
        p = jnp.exp2(s - m)
        top[g] = m
        total[g] = jnp.sum(p, axis=0, keepdims=True)
        acc[g] = jnp.dot(turned[0], p.astype(jnp.bfloat16), preferred_element_type=jnp.float32)
    for j in range(1, parts):

        @pl.when(jnp.bitwise_xor(r, j) < r)
        def _():
            for g in range(pair):
                s = scores(j, g)
                m = jnp.maximum(top[g], jnp.max(s, axis=0, keepdims=True))
                keep = jnp.exp2(top[g] - m)
                p = jnp.exp2(s - m)
                top[g] = m
                total[g] = total[g] * keep + jnp.sum(p, axis=0, keepdims=True)
                acc[g] = acc[g] * keep + jnp.dot(
                    turned[j], p.astype(jnp.bfloat16), preferred_element_type=jnp.float32
                )

    for g in range(pair):
        o_ref[:, g * HD : (g + 1) * HD] = (acc[g] / total[g]).T.astype(o_ref.dtype)


def attend(r, queries, pieces):
    tok, cols = queries[0].shape
    chunks, parts = len(queries), len(pieces)
    pair = 2 if cols // HD % 2 == 0 else 1
    per = cols // (HD * pair)
    heads = chunks * cols // HD

    def query_spec(i):
        return pl.BlockSpec((tok, pair * HD), lambda h, r: (0, jnp.clip(h - i * per, 0, per - 1)))

    return pl.pallas_call(
        functools.partial(attend_kernel, parts, chunks, pair),
        grid_spec=pltpu.PrefetchScalarGridSpec(
            num_scalar_prefetch=1,
            grid=(chunks * per,),
            in_specs=[query_spec(i) for i in range(chunks)]
            + [pl.BlockSpec((tok, 2 * HD), lambda h, r: (0, 0)) for _ in pieces],
            out_specs=pl.BlockSpec((tok, pair * HD), lambda h, r: (0, h)),
            scratch_shapes=[
                pltpu.VMEM((tok, pair * HD), jnp.bfloat16),
                pltpu.VMEM((parts, HD, tok), jnp.bfloat16),
                pltpu.VMEM((pair, 1, tok), jnp.float32),
                pltpu.VMEM((pair, 1, tok), jnp.float32),
                pltpu.VMEM((pair, HD, tok), jnp.float32),
            ],
        ),
        out_shape=jax.ShapeDtypeStruct((tok, chunks * cols), jnp.bfloat16),
        compiler_params=pltpu.CompilerParams(
            dimension_semantics=("arbitrary",), vmem_limit_bytes=32 * MIB
        ),
        cost_estimate=SHORT,
    )(r.reshape(1), *queries, *pieces)


def finish_kernel(slots, per, count, r_ref, first_ref, second_ref, *refs):
    weights, (*old, o_ref, a_buf, w_buf, acc, a_sem, w_sem) = take(refs, count)
    steps = []
    depth = first_ref.shape[2]
    rows = depth + second_ref.shape[2]
    for k in range(*slots):
        for g, panel_ref in enumerate((first_ref, second_ref)):
            at = pl.ds(k % per * rows + g * depth, depth)
            if len(weights[0].shape) == 3:
                right = weights[0].at[jnp.bitwise_xor(r_ref[0], k // per), at, :]
            else:
                right = weights[k // per].at[at, :]
            steps.append((panel_ref.at[k], [[right]]))
    acc[...] = old[0][...] if old else jnp.zeros_like(acc)
    multiply(steps, a_buf, [w_buf], [acc], a_sem, w_sem)
    o_ref[...] = acc[...].astype(o_ref.dtype)


def finish(r, panels, slots, weights, per, dtype, total=None):
    _, tok, wide = panels[0].shape
    cols = weights[0].shape[-1]
    count = 2 * (slots[1] - slots[0])
    hbm = pl.BlockSpec(memory_space=pl.ANY)
    vmem = pl.BlockSpec(memory_space=pltpu.VMEM)
    old = [] if total is None else [total]
    return pl.pallas_call(
        functools.partial(finish_kernel, slots, per, len(weights)),
        in_specs=[pl.BlockSpec(memory_space=pltpu.SMEM)]
        + [hbm] * (2 + len(weights))
        + [vmem] * len(old),
        out_specs=vmem,
        out_shape=jax.ShapeDtypeStruct((tok, cols), dtype),
        scratch_shapes=[
            pltpu.VMEM((count, tok, wide), jnp.bfloat16),
            pltpu.VMEM((count, wide, cols), jnp.bfloat16),
            pltpu.VMEM((tok, cols), jnp.float32),
            pltpu.SemaphoreType.DMA((count,)),
            pltpu.SemaphoreType.DMA((1, count)),
        ],
        compiler_params=pltpu.CompilerParams(vmem_limit_bytes=60 * MIB),
        cost_estimate=SHORT,
    )(r.reshape(1), *panels, *weights, *old)


def per_device(hidden, norm_gain, wq, wk, wv, wo):
    tok, feat = hidden.shape
    n_row, n_col = lax.axis_size("row"), lax.axis_size("col")
    r, c = lax.axis_index("row"), lax.axis_index("col")
    depth = feat * n_col
    rows = wq.shape[0]
    cols = wq.shape[1]

    kv_cols = wk.shape[1]
    group = max(1, HD // kv_cols)
    stacked = jnp.stack((wk, wv), axis=1)
    for bit in range(group.bit_length() - 1):
        other = swap(stacked, "col", 1 << bit)
        stacked = order_pair(stacked, other, c, bit, 2)
    stacked = stacked.reshape(rows, 2 * HD)

    n_heads = cols // HD
    first_heads = n_heads // 2
    late_heads = n_heads - first_heads
    if n_heads >= 4:
        quarter = late_heads // 2
        sizes = [first_heads // 2, first_heads - first_heads // 2]
        sizes += [n for n in (quarter // 2, quarter - quarter // 2, late_heads - quarter) if n > 0]
    else:
        sizes = [first_heads, late_heads]
    early = 2 if n_heads >= 4 else 1
    wide, rest = first_heads * HD, late_heads * HD
    chunks = [
        wq[:, sum(sizes[:i]) * HD : sum(sizes[: i + 1]) * HD] for i in range(len(sizes))
    ]

    def by_block(far):
        return [list(pieces) for pieces in zip(*far)]

    half = HD // 2
    positions = r * tok + jnp.arange(tok)
    freqs = 10000.0 ** (-jnp.arange(half).astype(jnp.float32) / half)
    angles = positions.astype(jnp.float32)[:, None] * freqs[None, :]
    cosine, sine = jnp.cos(angles), jnp.sin(angles)
    cosine = jnp.concatenate([cosine, cosine], axis=1)
    sine = jnp.concatenate([-sine, sine], axis=1)
    factor = HD ** (-0.5) * math.log2(math.e)

    per = rows // feat

    def put(panel, found):
        for source, first, piece in found:
            slot = (source // per ^ r) * per + source % per
            panel = lax.dynamic_update_slice(panel, piece[None], (slot, first, 0))
        return panel

    def put_hidden(panel, squares, found):
        for source, first, piece in found:
            wider = piece.astype(jnp.float32)
            sums = jnp.sum(wider * wider, axis=1)
            for h in range(2):
                if first <= h * tok // 2 < first + piece.shape[0]:
                    at = h * tok // 2 - first
                    squares[h] += sums[at : at + tok // 2]
            gain = lax.dynamic_slice(norm_gain, (source * feat,), (feat,))
            panel = put(panel, [(source, first, (wider * gain).astype(jnp.bfloat16))])
        return panel, squares

    ring = Ring(hidden, 1)
    hops = n_col // 2
    x_sent = exchange(stacked)
    got_x = []
    zeros = [jnp.zeros((tok // 2,), jnp.float32)] * 2
    panel, squares = put_hidden(blank((n_col, tok, feat)), zeros, ring.found)
    for i in range(hops):
        last_hop = i == hops - 1
        tie = ring.last[0][1]
        sent = [] if x_sent is None else [x_sent]
        ahead = chunks[i : i + 1] if i < len(sizes) - 1 else []
        beside = [panel, *squares, cosine, sine, *sent, *ahead]
        if last_hop:
            near = gather_near(after(stacked, tie))
            kv_weights = [*near, *gather_near(after(got_x[0], tie))]
            beside += kv_weights
        found, beside = ring.hop(beside)
        (panel, *squares, cosine, sine), beside = take(beside, 5)
        panel, squares = put_hidden(panel, squares, found)
        sent, ahead, kv_weights = take(beside, len(sent), len(ahead))
        got_x += sent
        x_sent = exchange(ahead[0]) if ahead else None
    blocks_near = len(kv_weights) // 2
    kv_near, kv_far = take(kv_weights, blocks_near)
    scale = lax.rsqrt(jnp.concatenate(squares) / depth + 1e-05)[:, None]

    kv = project(panel, kv_near, by_block([kv_far]), 0, 1, 1.0, scale, cosine, sine)
    scale = after(scale, kv)
    q_far = [gather_near(after(x, *kv_weights)) for x in got_x[1 : 1 + early]]
    q_near = gather_near(after(wq, *kv_weights))
    queries = project(
        panel, q_near, by_block(q_far[:early]), 0, first_heads, factor, scale, cosine, sine
    )
    beside = [exchange(kv), queries, chunks[-1], *gather_near(kv)]
    if x_sent is not None:
        beside.append(x_sent)
    kv_other, queries, last_chunk, *beside = lax.optimization_barrier(tuple(beside))
    kv_pieces, arrived = take(beside, blocks_near)
    kv_pieces = [*kv_pieces, *gather_near(kv_other)]
    late_far = [gather_near(piece) for piece in (*got_x[1 + early :], *arrived)]
    late_far = [list(far) for far in late_far]
    last_other = exchange(last_chunk)
    o_weights = lax.all_gather(after(wo, kv_other), "row")
    heads = attend(r, [queries], kv_pieces)

    ring = Ring(heads, 1)
    panels = [put(blank((n_col, tok, wide)), ring.found), blank((n_col, tok, rest))]
    tables = scale, cosine, sine
    late, first = [], wide
    if late_far:
        late_far = by_block(late_far)
        late.append(project(panel, q_near, late_far, first, -1, factor, *tables))
        first += late[0].shape[1]
    found, (last_other, *rest_of) = ring.hop([last_other, *panels, *late])
    panels, late = take(rest_of, 2)
    panels[0] = put(panels[0], found)
    last_far = by_block([gather_near(last_other)])
    late = [*late, project(panel, q_near, last_far, first, -1, factor, *tables)]
    found, (panels[0], *late) = ring.hop([panels[0], *late])
    panels[0] = put(panels[0], found)
    heads = attend(r, late, kv_pieces)
    o_near = gather_near(after(wo, late[-1]))
    found, (heads, panels[0], *o_near) = ring.hop([heads, panels[0], *o_near])
    panels[0] = put(panels[0], found)
    second = Ring(heads, 1)
    panels[1] = put(panels[1], second.found)
    for i in range(hops):
        found, (panels[0],) = ring.hop([panels[0]])
        panels[0] = put(panels[0], found)
        found, (panels[1],) = second.hop([panels[1]])
        panels[1] = put(panels[1], found)

    half = n_col // 2
    total = finish(r, panels, (0, half), o_near, per, jnp.float32)
    return finish(r, panels, (half, n_col), [after(o_weights, total)], per, jnp.bfloat16, total)


def solution(mesh):
    in_specs = (
        P("row", "col"),
        P(),
        P("row", "col"),
        P("row", "col"),
        P("row", "col"),
        P("row", "col"),
    )
    out_specs = P("row", "col")
    return jax.shard_map(
        per_device, mesh=mesh, in_specs=in_specs, out_specs=out_specs, check_vma=False
    )
```

```python
import functools
import math

import jax
import jax.numpy as jnp
from jax import lax
from jax.experimental import pallas as pl
from jax.experimental.pallas import tpu as pltpu
from jax.sharding import PartitionSpec as P

HD = 128
MIB = 1 << 20
SHORT = pl.CostEstimate(flops=1, bytes_accessed=1, transcendentals=0)


def after(array, *earlier):
    if not earlier:
        return array
    return lax.optimization_barrier((array, *earlier))[0]


def swap(array, axis, mask):
    return lax.ppermute(array, axis, [(i, i ^ mask) for i in range(lax.axis_size(axis))])


def row_bits():
    return [1 << b for b in reversed(range((lax.axis_size("row")).bit_length() - 1))]


def exchange(array, *earlier):
    return swap(after(array, *earlier), "row", row_bits()[0])


def gather_near(array, *earlier):
    pieces = {0: after(array, *earlier)}
    for bit in row_bits()[1:]:
        pieces.update({j ^ bit: swap(p, "row", bit) for j, p in pieces.items()})
    return [pieces[j] for j in range(len(pieces))]


def order_pair(mine, other, col_index, bit, axis_dim):
    upper = col_index // 2**bit % 2 == 1
    lower_part = jnp.where(upper, other, mine)
    upper_part = jnp.where(upper, mine, other)
    return jnp.concatenate([lower_part, upper_part], axis=axis_dim)


def ring_order(n):
    return list(range(0, n, 2)) + list(range(1, n, 2))[::-1]


def ring_source(c, hops, n):
    at = jnp.where(c % 2 == 0, c // 2, n - 1 - c // 2)
    at = (at - hops) % n
    return jnp.where(at < n // 2, 2 * at, 2 * (n - 1 - at) + 1)


def take(refs, *counts):
    out, at = [], 0
    for n in counts:
        out.append(refs[at : at + n])
        at += n
    return *out, refs[at:]


class Ring:
    def __init__(self, block, pieces):
        n = lax.axis_size("col")
        order = ring_order(n)
        self.n, self.hops = n, 0
        self.up = [(order[i], order[(i + 1) % n]) for i in range(n)]
        self.down = [(b, a) for a, b in self.up]
        self.rows = block.shape[0]
        self.found = [(lax.axis_index("col"), 0, block)]
        self.height = self.rows // pieces
        parts = [block[i * self.height : (i + 1) * self.height] for i in range(pieces)]
        self.last = [(p, p) for p in parts]

    def hop(self, beside=()):
        if self.hops == self.n // 2:
            return [], list(beside)
        c, half = self.found[0][0], self.rows // 2
        self.hops += 1
        found = []
        for i, (below, above) in enumerate(self.last):
            top = i * self.height
            firsts = [top, top]
            sends = [(below, self.up), (above, self.down)]
            if self.hops == self.n // 2:
                if len(self.last) == 1:
                    sends = [(below[:half], self.up), (above[half:], self.down)]
                    firsts = [0, half]
                else:
                    sends = [sends[0], None] if top < half else [None, sends[1]]
            got = [None if s is None else lax.ppermute(s[0], "col", s[1]) for s in sends]
            more = list(beside) if i == len(self.last) - 1 else []
            here = [g for g in got if g is not None]
            here, more = take(lax.optimization_barrier((*here, *more)), len(here))
            here = list(here)
            got = [None if g is None else here.pop(0) for g in got]
            self.last[i] = tuple(got)
            for way, piece in enumerate(got):
                if piece is not None:
                    hops = self.hops if way == 0 else -self.hops
                    found.append((ring_source(c, hops, self.n), firsts[way], piece))
        self.found += found
        return found, list(more)


def blank(shape):
    return pl.pallas_call(
        lambda o_ref: None,
        out_specs=pl.BlockSpec(memory_space=pl.ANY),
        out_shape=jax.ShapeDtypeStruct(shape, jnp.bfloat16),
    )()


def multiply(steps, w_buf, acc, sems):
    for i, (_, chunks) in enumerate(steps):
        at = 0
        for chunk in chunks:
            wide = chunk.shape[1]
            into = w_buf.at[i, :, pl.ds(at, wide)]
            pltpu.make_async_copy(chunk, into, sems.at[i]).start()
            at += wide
    for i, (left, _) in enumerate(steps):
        pltpu.make_async_copy(w_buf.at[i], w_buf.at[i], sems.at[i]).wait()
        acc[...] += jnp.dot(left(), w_buf[i], preferred_element_type=jnp.float32)


def project_kernel(near, far, chunks, first, heads, factor, panel_ref, *refs):
    near_refs, far_refs, (scale_ref, cos_ref, sin_ref), rest = take(refs, near, far * chunks, 3)
    o_ref, w_buf, acc, sems = rest
    slots, _, depth = panel_ref.shape
    per = slots // (near + far)
    cols = acc.shape[1]
    steps = []
    for k in range(slots):
        p, rows = k // per, pl.ds(k % per * depth, depth)
        if p < near:
            right = [near_refs[p].at[rows, pl.ds(first, cols)]]
        else:
            at = (p - near) * chunks
            right = [ref.at[rows, :] for ref in far_refs[at : at + chunks]]
        steps.append((functools.partial(panel_ref.__getitem__, k), right))
    acc[...] = jnp.zeros_like(acc)
    multiply(steps, w_buf, acc, sems)
    scale = scale_ref[...] * factor
    for h in range(cols // HD):
        at = pl.ds(h * HD, HD)
        x = acc[:, at] * scale
        if heads < 0 or h < heads:
            x = x * cos_ref[...] + pltpu.roll(x, HD // 2, 1) * sin_ref[...]
        o_ref[:, at] = x.astype(o_ref.dtype)


def project(panel, near, far, first, heads, factor, scale, cos, sin):
    slots, tok, depth = panel.shape
    chunks = len(far[0])
    cols = sum(w.shape[1] for w in far[0])
    hbm = pl.BlockSpec(memory_space=pl.ANY)
    vmem = pl.BlockSpec(memory_space=pltpu.VMEM)
    return pl.pallas_call(
        functools.partial(project_kernel, len(near), len(far), chunks, first, heads, factor),
        in_specs=[vmem] + [hbm] * (len(near) + len(far) * chunks) + [vmem] * 3,
        out_specs=vmem,
        out_shape=jax.ShapeDtypeStruct((tok, cols), jnp.bfloat16),
        scratch_shapes=[
            pltpu.VMEM((slots, depth, cols), jnp.bfloat16),
            pltpu.VMEM((tok, cols), jnp.float32),
            pltpu.SemaphoreType.DMA((slots,)),
        ],
        compiler_params=pltpu.CompilerParams(vmem_limit_bytes=18 * MIB),
        cost_estimate=SHORT,
    )(panel, *near, *[w for pieces in far for w in pieces], scale, cos, sin)


def attend_kernel(parts, chunks, pair, r_ref, *refs):
    chunk_refs, pieces = refs[:chunks], refs[chunks : chunks + parts]
    o_ref, q_ref, turned, top, total, acc = refs[chunks + parts :]
    r = r_ref[0]
    tok = q_ref.shape[0]
    step = pl.program_id(0)
    per = pl.num_programs(0) // chunks
    for i in range(chunks):

        @pl.when(step // per == i)
        def _():
            q_ref[...] = chunk_refs[i][...]

    dims = (((1,), (1,)), ((), ()))

    @pl.when(step == 0)
    def _():
        for j in range(parts):
            turned[j] = pieces[j][:, HD:].T

    def scores(j, g):
        return lax.dot_general(
            pieces[j][:, :HD],
            q_ref[:, g * HD : (g + 1) * HD],
            dims,
            preferred_element_type=jnp.float32,
        )

    key = lax.broadcasted_iota(jnp.int32, (tok, tok), 0)
    query = lax.broadcasted_iota(jnp.int32, (tok, tok), 1)
    for g in range(pair):
        s = jnp.where(key <= query, scores(0, g), -jnp.inf)
        m = jnp.max(s, axis=0, keepdims=True)
        p = jnp.exp2(s - m)
        top[g] = m
        total[g] = jnp.sum(p, axis=0, keepdims=True)
        acc[g] = jnp.dot(turned[0], p.astype(jnp.bfloat16), preferred_element_type=jnp.float32)
    for j in range(1, parts):

        @pl.when(jnp.bitwise_xor(r, j) < r)
        def _():
            for g in range(pair):
                s = scores(j, g)
                m = jnp.maximum(top[g], jnp.max(s, axis=0, keepdims=True))
                keep = jnp.exp2(top[g] - m)
                p = jnp.exp2(s - m)
                top[g] = m
                total[g] = total[g] * keep + jnp.sum(p, axis=0, keepdims=True)
                acc[g] = acc[g] * keep + jnp.dot(
                    turned[j], p.astype(jnp.bfloat16), preferred_element_type=jnp.float32
                )

    for g in range(pair):
        o_ref[:, g * HD : (g + 1) * HD] = (acc[g] / total[g]).T.astype(o_ref.dtype)


def attend(r, queries, pieces):
    tok, cols = queries[0].shape
    chunks, parts = len(queries), len(pieces)
    pair = 2 if cols // HD % 2 == 0 else 1
    per = cols // (HD * pair)
    heads = chunks * cols // HD

    def query_spec(i):
        return pl.BlockSpec((tok, pair * HD), lambda h, r: (0, jnp.clip(h - i * per, 0, per - 1)))

    return pl.pallas_call(
        functools.partial(attend_kernel, parts, chunks, pair),
        grid_spec=pltpu.PrefetchScalarGridSpec(
            num_scalar_prefetch=1,
            grid=(chunks * per,),
            in_specs=[query_spec(i) for i in range(chunks)]
            + [pl.BlockSpec((tok, 2 * HD), lambda h, r: (0, 0)) for _ in pieces],
            out_specs=pl.BlockSpec((tok, pair * HD), lambda h, r: (0, h)),
            scratch_shapes=[
                pltpu.VMEM((tok, pair * HD), jnp.bfloat16),
                pltpu.VMEM((parts, HD, tok), jnp.bfloat16),
                pltpu.VMEM((pair, 1, tok), jnp.float32),
                pltpu.VMEM((pair, 1, tok), jnp.float32),
                pltpu.VMEM((pair, HD, tok), jnp.float32),
            ],
        ),
        out_shape=jax.ShapeDtypeStruct((tok, chunks * cols), jnp.bfloat16),
        compiler_params=pltpu.CompilerParams(
            dimension_semantics=("arbitrary",), vmem_limit_bytes=18 * MIB
        ),
        cost_estimate=SHORT,
    )(r.reshape(1), *queries, *pieces)


def finish_kernel(slots, per, count, r_ref, first_ref, second_ref, *refs):
    weights, (*old, o_ref, w_buf, acc, sems) = take(refs, count)
    steps = []
    depth = first_ref.shape[2]
    rows = depth + second_ref.shape[2]
    for k in range(*slots):
        for g, panel_ref in enumerate((first_ref, second_ref)):
            at = pl.ds(k % per * rows + g * depth, depth)
            if len(weights[0].shape) == 3:
                right = weights[0].at[jnp.bitwise_xor(r_ref[0], k // per), at, :]
            else:
                right = weights[k // per].at[at, :]
            steps.append((functools.partial(panel_ref.__getitem__, k), [right]))
    acc[...] = old[0][...] if old else jnp.zeros_like(acc)
    multiply(steps, w_buf, acc, sems)
    o_ref[...] = acc[...].astype(o_ref.dtype)


def finish(r, panels, slots, weights, per, dtype, limit, total=None):
    _, tok, wide = panels[0].shape
    cols = weights[0].shape[-1]
    count = 2 * (slots[1] - slots[0])
    hbm = pl.BlockSpec(memory_space=pl.ANY)
    vmem = pl.BlockSpec(memory_space=pltpu.VMEM)
    old = [] if total is None else [total]
    return pl.pallas_call(
        functools.partial(finish_kernel, slots, per, len(weights)),
        in_specs=[pl.BlockSpec(memory_space=pltpu.SMEM)]
        + [vmem] * 2
        + [hbm] * len(weights)
        + [vmem] * len(old),
        out_specs=vmem,
        out_shape=jax.ShapeDtypeStruct((tok, cols), dtype),
        scratch_shapes=[
            pltpu.VMEM((count, wide, cols), jnp.bfloat16),
            pltpu.VMEM((tok, cols), jnp.float32),
            pltpu.SemaphoreType.DMA((count,)),
        ],
        compiler_params=pltpu.CompilerParams(vmem_limit_bytes=limit * MIB),
        cost_estimate=SHORT,
    )(r.reshape(1), *panels, *weights, *old)


def per_device(hidden, norm_gain, wq, wk, wv, wo):
    tok, feat = hidden.shape
    n_row, n_col = lax.axis_size("row"), lax.axis_size("col")
    r, c = lax.axis_index("row"), lax.axis_index("col")
    depth = feat * n_col
    rows = wq.shape[0]
    cols = wq.shape[1]

    kv_cols = wk.shape[1]
    group = max(1, HD // kv_cols)
    stacked = jnp.stack((wk, wv), axis=1)
    for bit in range(group.bit_length() - 1):
        other = swap(stacked, "col", 1 << bit)
        stacked = order_pair(stacked, other, c, bit, 2)
    stacked = stacked.reshape(rows, 2 * HD)

    n_heads = cols // HD
    first_heads = n_heads // 2
    late_heads = n_heads - first_heads
    if n_heads >= 4:
        quarter = late_heads // 2
        sizes = [first_heads // 2, first_heads - first_heads // 2]
        sizes += [n for n in (quarter // 2, quarter - quarter // 2, late_heads - quarter) if n > 0]
    else:
        sizes = [first_heads, late_heads]
    early = 2 if n_heads >= 4 else 1
    wide, rest = first_heads * HD, late_heads * HD
    chunks = [
        wq[:, sum(sizes[:i]) * HD : sum(sizes[: i + 1]) * HD] for i in range(len(sizes))
    ]

    def by_block(far):
        return [list(pieces) for pieces in zip(*far)]

    half = HD // 2
    positions = r * tok + jnp.arange(tok)
    freqs = 10000.0 ** (-jnp.arange(half).astype(jnp.float32) / half)
    angles = positions.astype(jnp.float32)[:, None] * freqs[None, :]
    cosine, sine = jnp.cos(angles), jnp.sin(angles)
    cosine = jnp.concatenate([cosine, cosine], axis=1)
    sine = jnp.concatenate([-sine, sine], axis=1)
    factor = HD ** (-0.5) * math.log2(math.e)

    per = rows // feat

    def put(panel, found):
        for source, first, piece in found:
            slot = (source // per ^ r) * per + source % per
            panel = lax.dynamic_update_slice(panel, piece[None], (slot, first, 0))
        return panel

    def put_hidden(panel, squares, found):
        for source, first, piece in found:
            wider = piece.astype(jnp.float32)
            sums = jnp.sum(wider * wider, axis=1)
            for h in range(2):
                if first <= h * tok // 2 < first + piece.shape[0]:
                    at = h * tok // 2 - first
                    squares[h] += sums[at : at + tok // 2]
            gain = lax.dynamic_slice(norm_gain, (source * feat,), (feat,))
            panel = put(panel, [(source, first, (wider * gain).astype(jnp.bfloat16))])
        return panel, squares

    ring = Ring(hidden, 1)
    hops = n_col // 2
    x_sent = exchange(stacked)
    got_x = []
    zeros = [jnp.zeros((tok // 2,), jnp.float32)] * 2
    panel, squares = put_hidden(blank((n_col, tok, feat)), zeros, ring.found)
    for i in range(hops):
        last_hop = i == hops - 1
        tie = ring.last[0][1]
        sent = [] if x_sent is None else [x_sent]
        ahead = chunks[i : i + 1] if i < len(sizes) - 1 else []
        beside = [panel, *squares, cosine, sine, *sent, *ahead]
        if last_hop:
            near = gather_near(after(stacked, tie))
            kv_weights = [*near, *gather_near(after(got_x[0], tie))]
            beside += kv_weights
        found, beside = ring.hop(beside)
        (panel, *squares, cosine, sine), beside = take(beside, 5)
        panel, squares = put_hidden(panel, squares, found)
        sent, ahead, kv_weights = take(beside, len(sent), len(ahead))
        got_x += sent
        x_sent = exchange(ahead[0]) if ahead else None
    blocks_near = len(kv_weights) // 2
    kv_near, kv_far = take(kv_weights, blocks_near)
    scale = lax.rsqrt(jnp.concatenate(squares) / depth + 1e-05)[:, None]

    kv = project(panel, kv_near, by_block([kv_far]), 0, 1, 1.0, scale, cosine, sine)
    scale = after(scale, kv)
    q_far = [gather_near(after(x, *kv_weights)) for x in got_x[1 : 1 + early]]
    q_near = gather_near(after(wq, *kv_weights))
    queries = project(
        panel, q_near, by_block(q_far[:early]), 0, first_heads, factor, scale, cosine, sine
    )
    beside = [exchange(kv), queries, chunks[-1], *gather_near(kv)]
    if x_sent is not None:
        beside.append(x_sent)
    kv_other, queries, last_chunk, *beside = lax.optimization_barrier(tuple(beside))
    kv_pieces, arrived = take(beside, blocks_near)
    kv_pieces = [*kv_pieces, *gather_near(kv_other)]
    late_far = [gather_near(piece) for piece in (*got_x[1 + early :], *arrived)]
    late_far = [list(far) for far in late_far]
    last_other = exchange(last_chunk)
    o_weights = lax.all_gather(after(wo, kv_other), "row")
    heads = attend(r, [queries], kv_pieces)

    ring = Ring(heads, 1)
    panels = [put(blank((n_col, tok, wide)), ring.found), blank((n_col, tok, rest))]
    tables = scale, cosine, sine
    late, first = [], wide
    if late_far:
        late_far = by_block(late_far)
        late.append(project(panel, q_near, late_far, first, -1, factor, *tables))
        first += late[0].shape[1]
    found, (last_other, *rest_of) = ring.hop([last_other, *panels, *late])
    panels, late = take(rest_of, 2)
    panels[0] = put(panels[0], found)
    last_far = by_block([gather_near(last_other)])
    late = [*late, project(panel, q_near, last_far, first, -1, factor, *tables)]
    found, (panels[0], *late) = ring.hop([panels[0], *late])
    panels[0] = put(panels[0], found)
    heads = attend(r, late, kv_pieces)
    o_near = gather_near(after(wo, late[-1]))
    found, (heads, panels[0], *o_near) = ring.hop([heads, panels[0], *o_near])
    panels[0] = put(panels[0], found)
    second = Ring(heads, 1)
    panels[1] = put(panels[1], second.found)
    for i in range(hops):
        found, (panels[0],) = ring.hop([panels[0]])
        panels[0] = put(panels[0], found)
        found, (panels[1],) = second.hop([panels[1]])
        panels[1] = put(panels[1], found)

    half = n_col // 2
    total = finish(r, panels, (0, half), o_near, per, jnp.float32, 18)
    return finish(r, panels, (half, n_col), [o_weights], per, jnp.bfloat16, 44, total)


def solution(mesh):
    in_specs = (
        P("row", "col"),
        P(),
        P("row", "col"),
        P("row", "col"),
        P("row", "col"),
        P("row", "col"),
    )
    out_specs = P("row", "col")
    return jax.shard_map(
        per_device, mesh=mesh, in_specs=in_specs, out_specs=out_specs, check_vma=False
    )
```

```python
import functools
import math

import jax
import jax.numpy as jnp
from jax import lax
from jax.experimental import pallas as pl
from jax.experimental.pallas import tpu as pltpu
from jax.sharding import PartitionSpec as P

HD = 128
MIB = 1 << 20
SHORT = pl.CostEstimate(flops=1, bytes_accessed=1, transcendentals=0)


def after(array, *earlier):
    if not earlier:
        return array
    return lax.optimization_barrier((array, *earlier))[0]


def swap(array, axis, mask):
    return lax.ppermute(array, axis, [(i, i ^ mask) for i in range(lax.axis_size(axis))])


def row_bits():
    return [1 << b for b in reversed(range((lax.axis_size("row")).bit_length() - 1))]


def exchange(array, *earlier):
    return swap(after(array, *earlier), "row", row_bits()[0])


def gather_near(array, *earlier):
    pieces = {0: after(array, *earlier)}
    for bit in row_bits()[1:]:
        pieces.update({j ^ bit: swap(p, "row", bit) for j, p in pieces.items()})
    return [pieces[j] for j in range(len(pieces))]


def order_pair(mine, other, col_index, bit, axis_dim):
    upper = col_index // 2**bit % 2 == 1
    lower_part = jnp.where(upper, other, mine)
    upper_part = jnp.where(upper, mine, other)
    return jnp.concatenate([lower_part, upper_part], axis=axis_dim)


def ring_order(n):
    return list(range(0, n, 2)) + list(range(1, n, 2))[::-1]


def ring_source(c, hops, n):
    at = jnp.where(c % 2 == 0, c // 2, n - 1 - c // 2)
    at = (at - hops) % n
    return jnp.where(at < n // 2, 2 * at, 2 * (n - 1 - at) + 1)


def take(refs, *counts):
    out, at = [], 0
    for n in counts:
        out.append(refs[at : at + n])
        at += n
    return *out, refs[at:]


class Ring:
    def __init__(self, block, pieces):
        n = lax.axis_size("col")
        order = ring_order(n)
        self.n, self.hops = n, 0
        self.up = [(order[i], order[(i + 1) % n]) for i in range(n)]
        self.down = [(b, a) for a, b in self.up]
        self.rows = block.shape[0]
        self.found = [(lax.axis_index("col"), 0, block)]
        self.height = self.rows // pieces
        parts = [block[i * self.height : (i + 1) * self.height] for i in range(pieces)]
        self.last = [(p, p) for p in parts]

    def hop(self, beside=()):
        if self.hops == self.n // 2:
            return [], list(beside)
        c, half = self.found[0][0], self.rows // 2
        self.hops += 1
        found = []
        for i, (below, above) in enumerate(self.last):
            top = i * self.height
            firsts = [top, top]
            sends = [(below, self.up), (above, self.down)]
            if self.hops == self.n // 2:
                if len(self.last) == 1:
                    sends = [(below[:half], self.up), (above[half:], self.down)]
                    firsts = [0, half]
                else:
                    sends = [sends[0], None] if top < half else [None, sends[1]]
            got = [None if s is None else lax.ppermute(s[0], "col", s[1]) for s in sends]
            more = list(beside) if i == len(self.last) - 1 else []
            here = [g for g in got if g is not None]
            here, more = take(lax.optimization_barrier((*here, *more)), len(here))
            here = list(here)
            got = [None if g is None else here.pop(0) for g in got]
            self.last[i] = tuple(got)
            for way, piece in enumerate(got):
                if piece is not None:
                    hops = self.hops if way == 0 else -self.hops
                    found.append((ring_source(c, hops, self.n), firsts[way], piece))
        self.found += found
        return found, list(more)


def blank(shape):
    return pl.pallas_call(
        lambda o_ref: None,
        out_specs=pl.BlockSpec(memory_space=pl.ANY),
        out_shape=jax.ShapeDtypeStruct(shape, jnp.bfloat16),
    )()


def multiply(lefts, rights, w_buf, acc, sems):
    for i, chunks in enumerate(rights):
        at = 0
        for chunk in chunks:
            wide = chunk.shape[1]
            into = w_buf.at[i, :, pl.ds(at, wide)]
            pltpu.make_async_copy(chunk, into, sems.at[i]).start()
            at += wide

    def body(k, carry):
        for g, left in enumerate(lefts):
            i = k * len(lefts) + g
            pltpu.make_async_copy(w_buf.at[i], w_buf.at[i], sems.at[i]).wait()
            acc[...] += jnp.dot(left[k], w_buf[i], preferred_element_type=jnp.float32)
        return carry

    lax.fori_loop(0, len(rights) // len(lefts), body, 0)


def project_kernel(near, far, chunks, first, heads, factor, panel_ref, *refs):
    near_refs, far_refs, (scale_ref, cos_ref, sin_ref), rest = take(refs, near, far * chunks, 3)
    o_ref, w_buf, acc, sems = rest
    slots, _, depth = panel_ref.shape
    per = slots // (near + far)
    cols = acc.shape[1]
    rights = []
    for k in range(slots):
        p, rows = k // per, pl.ds(k % per * depth, depth)
        if p < near:
            right = [near_refs[p].at[rows, pl.ds(first, cols)]]
        else:
            at = (p - near) * chunks
            right = [ref.at[rows, :] for ref in far_refs[at : at + chunks]]
        rights.append(right)
    acc[...] = jnp.zeros_like(acc)
    multiply([panel_ref], rights, w_buf, acc, sems)
    scale = scale_ref[...] * factor
    for h in range(cols // HD):
        at = pl.ds(h * HD, HD)
        x = acc[:, at] * scale
        if heads < 0 or h < heads:
            x = x * cos_ref[...] + pltpu.roll(x, HD // 2, 1) * sin_ref[...]
        o_ref[:, at] = x.astype(o_ref.dtype)


def project(panel, near, far, first, heads, factor, scale, cos, sin):
    slots, tok, depth = panel.shape
    chunks = len(far[0])
    cols = sum(w.shape[1] for w in far[0])
    hbm = pl.BlockSpec(memory_space=pl.ANY)
    vmem = pl.BlockSpec(memory_space=pltpu.VMEM)
    return pl.pallas_call(
        functools.partial(project_kernel, len(near), len(far), chunks, first, heads, factor),
        in_specs=[vmem] + [hbm] * (len(near) + len(far) * chunks) + [vmem] * 3,
        out_specs=vmem,
        out_shape=jax.ShapeDtypeStruct((tok, cols), jnp.bfloat16),
        scratch_shapes=[
            pltpu.VMEM((slots, depth, cols), jnp.bfloat16),
            pltpu.VMEM((tok, cols), jnp.float32),
            pltpu.SemaphoreType.DMA((slots,)),
        ],
        compiler_params=pltpu.CompilerParams(vmem_limit_bytes=24 * MIB),
        cost_estimate=SHORT,
    )(panel, *near, *[w for pieces in far for w in pieces], scale, cos, sin)


def attend_kernel(parts, chunks, r_ref, *refs):
    chunk_refs, pieces, (o_ref, q, keys, values, top, total, acc) = take(refs, chunks, parts)
    r = r_ref[0]
    tok = q.shape[0]
    step = pl.program_id(0)
    per = pl.num_programs(0) // chunks
    for i in range(chunks):

        @pl.when(step // per == i)
        def _():
            q[...] = chunk_refs[i][...]

    @pl.when(step == 0)
    def _():
        for j in range(parts):
            keys[j] = pieces[j][:, :HD]
            values[j] = pieces[j][:, HD:].T

    def scores(j):
        dims = (((1,), (1,)), ((), ()))
        return lax.dot_general(keys[j], q[...], dims, preferred_element_type=jnp.float32)

    def weigh(j, p):
        return jnp.dot(values[j], p.astype(jnp.bfloat16), preferred_element_type=jnp.float32)

    key = lax.broadcasted_iota(jnp.int32, (tok, tok), 0)
    query = lax.broadcasted_iota(jnp.int32, (tok, tok), 1)
    s = jnp.where(key <= query, scores(0), -jnp.inf)
    m = jnp.max(s, axis=0, keepdims=True)
    p = jnp.exp2(s - m)
    top[...] = m
    total[...] = jnp.sum(p, axis=0, keepdims=True)
    acc[...] = weigh(0, p)

    def body(t, carry):
        j = jnp.bitwise_xor(r, t)
        s = scores(j)
        m = jnp.maximum(top[...], jnp.max(s, axis=0, keepdims=True))
        keep = jnp.exp2(top[...] - m)
        p = jnp.exp2(s - m)
        top[...] = m
        total[...] = total[...] * keep + jnp.sum(p, axis=0, keepdims=True)
        acc[...] = acc[...] * keep + weigh(j, p)
        return carry

    lax.fori_loop(0, r, body, 0)
    o_ref[...] = (acc[...] / total[...]).T.astype(o_ref.dtype)


def attend(r, queries, pieces):
    tok, cols = queries[0].shape
    chunks, parts = len(queries), len(pieces)
    per = cols // HD

    def query_spec(i):
        return pl.BlockSpec((tok, HD), lambda h, r: (0, jnp.clip(h - i * per, 0, per - 1)))

    return pl.pallas_call(
        functools.partial(attend_kernel, parts, chunks),
        grid_spec=pltpu.PrefetchScalarGridSpec(
            num_scalar_prefetch=1,
            grid=(chunks * per,),
            in_specs=[query_spec(i) for i in range(chunks)]
            + [pl.BlockSpec((tok, 2 * HD), lambda h, r: (0, 0)) for _ in pieces],
            out_specs=pl.BlockSpec((tok, HD), lambda h, r: (0, h)),
            scratch_shapes=[
                pltpu.VMEM((tok, HD), jnp.bfloat16),
                pltpu.VMEM((parts, tok, HD), jnp.bfloat16),
                pltpu.VMEM((parts, HD, tok), jnp.bfloat16),
                pltpu.VMEM((1, tok), jnp.float32),
                pltpu.VMEM((1, tok), jnp.float32),
                pltpu.VMEM((HD, tok), jnp.float32),
            ],
        ),
        out_shape=jax.ShapeDtypeStruct((tok, chunks * cols), jnp.bfloat16),
        compiler_params=pltpu.CompilerParams(
            dimension_semantics=("arbitrary",), vmem_limit_bytes=24 * MIB
        ),
        cost_estimate=SHORT,
    )(r.reshape(1), *queries, *pieces)


def finish_kernel(slots, per, count, r_ref, first_ref, second_ref, *refs):
    weights, (*old, o_ref, w_buf, acc, sems) = take(refs, count)
    rights = []
    depth = first_ref.shape[2]
    rows = depth + second_ref.shape[2]
    for k in range(*slots):
        for g in range(2):
            at = pl.ds(k % per * rows + g * depth, depth)
            if len(weights[0].shape) == 3:
                right = weights[0].at[jnp.bitwise_xor(r_ref[0], k // per), at, :]
            else:
                right = weights[k // per].at[at, :]
            rights.append([right])
    acc[...] = old[0][...] if old else jnp.zeros_like(acc)
    lefts = [ref.at[pl.ds(slots[0], slots[1] - slots[0])] for ref in (first_ref, second_ref)]
    multiply(lefts, rights, w_buf, acc, sems)
    o_ref[...] = acc[...].astype(o_ref.dtype)


def finish(r, panels, slots, weights, per, dtype, limit, total=None):
    _, tok, wide = panels[0].shape
    cols = weights[0].shape[-1]
    count = 2 * (slots[1] - slots[0])
    hbm = pl.BlockSpec(memory_space=pl.ANY)
    vmem = pl.BlockSpec(memory_space=pltpu.VMEM)
    old = [] if total is None else [total]
    return pl.pallas_call(
        functools.partial(finish_kernel, slots, per, len(weights)),
        in_specs=[pl.BlockSpec(memory_space=pltpu.SMEM)]
        + [vmem] * 2
        + [hbm] * len(weights)
        + [vmem] * len(old),
        out_specs=vmem,
        out_shape=jax.ShapeDtypeStruct((tok, cols), dtype),
        scratch_shapes=[
            pltpu.VMEM((count, wide, cols), jnp.bfloat16),
            pltpu.VMEM((tok, cols), jnp.float32),
            pltpu.SemaphoreType.DMA((count,)),
        ],
        compiler_params=pltpu.CompilerParams(vmem_limit_bytes=limit * MIB),
        cost_estimate=SHORT,
    )(r.reshape(1), *panels, *weights, *old)


def per_device(hidden, norm_gain, wq, wk, wv, wo):
    tok, feat = hidden.shape
    n_row, n_col = lax.axis_size("row"), lax.axis_size("col")
    r, c = lax.axis_index("row"), lax.axis_index("col")
    depth = feat * n_col
    rows = wq.shape[0]
    cols = wq.shape[1]

    kv_cols = wk.shape[1]
    group = max(1, HD // kv_cols)
    stacked = jnp.stack((wk, wv), axis=1)
    for bit in range(group.bit_length() - 1):
        other = swap(stacked, "col", 1 << bit)
        stacked = order_pair(stacked, other, c, bit, 2)
    stacked = stacked.reshape(rows, 2 * HD)

    n_heads = cols // HD
    first_heads = n_heads // 2
    late_heads = n_heads - first_heads
    if n_heads >= 4:
        quarter = late_heads // 2
        sizes = [first_heads // 2, first_heads - first_heads // 2]
        sizes += [n for n in (quarter // 2, quarter - quarter // 2, late_heads - quarter) if n > 0]
    else:
        sizes = [first_heads, late_heads]
    early = 2 if n_heads >= 4 else 1
    wide, rest = first_heads * HD, late_heads * HD
    chunks = [
        wq[:, sum(sizes[:i]) * HD : sum(sizes[: i + 1]) * HD] for i in range(len(sizes))
    ]

    def by_block(far):
        return [list(pieces) for pieces in zip(*far)]

    half = HD // 2
    positions = r * tok + jnp.arange(tok)
    freqs = 10000.0 ** (-jnp.arange(half).astype(jnp.float32) / half)
    angles = positions.astype(jnp.float32)[:, None] * freqs[None, :]
    cosine, sine = jnp.cos(angles), jnp.sin(angles)
    cosine = jnp.concatenate([cosine, cosine], axis=1)
    sine = jnp.concatenate([-sine, sine], axis=1)
    factor = HD ** (-0.5) * math.log2(math.e)

    per = rows // feat

    def put(panel, found):
        for source, first, piece in found:
            slot = (source // per ^ r) * per + source % per
            panel = lax.dynamic_update_slice(panel, piece[None], (slot, first, 0))
        return panel

    def put_hidden(panel, squares, found):
        for source, first, piece in found:
            wider = piece.astype(jnp.float32)
            sums = jnp.sum(wider * wider, axis=1)
            for h in range(2):
                if first <= h * tok // 2 < first + piece.shape[0]:
                    at = h * tok // 2 - first
                    squares[h] += sums[at : at + tok // 2]
            gain = lax.dynamic_slice(norm_gain, (source * feat,), (feat,))
            panel = put(panel, [(source, first, (wider * gain).astype(jnp.bfloat16))])
        return panel, squares

    ring = Ring(hidden, 1)
    hops = n_col // 2
    x_sent = exchange(stacked)
    got_x = []
    zeros = [jnp.zeros((tok // 2,), jnp.float32)] * 2
    panel, squares = put_hidden(blank((n_col, tok, feat)), zeros, ring.found)
    for i in range(hops):
        last_hop = i == hops - 1
        tie = ring.last[0][1]
        sent = [] if x_sent is None else [x_sent]
        ahead = chunks[i : i + 1] if i < len(sizes) - 1 else []
        beside = [panel, *squares, cosine, sine, *sent, *ahead]
        if last_hop:
            near = gather_near(after(stacked, tie))
            kv_weights = [*near, *gather_near(after(got_x[0], tie))]
            beside += kv_weights
        found, beside = ring.hop(beside)
        (panel, *squares, cosine, sine), beside = take(beside, 5)
        panel, squares = put_hidden(panel, squares, found)
        sent, ahead, kv_weights = take(beside, len(sent), len(ahead))
        got_x += sent
        x_sent = exchange(ahead[0]) if ahead else None
    blocks_near = len(kv_weights) // 2
    kv_near, kv_far = take(kv_weights, blocks_near)
    scale = lax.rsqrt(jnp.concatenate(squares) / depth + 1e-05)[:, None]

    kv = project(panel, kv_near, by_block([kv_far]), 0, 1, 1.0, scale, cosine, sine)
    scale = after(scale, kv)
    q_far = [gather_near(after(x, *kv_weights)) for x in got_x[1 : 1 + early]]
    q_near = gather_near(after(wq, *kv_weights))
    queries = project(
        panel, q_near, by_block(q_far[:early]), 0, first_heads, factor, scale, cosine, sine
    )
    beside = [exchange(kv), queries, chunks[-1], *gather_near(kv)]
    if x_sent is not None:
        beside.append(x_sent)
    kv_other, queries, last_chunk, *beside = lax.optimization_barrier(tuple(beside))
    kv_pieces, arrived = take(beside, blocks_near)
    kv_pieces = [*kv_pieces, *gather_near(kv_other)]
    late_far = [gather_near(piece) for piece in (*got_x[1 + early :], *arrived)]
    late_far = [list(far) for far in late_far]
    last_other = exchange(last_chunk)
    o_weights = lax.all_gather(after(wo, kv_other), "row")
    heads = attend(r, [queries], kv_pieces)

    ring = Ring(heads, 1)
    panels = [put(blank((n_col, tok, wide)), ring.found), blank((n_col, tok, rest))]
    tables = scale, cosine, sine
    late, first = [], wide
    if late_far:
        late_far = by_block(late_far)
        late.append(project(panel, q_near, late_far, first, -1, factor, *tables))
        first += late[0].shape[1]
    found, (last_other, *rest_of) = ring.hop([last_other, *panels, *late])
    panels, late = take(rest_of, 2)
    panels[0] = put(panels[0], found)
    last_far = by_block([gather_near(last_other)])
    late = [*late, project(panel, q_near, last_far, first, -1, factor, *tables)]
    found, (panels[0], *late) = ring.hop([panels[0], *late])
    panels[0] = put(panels[0], found)
    heads = attend(r, late, kv_pieces)
    o_near = gather_near(after(wo, late[-1]))
    found, (heads, panels[0], *o_near) = ring.hop([heads, panels[0], *o_near])
    panels[0] = put(panels[0], found)
    second = Ring(heads, 1)
    panels[1] = put(panels[1], second.found)
    for i in range(hops):
        found, (panels[0],) = ring.hop([panels[0]])
        panels[0] = put(panels[0], found)
        found, (panels[1],) = second.hop([panels[1]])
        panels[1] = put(panels[1], found)

    half = n_col // 2
    total = finish(r, panels, (0, half), o_near, per, jnp.float32, 52)
    return finish(r, panels, (half, n_col), [o_weights], per, jnp.bfloat16, 52, total)


def solution(mesh):
    in_specs = (
        P("row", "col"),
        P(),
        P("row", "col"),
        P("row", "col"),
        P("row", "col"),
        P("row", "col"),
    )
    out_specs = P("row", "col")
    return jax.shard_map(
        per_device, mesh=mesh, in_specs=in_specs, out_specs=out_specs, check_vma=False
    )
```

```python
import functools
import math

import jax
import jax.numpy as jnp
from jax import lax
from jax.experimental import pallas as pl
from jax.experimental.pallas import tpu as pltpu
from jax.sharding import PartitionSpec as P

HD = 128
MIB = 1 << 20
SHORT = pl.CostEstimate(flops=1, bytes_accessed=1, transcendentals=0)


def after(array, *earlier):
    if not earlier:
        return array
    return lax.optimization_barrier((array, *earlier))[0]


def swap(array, axis, mask):
    return lax.ppermute(array, axis, [(i, i ^ mask) for i in range(lax.axis_size(axis))])


def row_bits():
    return [1 << b for b in reversed(range((lax.axis_size("row")).bit_length() - 1))]


def exchange(array, *earlier):
    return swap(after(array, *earlier), "row", row_bits()[0])


def gather_near(array, *earlier):
    pieces = {0: after(array, *earlier)}
    for bit in row_bits()[1:]:
        pieces.update({j ^ bit: swap(p, "row", bit) for j, p in pieces.items()})
    return [pieces[j] for j in range(len(pieces))]


def order_pair(mine, other, col_index, bit, axis_dim):
    upper = col_index // 2**bit % 2 == 1
    lower_part = jnp.where(upper, other, mine)
    upper_part = jnp.where(upper, mine, other)
    return jnp.concatenate([lower_part, upper_part], axis=axis_dim)


def ring_order(n):
    return list(range(0, n, 2)) + list(range(1, n, 2))[::-1]


def ring_source(c, hops, n):
    at = jnp.where(c % 2 == 0, c // 2, n - 1 - c // 2)
    at = (at - hops) % n
    return jnp.where(at < n // 2, 2 * at, 2 * (n - 1 - at) + 1)


def take(refs, *counts):
    out, at = [], 0
    for n in counts:
        out.append(refs[at : at + n])
        at += n
    return *out, refs[at:]


class Ring:
    def __init__(self, block, pieces):
        n = lax.axis_size("col")
        order = ring_order(n)
        self.n, self.hops = n, 0
        self.up = [(order[i], order[(i + 1) % n]) for i in range(n)]
        self.down = [(b, a) for a, b in self.up]
        self.rows = block.shape[0]
        self.found = [(lax.axis_index("col"), 0, block)]
        self.height = self.rows // pieces
        parts = [block[i * self.height : (i + 1) * self.height] for i in range(pieces)]
        self.last = [(p, p) for p in parts]

    def hop(self, beside=()):
        if self.hops == self.n // 2:
            return [], list(beside)
        c, half = self.found[0][0], self.rows // 2
        self.hops += 1
        found = []
        for i, (below, above) in enumerate(self.last):
            top = i * self.height
            firsts = [top, top]
            sends = [(below, self.up), (above, self.down)]
            if self.hops == self.n // 2:
                if len(self.last) == 1:
                    sends = [(below[:half], self.up), (above[half:], self.down)]
                    firsts = [0, half]
                else:
                    sends = [sends[0], None] if top < half else [None, sends[1]]
            got = [None if s is None else lax.ppermute(s[0], "col", s[1]) for s in sends]
            more = list(beside) if i == len(self.last) - 1 else []
            here = [g for g in got if g is not None]
            here, more = take(lax.optimization_barrier((*here, *more)), len(here))
            here = list(here)
            got = [None if g is None else here.pop(0) for g in got]
            self.last[i] = tuple(got)
            for way, piece in enumerate(got):
                if piece is not None:
                    hops = self.hops if way == 0 else -self.hops
                    found.append((ring_source(c, hops, self.n), firsts[way], piece))
        self.found += found
        return found, list(more)


def blank(shape):
    return pl.pallas_call(
        lambda o_ref: None,
        out_specs=pl.BlockSpec(memory_space=pl.ANY),
        out_shape=jax.ShapeDtypeStruct(shape, jnp.bfloat16),
    )()


def multiply(steps, a_buf, w_bufs, accs, a_sem, w_sem):
    for i, (left, rights) in enumerate(steps):
        pltpu.make_async_copy(left, a_buf.at[i], a_sem.at[i]).start()
        for g, chunks in enumerate(rights):
            at = 0
            for chunk in chunks:
                wide = chunk.shape[1]
                into = w_bufs[g].at[i, :, pl.ds(at, wide)]
                pltpu.make_async_copy(chunk, into, w_sem.at[g, i]).start()
                at += wide

    def body(i, carry):
        pltpu.make_async_copy(a_buf.at[i], a_buf.at[i], a_sem.at[i]).wait()
        for g, acc in enumerate(accs):
            pltpu.make_async_copy(w_bufs[g].at[i], w_bufs[g].at[i], w_sem.at[g, i]).wait()
            acc[...] += jnp.dot(a_buf[i], w_bufs[g][i], preferred_element_type=jnp.float32)
        return carry

    lax.fori_loop(0, len(steps), body, 0)


def project_kernel(near, far, chunks, first, heads, factor, panel_ref, *refs):
    near_refs, far_refs, (scale_ref, cos_ref, sin_ref), rest = take(refs, near, far * chunks, 3)
    o_ref, a_buf, w_buf, acc, a_sem, w_sem = rest
    slots, _, depth = panel_ref.shape
    per = slots // (near + far)
    cols = acc.shape[1]
    steps = []
    for k in range(slots):
        p, rows = k // per, pl.ds(k % per * depth, depth)
        if p < near:
            right = [near_refs[p].at[rows, pl.ds(first, cols)]]
        else:
            at = (p - near) * chunks
            right = [ref.at[rows, :] for ref in far_refs[at : at + chunks]]
        steps.append((panel_ref.at[k], [right]))
    acc[...] = jnp.zeros_like(acc)
    multiply(steps, a_buf, [w_buf], [acc], a_sem, w_sem)
    scale = scale_ref[...] * factor
    for h in range(cols // HD):
        at = pl.ds(h * HD, HD)
        x = acc[:, at] * scale
        if heads < 0 or h < heads:
            x = x * cos_ref[...] + pltpu.roll(x, HD // 2, 1) * sin_ref[...]
        o_ref[:, at] = x.astype(o_ref.dtype)


def project(panel, near, far, first, heads, factor, scale, cos, sin):
    slots, tok, depth = panel.shape
    chunks = len(far[0])
    cols = sum(w.shape[1] for w in far[0])
    hbm = pl.BlockSpec(memory_space=pl.ANY)
    vmem = pl.BlockSpec(memory_space=pltpu.VMEM)
    return pl.pallas_call(
        functools.partial(project_kernel, len(near), len(far), chunks, first, heads, factor),
        in_specs=[hbm] * (1 + len(near) + len(far) * chunks) + [vmem] * 3,
        out_specs=vmem,
        out_shape=jax.ShapeDtypeStruct((tok, cols), jnp.bfloat16),
        scratch_shapes=[
            pltpu.VMEM((slots, tok, depth), jnp.bfloat16),
            pltpu.VMEM((slots, depth, cols), jnp.bfloat16),
            pltpu.VMEM((tok, cols), jnp.float32),
            pltpu.SemaphoreType.DMA((slots,)),
            pltpu.SemaphoreType.DMA((1, slots)),
        ],
        compiler_params=pltpu.CompilerParams(vmem_limit_bytes=60 * MIB),
        cost_estimate=SHORT,
    )(panel, *near, *[w for pieces in far for w in pieces], scale, cos, sin)


def attend_kernel(parts, chunks, pair, r_ref, *refs):
    chunk_refs, pieces = refs[:chunks], refs[chunks : chunks + parts]
    o_ref, q_ref, turned, top, total, acc = refs[chunks + parts :]
    r = r_ref[0]
    tok = q_ref.shape[0]
    step = pl.program_id(0)
    per = pl.num_programs(0) // chunks
    for i in range(chunks):

        @pl.when(step // per == i)
        def _():
            q_ref[...] = chunk_refs[i][...]

    dims = (((1,), (1,)), ((), ()))

    @pl.when(step == 0)
    def _():
        for j in range(parts):
            turned[j] = pieces[j][:, HD:].T

    def scores(j, g):
        return lax.dot_general(
            pieces[j][:, :HD],
            q_ref[:, g * HD : (g + 1) * HD],
            dims,
            preferred_element_type=jnp.float32,
        )

    key = lax.broadcasted_iota(jnp.int32, (tok, tok), 0)
    query = lax.broadcasted_iota(jnp.int32, (tok, tok), 1)
    for g in range(pair):
        s = jnp.where(key <= query, scores(0, g), -jnp.inf)
        m = jnp.max(s, axis=0, keepdims=True)
        p = jnp.exp2(s - m)
        top[g] = m
        total[g] = jnp.sum(p, axis=0, keepdims=True)
        acc[g] = jnp.dot(turned[0], p.astype(jnp.bfloat16), preferred_element_type=jnp.float32)
    for j in range(1, parts):

        @pl.when(jnp.bitwise_xor(r, j) < r)
        def _():
            for g in range(pair):
                s = scores(j, g)
                m = jnp.maximum(top[g], jnp.max(s, axis=0, keepdims=True))
                keep = jnp.exp2(top[g] - m)
                p = jnp.exp2(s - m)
                top[g] = m
                total[g] = total[g] * keep + jnp.sum(p, axis=0, keepdims=True)
                acc[g] = acc[g] * keep + jnp.dot(
                    turned[j], p.astype(jnp.bfloat16), preferred_element_type=jnp.float32
                )

    for g in range(pair):
        o_ref[:, g * HD : (g + 1) * HD] = (acc[g] / total[g]).T.astype(o_ref.dtype)


def attend(r, queries, pieces):
    tok, cols = queries[0].shape
    chunks, parts = len(queries), len(pieces)
    pair = 2 if cols // HD % 2 == 0 else 1
    per = cols // (HD * pair)
    heads = chunks * cols // HD

    def query_spec(i):
        return pl.BlockSpec((tok, pair * HD), lambda h, r: (0, jnp.clip(h - i * per, 0, per - 1)))

    return pl.pallas_call(
        functools.partial(attend_kernel, parts, chunks, pair),
        grid_spec=pltpu.PrefetchScalarGridSpec(
            num_scalar_prefetch=1,
            grid=(chunks * per,),
            in_specs=[query_spec(i) for i in range(chunks)]
            + [pl.BlockSpec((tok, 2 * HD), lambda h, r: (0, 0)) for _ in pieces],
            out_specs=pl.BlockSpec((tok, pair * HD), lambda h, r: (0, h)),
            scratch_shapes=[
                pltpu.VMEM((tok, pair * HD), jnp.bfloat16),
                pltpu.VMEM((parts, HD, tok), jnp.bfloat16),
                pltpu.VMEM((pair, 1, tok), jnp.float32),
                pltpu.VMEM((pair, 1, tok), jnp.float32),
                pltpu.VMEM((pair, HD, tok), jnp.float32),
            ],
        ),
        out_shape=jax.ShapeDtypeStruct((tok, chunks * cols), jnp.bfloat16),
        compiler_params=pltpu.CompilerParams(
            dimension_semantics=("arbitrary",), vmem_limit_bytes=32 * MIB
        ),
        cost_estimate=SHORT,
    )(r.reshape(1), *queries, *pieces)


def finish_kernel(steps, per, rows, n_panels, near, others, r_ref, *refs):
    panels, near_refs, rest = take(refs, n_panels, near)
    gathered, (*old, o_ref, a_buf, w_buf, acc, a_sem, w_sem) = take(rest, others)
    depth = a_buf.shape[2]
    plan = []
    for g, k in steps:
        at = pl.ds(k % per * rows + g * depth, depth)
        if k // per < near:
            right = near_refs[k // per].at[at, :]
        else:
            right = gathered[0].at[jnp.bitwise_xor(r_ref[0], k // per), at, :]
        plan.append((panels[g].at[k], [[right]]))
    acc[...] = old[0][...] if old else jnp.zeros_like(acc)
    multiply(plan, a_buf, [w_buf], [acc], a_sem, w_sem)
    o_ref[...] = acc[...].astype(o_ref.dtype)


def finish(r, panels, steps, near, gathered, per, rows, dtype, total=None):
    _, tok, wide = panels[0].shape
    cols = near[0].shape[1]
    count = len(steps)
    others = [] if gathered is None else [gathered]
    old = [] if total is None else [total]
    hbm = pl.BlockSpec(memory_space=pl.ANY)
    vmem = pl.BlockSpec(memory_space=pltpu.VMEM)
    return pl.pallas_call(
        functools.partial(
            finish_kernel, steps, per, rows, len(panels), len(near), len(others)
        ),
        in_specs=[pl.BlockSpec(memory_space=pltpu.SMEM)]
        + [hbm] * (len(panels) + len(near) + len(others))
        + [vmem] * len(old),
        out_specs=vmem,
        out_shape=jax.ShapeDtypeStruct((tok, cols), dtype),
        scratch_shapes=[
            pltpu.VMEM((count, tok, wide), jnp.bfloat16),
            pltpu.VMEM((count, wide, cols), jnp.bfloat16),
            pltpu.VMEM((tok, cols), jnp.float32),
            pltpu.SemaphoreType.DMA((count,)),
            pltpu.SemaphoreType.DMA((1, count)),
        ],
        compiler_params=pltpu.CompilerParams(vmem_limit_bytes=60 * MIB),
        cost_estimate=SHORT,
    )(r.reshape(1), *panels, *near, *others, *old)


def per_device(hidden, norm_gain, wq, wk, wv, wo):
    tok, feat = hidden.shape
    n_row, n_col = lax.axis_size("row"), lax.axis_size("col")
    r, c = lax.axis_index("row"), lax.axis_index("col")
    depth = feat * n_col
    rows = wq.shape[0]
    cols = wq.shape[1]

    kv_cols = wk.shape[1]
    group = max(1, HD // kv_cols)
    stacked = jnp.stack((wk, wv), axis=1)
    for bit in range(group.bit_length() - 1):
        other = swap(stacked, "col", 1 << bit)
        stacked = order_pair(stacked, other, c, bit, 2)
    stacked = stacked.reshape(rows, 2 * HD)

    n_heads = cols // HD
    first_heads = n_heads // 2
    late_heads = n_heads - first_heads
    if n_heads >= 4:
        sizes = [first_heads // 2, first_heads - first_heads // 2]
        sizes += [n for n in (late_heads // 4, late_heads - late_heads // 4) if n > 0]
    else:
        sizes = [first_heads, late_heads]
    early = 2 if n_heads >= 4 else 1
    wide, rest = first_heads * HD, late_heads * HD
    chunks = [
        wq[:, sum(sizes[:i]) * HD : sum(sizes[: i + 1]) * HD] for i in range(len(sizes))
    ]

    def by_block(far):
        return [list(pieces) for pieces in zip(*far)]

    half = HD // 2
    positions = r * tok + jnp.arange(tok)
    freqs = 10000.0 ** (-jnp.arange(half).astype(jnp.float32) / half)
    angles = positions.astype(jnp.float32)[:, None] * freqs[None, :]
    cosine, sine = jnp.cos(angles), jnp.sin(angles)
    cosine = jnp.concatenate([cosine, cosine], axis=1)
    sine = jnp.concatenate([-sine, sine], axis=1)
    factor = HD ** (-0.5) * math.log2(math.e)

    per = rows // feat

    def put(panel, found):
        for source, first, piece in found:
            slot = (source // per ^ r) * per + source % per
            panel = lax.dynamic_update_slice(panel, piece[None], (slot, first, 0))
        return panel

    def put_hidden(panel, squares, found):
        for source, first, piece in found:
            wider = piece.astype(jnp.float32)
            sums = jnp.sum(wider * wider, axis=1)
            for h in range(2):
                if first <= h * tok // 2 < first + piece.shape[0]:
                    at = h * tok // 2 - first
                    squares[h] += sums[at : at + tok // 2]
            gain = lax.dynamic_slice(norm_gain, (source * feat,), (feat,))
            panel = put(panel, [(source, first, (wider * gain).astype(jnp.bfloat16))])
        return panel, squares

    ring = Ring(hidden, 1)
    hops = n_col // 2
    x_sent = exchange(stacked)
    got_x = []
    zeros = [jnp.zeros((tok // 2,), jnp.float32)] * 2
    panel, squares = put_hidden(blank((n_col, tok, feat)), zeros, ring.found)
    for i in range(hops):
        last_hop = i == hops - 1
        tie = ring.last[0][1]
        sent = [] if x_sent is None else [x_sent]
        ahead = chunks[i : i + 1]
        beside = [panel, *squares, cosine, sine, *sent, *ahead]
        if last_hop:
            near = gather_near(after(stacked, tie))
            kv_weights = [*near, *gather_near(after(got_x[0], tie))]
            beside += kv_weights
        found, beside = ring.hop(beside)
        (panel, *squares, cosine, sine), beside = take(beside, 5)
        panel, squares = put_hidden(panel, squares, found)
        sent, ahead, kv_weights = take(beside, len(sent), len(ahead))
        got_x += sent
        x_sent = exchange(ahead[0]) if ahead else None
    blocks_near = len(kv_weights) // 2
    kv_near, kv_far = take(kv_weights, blocks_near)
    scale = lax.rsqrt(jnp.concatenate(squares) / depth + 1e-05)[:, None]

    kv = project(panel, kv_near, by_block([kv_far]), 0, 1, 1.0, scale, cosine, sine)
    scale = after(scale, kv)
    q_far = [gather_near(after(x, *kv_weights)) for x in got_x[1 : 1 + early]]
    q_near = gather_near(after(wq, *kv_weights))
    queries = project(
        panel, q_near, by_block(q_far[:early]), 0, first_heads, factor, scale, cosine, sine
    )
    beside = [exchange(kv), queries, *gather_near(kv)]
    if x_sent is not None:
        beside.append(x_sent)
    kv_other, queries, *beside = lax.optimization_barrier(tuple(beside))
    kv_pieces, arrived = take(beside, blocks_near)
    kv_pieces = [*kv_pieces, *gather_near(kv_other)]
    late_far = [list(gather_near(piece)) for piece in (*got_x[1 + early :], *arrived)]
    o_weights = lax.all_gather(after(wo, kv_other), "row")
    heads = attend(r, [queries], kv_pieces)

    ring = Ring(heads, 1)
    panels = [put(blank((n_col, tok, wide)), ring.found), blank((n_col, tok, rest))]
    late = project(
        panel, q_near, by_block(late_far), wide, -1, factor, scale, cosine, sine
    )
    found, (late, *panels) = ring.hop([late, *panels])
    panels[0] = put(panels[0], found)
    heads = attend(r, [late], kv_pieces)
    o_near = gather_near(after(wo, late))
    found, (heads, panels[0], *o_near) = ring.hop([heads, panels[0], *o_near])
    panels[0] = put(panels[0], found)
    second = Ring(heads, 1)
    panels[1] = put(panels[1], second.found)
    half = n_col // 2
    for i in range(hops):
        found, (panels[0],) = ring.hop([panels[0]])
        panels[0] = put(panels[0], found)
        beside = [panels[1]]
        if i == hops - 1:
            steps = [(0, k) for k in range(half)]
            beside.append(finish(r, panels[:1], steps, o_near, None, per, cols, jnp.float32))
        found, (panels[1], *beside) = second.hop(beside)
        panels[1] = put(panels[1], found)
    (total,) = beside

    steps = [(1, k) for k in range(half)] + [(g, k) for k in range(half, n_col) for g in (0, 1)]
    return finish(r, panels, steps, o_near, o_weights, per, cols, jnp.bfloat16, total)


def solution(mesh):
    in_specs = (
        P("row", "col"),
        P(),
        P("row", "col"),
        P("row", "col"),
        P("row", "col"),
        P("row", "col"),
    )
    out_specs = P("row", "col")
    return jax.shard_map(
        per_device, mesh=mesh, in_specs=in_specs, out_specs=out_specs, check_vma=False
    )
```

```python
import functools
import math

import jax
import jax.numpy as jnp
from jax import lax
from jax.experimental import pallas as pl
from jax.experimental.pallas import tpu as pltpu
from jax.sharding import PartitionSpec as P

HD = 128
MIB = 1 << 20
SHORT = pl.CostEstimate(flops=1, bytes_accessed=1, transcendentals=0)


def after(array, *earlier):
    if not earlier:
        return array
    return lax.optimization_barrier((array, *earlier))[0]


def swap(array, axis, mask):
    return lax.ppermute(array, axis, [(i, i ^ mask) for i in range(lax.axis_size(axis))])


def row_bits():
    return [1 << b for b in reversed(range((lax.axis_size("row")).bit_length() - 1))]


def exchange(array, *earlier):
    return swap(after(array, *earlier), "row", row_bits()[0])


def gather_near(array, *earlier):
    pieces = {0: after(array, *earlier)}
    for bit in row_bits()[1:]:
        pieces.update({j ^ bit: swap(p, "row", bit) for j, p in pieces.items()})
    return [pieces[j] for j in range(len(pieces))]


def order_pair(mine, other, col_index, bit, axis_dim):
    upper = col_index // 2**bit % 2 == 1
    lower_part = jnp.where(upper, other, mine)
    upper_part = jnp.where(upper, mine, other)
    return jnp.concatenate([lower_part, upper_part], axis=axis_dim)


def ring_order(n):
    return list(range(0, n, 2)) + list(range(1, n, 2))[::-1]


def ring_source(c, hops, n):
    at = jnp.where(c % 2 == 0, c // 2, n - 1 - c // 2)
    at = (at - hops) % n
    return jnp.where(at < n // 2, 2 * at, 2 * (n - 1 - at) + 1)


def take(refs, *counts):
    out, at = [], 0
    for n in counts:
        out.append(refs[at : at + n])
        at += n
    return *out, refs[at:]


class Ring:
    def __init__(self, block, pieces):
        n = lax.axis_size("col")
        order = ring_order(n)
        self.n, self.hops = n, 0
        self.up = [(order[i], order[(i + 1) % n]) for i in range(n)]
        self.down = [(b, a) for a, b in self.up]
        self.rows = block.shape[0]
        self.found = [(lax.axis_index("col"), 0, block)]
        self.height = self.rows // pieces
        parts = [block[i * self.height : (i + 1) * self.height] for i in range(pieces)]
        self.last = [(p, p) for p in parts]

    def hop(self, beside=()):
        if self.hops == self.n // 2:
            return [], list(beside)
        c, half = self.found[0][0], self.rows // 2
        self.hops += 1
        found = []
        for i, (below, above) in enumerate(self.last):
            top = i * self.height
            firsts = [top, top]
            sends = [(below, self.up), (above, self.down)]
            if self.hops == self.n // 2:
                if len(self.last) == 1:
                    sends = [(below[:half], self.up), (above[half:], self.down)]
                    firsts = [0, half]
                else:
                    sends = [sends[0], None] if top < half else [None, sends[1]]
            got = [None if s is None else lax.ppermute(s[0], "col", s[1]) for s in sends]
            more = list(beside) if i == len(self.last) - 1 else []
            here = [g for g in got if g is not None]
            here, more = take(lax.optimization_barrier((*here, *more)), len(here))
            here = list(here)
            got = [None if g is None else here.pop(0) for g in got]
            self.last[i] = tuple(got)
            for way, piece in enumerate(got):
                if piece is not None:
                    hops = self.hops if way == 0 else -self.hops
                    found.append((ring_source(c, hops, self.n), firsts[way], piece))
        self.found += found
        return found, list(more)


def blank(shape):
    return pl.pallas_call(
        lambda o_ref: None,
        out_specs=pl.BlockSpec(memory_space=pl.ANY),
        out_shape=jax.ShapeDtypeStruct(shape, jnp.bfloat16),
    )()


def multiply(steps, a_buf, w_bufs, accs, a_sem, w_sem):
    for i, (left, rights) in enumerate(steps):
        pltpu.make_async_copy(left, a_buf.at[i], a_sem.at[i]).start()
        for g, chunks in enumerate(rights):
            at = 0
            for chunk in chunks:
                wide = chunk.shape[1]
                into = w_bufs[g].at[i, :, pl.ds(at, wide)]
                pltpu.make_async_copy(chunk, into, w_sem.at[g, i]).start()
                at += wide

    def body(i, carry):
        pltpu.make_async_copy(a_buf.at[i], a_buf.at[i], a_sem.at[i]).wait()
        for g, acc in enumerate(accs):
            pltpu.make_async_copy(w_bufs[g].at[i], w_bufs[g].at[i], w_sem.at[g, i]).wait()
            acc[...] += jnp.dot(a_buf[i], w_bufs[g][i], preferred_element_type=jnp.float32)
        return carry

    lax.fori_loop(0, len(steps), body, 0)


def project_kernel(near, far, chunks, first, heads, factor, panel_ref, *refs):
    near_refs, far_refs, (scale_ref, cos_ref, sin_ref), rest = take(refs, near, far * chunks, 3)
    o_ref, a_buf, w_buf, acc, a_sem, w_sem = rest
    slots, _, depth = panel_ref.shape
    per = slots // (near + far)
    cols = acc.shape[1]
    steps = []
    for k in range(slots):
        p, rows = k // per, pl.ds(k % per * depth, depth)
        if p < near:
            right = [near_refs[p].at[rows, pl.ds(first, cols)]]
        else:
            at = (p - near) * chunks
            right = [ref.at[rows, :] for ref in far_refs[at : at + chunks]]
        steps.append((panel_ref.at[k], [right]))
    acc[...] = jnp.zeros_like(acc)
    multiply(steps, a_buf, [w_buf], [acc], a_sem, w_sem)
    scale = scale_ref[...] * factor
    for h in range(cols // HD):
        at = pl.ds(h * HD, HD)
        x = acc[:, at] * scale
        if heads < 0 or h < heads:
            x = x * cos_ref[...] + pltpu.roll(x, HD // 2, 1) * sin_ref[...]
        o_ref[:, at] = x.astype(o_ref.dtype)


def project(panel, near, far, first, heads, factor, scale, cos, sin):
    slots, tok, depth = panel.shape
    chunks = len(far[0])
    cols = sum(w.shape[1] for w in far[0])
    hbm = pl.BlockSpec(memory_space=pl.ANY)
    vmem = pl.BlockSpec(memory_space=pltpu.VMEM)
    return pl.pallas_call(
        functools.partial(project_kernel, len(near), len(far), chunks, first, heads, factor),
        in_specs=[hbm] * (1 + len(near) + len(far) * chunks) + [vmem] * 3,
        out_specs=vmem,
        out_shape=jax.ShapeDtypeStruct((tok, cols), jnp.bfloat16),
        scratch_shapes=[
            pltpu.VMEM((slots, tok, depth), jnp.bfloat16),
            pltpu.VMEM((slots, depth, cols), jnp.bfloat16),
            pltpu.VMEM((tok, cols), jnp.float32),
            pltpu.SemaphoreType.DMA((slots,)),
            pltpu.SemaphoreType.DMA((1, slots)),
        ],
        compiler_params=pltpu.CompilerParams(vmem_limit_bytes=60 * MIB),
        cost_estimate=SHORT,
    )(panel, *near, *[w for pieces in far for w in pieces], scale, cos, sin)


def attend_kernel(parts, chunks, pair, r_ref, *refs):
    chunk_refs, pieces = refs[:chunks], refs[chunks : chunks + parts]
    o_ref, q_ref, turned, top, total, acc = refs[chunks + parts :]
    r = r_ref[0]
    tok = q_ref.shape[0]
    step = pl.program_id(0)
    per = pl.num_programs(0) // chunks
    for i in range(chunks):

        @pl.when(step // per == i)
        def _():
            q_ref[...] = chunk_refs[i][...]

    dims = (((1,), (1,)), ((), ()))

    @pl.when(step == 0)
    def _():
        for j in range(parts):
            turned[j] = pieces[j][:, HD:].T

    def scores(j, g):
        return lax.dot_general(
            pieces[j][:, :HD],
            q_ref[:, g * HD : (g + 1) * HD],
            dims,
            preferred_element_type=jnp.float32,
        )

    key = lax.broadcasted_iota(jnp.int32, (tok, tok), 0)
    query = lax.broadcasted_iota(jnp.int32, (tok, tok), 1)
    for g in range(pair):
        s = jnp.where(key <= query, scores(0, g), -jnp.inf)
        m = jnp.max(s, axis=0, keepdims=True)
        p = jnp.exp2(s - m)
        top[g] = m
        total[g] = jnp.sum(p, axis=0, keepdims=True)
        acc[g] = jnp.dot(turned[0], p.astype(jnp.bfloat16), preferred_element_type=jnp.float32)
    for j in range(1, parts):

        @pl.when(jnp.bitwise_xor(r, j) < r)
        def _():
            for g in range(pair):
                s = scores(j, g)
                m = jnp.maximum(top[g], jnp.max(s, axis=0, keepdims=True))
                keep = jnp.exp2(top[g] - m)
                p = jnp.exp2(s - m)
                top[g] = m
                total[g] = total[g] * keep + jnp.sum(p, axis=0, keepdims=True)
                acc[g] = acc[g] * keep + jnp.dot(
                    turned[j], p.astype(jnp.bfloat16), preferred_element_type=jnp.float32
                )

    for g in range(pair):
        o_ref[:, g * HD : (g + 1) * HD] = (acc[g] / total[g]).T.astype(o_ref.dtype)


def attend(r, queries, pieces):
    tok, cols = queries[0].shape
    chunks, parts = len(queries), len(pieces)
    pair = 2 if cols // HD % 2 == 0 else 1
    per = cols // (HD * pair)
    heads = chunks * cols // HD

    def query_spec(i):
        return pl.BlockSpec((tok, pair * HD), lambda h, r: (0, jnp.clip(h - i * per, 0, per - 1)))

    return pl.pallas_call(
        functools.partial(attend_kernel, parts, chunks, pair),
        grid_spec=pltpu.PrefetchScalarGridSpec(
            num_scalar_prefetch=1,
            grid=(chunks * per,),
            in_specs=[query_spec(i) for i in range(chunks)]
            + [pl.BlockSpec((tok, 2 * HD), lambda h, r: (0, 0)) for _ in pieces],
            out_specs=pl.BlockSpec((tok, pair * HD), lambda h, r: (0, h)),
            scratch_shapes=[
                pltpu.VMEM((tok, pair * HD), jnp.bfloat16),
                pltpu.VMEM((parts, HD, tok), jnp.bfloat16),
                pltpu.VMEM((pair, 1, tok), jnp.float32),
                pltpu.VMEM((pair, 1, tok), jnp.float32),
                pltpu.VMEM((pair, HD, tok), jnp.float32),
            ],
        ),
        out_shape=jax.ShapeDtypeStruct((tok, chunks * cols), jnp.bfloat16),
        compiler_params=pltpu.CompilerParams(
            dimension_semantics=("arbitrary",), vmem_limit_bytes=32 * MIB
        ),
        cost_estimate=SHORT,
    )(r.reshape(1), *queries, *pieces)


def finish_kernel(steps, per, rows, n_panels, near, others, r_ref, *refs):
    panels, near_refs, rest = take(refs, n_panels, near)
    gathered, (*old, o_ref, a_buf, w_buf, acc, a_sem, w_sem) = take(rest, others)
    depth = a_buf.shape[2]
    plan = []
    for g, k in steps:
        at = pl.ds(k % per * rows + g * depth, depth)
        if k // per < near:
            right = near_refs[k // per].at[at, :]
        else:
            right = gathered[0].at[jnp.bitwise_xor(r_ref[0], k // per), at, :]
        plan.append((panels[g].at[k], [[right]]))
    acc[...] = old[0][...] if old else jnp.zeros_like(acc)
    multiply(plan, a_buf, [w_buf], [acc], a_sem, w_sem)
    o_ref[...] = acc[...].astype(o_ref.dtype)


def finish(r, panels, steps, near, gathered, per, rows, dtype, total=None):
    _, tok, wide = panels[0].shape
    cols = near[0].shape[1]
    count = len(steps)
    others = [] if gathered is None else [gathered]
    old = [] if total is None else [total]
    hbm = pl.BlockSpec(memory_space=pl.ANY)
    vmem = pl.BlockSpec(memory_space=pltpu.VMEM)
    return pl.pallas_call(
        functools.partial(
            finish_kernel, steps, per, rows, len(panels), len(near), len(others)
        ),
        in_specs=[pl.BlockSpec(memory_space=pltpu.SMEM)]
        + [hbm] * (len(panels) + len(near) + len(others))
        + [vmem] * len(old),
        out_specs=vmem,
        out_shape=jax.ShapeDtypeStruct((tok, cols), dtype),
        scratch_shapes=[
            pltpu.VMEM((count, tok, wide), jnp.bfloat16),
            pltpu.VMEM((count, wide, cols), jnp.bfloat16),
            pltpu.VMEM((tok, cols), jnp.float32),
            pltpu.SemaphoreType.DMA((count,)),
            pltpu.SemaphoreType.DMA((1, count)),
        ],
        compiler_params=pltpu.CompilerParams(vmem_limit_bytes=60 * MIB),
        cost_estimate=SHORT,
    )(r.reshape(1), *panels, *near, *others, *old)


def per_device(hidden, norm_gain, wq, wk, wv, wo):
    tok, feat = hidden.shape
    n_row, n_col = lax.axis_size("row"), lax.axis_size("col")
    r, c = lax.axis_index("row"), lax.axis_index("col")
    depth = feat * n_col
    rows = wq.shape[0]
    cols = wq.shape[1]

    kv_cols = wk.shape[1]
    group = max(1, HD // kv_cols)
    stacked = jnp.stack((wk, wv), axis=1)
    for bit in range(group.bit_length() - 1):
        other = swap(stacked, "col", 1 << bit)
        stacked = order_pair(stacked, other, c, bit, 2)
    stacked = stacked.reshape(rows, 2 * HD)

    n_heads = cols // HD
    first_heads = n_heads // 2
    late_heads = n_heads - first_heads
    if n_heads >= 4:
        sizes = [first_heads // 2, first_heads - first_heads // 2]
        eighth = late_heads // 4
        sizes += [n for n in (eighth, late_heads - 2 * eighth, eighth) if n > 0]
    else:
        sizes = [first_heads, late_heads]
    early = 2 if n_heads >= 4 else 1
    wide, rest = first_heads * HD, late_heads * HD
    chunks = [
        wq[:, sum(sizes[:i]) * HD : sum(sizes[: i + 1]) * HD] for i in range(len(sizes))
    ]

    def by_block(far):
        return [list(pieces) for pieces in zip(*far)]

    half = HD // 2
    positions = r * tok + jnp.arange(tok)
    freqs = 10000.0 ** (-jnp.arange(half).astype(jnp.float32) / half)
    angles = positions.astype(jnp.float32)[:, None] * freqs[None, :]
    cosine, sine = jnp.cos(angles), jnp.sin(angles)
    cosine = jnp.concatenate([cosine, cosine], axis=1)
    sine = jnp.concatenate([-sine, sine], axis=1)
    factor = HD ** (-0.5) * math.log2(math.e)

    per = rows // feat

    def put(panel, found):
        for source, first, piece in found:
            slot = (source // per ^ r) * per + source % per
            panel = lax.dynamic_update_slice(panel, piece[None], (slot, first, 0))
        return panel

    def put_hidden(panel, squares, found):
        for source, first, piece in found:
            wider = piece.astype(jnp.float32)
            sums = jnp.sum(wider * wider, axis=1)
            for h in range(2):
                if first <= h * tok // 2 < first + piece.shape[0]:
                    at = h * tok // 2 - first
                    squares[h] += sums[at : at + tok // 2]
            gain = lax.dynamic_slice(norm_gain, (source * feat,), (feat,))
            panel = put(panel, [(source, first, (wider * gain).astype(jnp.bfloat16))])
        return panel, squares

    ring = Ring(hidden, 1)
    hops = n_col // 2
    x_sent = exchange(stacked)
    got_x = []
    zeros = [jnp.zeros((tok // 2,), jnp.float32)] * 2
    panel, squares = put_hidden(blank((n_col, tok, feat)), zeros, ring.found)
    for i in range(hops):
        last_hop = i == hops - 1
        tie = ring.last[0][1]
        sent = [] if x_sent is None else [x_sent]
        ahead = chunks[i : i + 1] if i < len(sizes) - 1 else []
        beside = [panel, *squares, cosine, sine, *sent, *ahead]
        if last_hop:
            near = gather_near(after(stacked, tie))
            kv_weights = [*near, *gather_near(after(got_x[0], tie))]
            beside += kv_weights
        found, beside = ring.hop(beside)
        (panel, *squares, cosine, sine), beside = take(beside, 5)
        panel, squares = put_hidden(panel, squares, found)
        sent, ahead, kv_weights = take(beside, len(sent), len(ahead))
        got_x += sent
        x_sent = exchange(ahead[0]) if ahead else None
    blocks_near = len(kv_weights) // 2
    kv_near, kv_far = take(kv_weights, blocks_near)
    scale = lax.rsqrt(jnp.concatenate(squares) / depth + 1e-05)[:, None]

    kv = project(panel, kv_near, by_block([kv_far]), 0, 1, 1.0, scale, cosine, sine)
    scale = after(scale, kv)
    q_far = [gather_near(after(x, *kv_weights)) for x in got_x[1 : 1 + early]]
    q_near = gather_near(after(wq, *kv_weights))
    queries = project(
        panel, q_near, by_block(q_far[:early]), 0, first_heads, factor, scale, cosine, sine
    )
    beside = [exchange(kv), queries, chunks[-1], *gather_near(kv)]
    if x_sent is not None:
        beside.append(x_sent)
    kv_other, queries, last_chunk, *beside = lax.optimization_barrier(tuple(beside))
    kv_pieces, arrived = take(beside, blocks_near)
    kv_pieces = [*kv_pieces, *gather_near(kv_other)]
    late_far = [list(gather_near(piece)) for piece in (*got_x[1 + early :], *arrived)]
    last_other = exchange(last_chunk)
    o_weights = lax.all_gather(after(wo, kv_other), "row")
    heads = attend(r, [queries], kv_pieces)

    ring = Ring(heads, 1)
    panels = [put(blank((n_col, tok, wide)), ring.found), blank((n_col, tok, rest))]
    tables = scale, cosine, sine
    late, first = [], wide
    if late_far:
        late.append(project(panel, q_near, by_block(late_far), first, -1, factor, *tables))
        first += late[0].shape[1]
    found, (last_other, *beside) = ring.hop([last_other, *panels, *late])
    panels, late = take(beside, 2)
    panels[0] = put(panels[0], found)
    last_far = by_block([gather_near(last_other)])
    late = [*late, project(panel, q_near, last_far, first, -1, factor, *tables)]
    late = jnp.concatenate(late, axis=1)
    heads = attend(r, [late], kv_pieces)
    o_near = gather_near(after(wo, last_other))
    found, (heads, panels[0], *o_near) = ring.hop([heads, panels[0], *o_near])
    panels[0] = put(panels[0], found)
    second = Ring(heads, 1)
    panels[1] = put(panels[1], second.found)
    half = n_col // 2
    for i in range(hops):
        found, (panels[0],) = ring.hop([panels[0]])
        panels[0] = put(panels[0], found)
        beside = [panels[1]]
        if i == hops - 1:
            steps = [(0, k) for k in range(half)]
            beside.append(finish(r, panels[:1], steps, o_near, None, per, cols, jnp.float32))
        found, (panels[1], *beside) = second.hop(beside)
        panels[1] = put(panels[1], found)
    (total,) = beside

    steps = [(1, k) for k in range(half)] + [(g, k) for k in range(half, n_col) for g in (0, 1)]
    return finish(r, panels, steps, o_near, o_weights, per, cols, jnp.bfloat16, total)


def solution(mesh):
    in_specs = (
        P("row", "col"),
        P(),
        P("row", "col"),
        P("row", "col"),
        P("row", "col"),
        P("row", "col"),
    )
    out_specs = P("row", "col")
    return jax.shard_map(
        per_device, mesh=mesh, in_specs=in_specs, out_specs=out_specs, check_vma=False
    )
```

```python
import functools
import math

import jax
import jax.numpy as jnp
from jax import lax
from jax.experimental import pallas as pl
from jax.experimental.pallas import tpu as pltpu
from jax.sharding import PartitionSpec as P

HD = 128
MIB = 1 << 20
SHORT = pl.CostEstimate(flops=1, bytes_accessed=1, transcendentals=0)


def after(array, *earlier):
    if not earlier:
        return array
    return lax.optimization_barrier((array, *earlier))[0]


def swap(array, axis, mask):
    return lax.ppermute(array, axis, [(i, i ^ mask) for i in range(lax.axis_size(axis))])


def row_bits():
    return [1 << b for b in reversed(range((lax.axis_size("row")).bit_length() - 1))]


def exchange(array, *earlier):
    return swap(after(array, *earlier), "row", row_bits()[0])


def gather_near(array, *earlier):
    pieces = {0: after(array, *earlier)}
    for bit in row_bits()[1:]:
        pieces.update({j ^ bit: swap(p, "row", bit) for j, p in pieces.items()})
    return [pieces[j] for j in range(len(pieces))]


def order_pair(mine, other, col_index, bit, axis_dim):
    upper = col_index // 2**bit % 2 == 1
    lower_part = jnp.where(upper, other, mine)
    upper_part = jnp.where(upper, mine, other)
    return jnp.concatenate([lower_part, upper_part], axis=axis_dim)


def ring_order(n):
    return list(range(0, n, 2)) + list(range(1, n, 2))[::-1]


def ring_source(c, hops, n):
    at = jnp.where(c % 2 == 0, c // 2, n - 1 - c // 2)
    at = (at - hops) % n
    return jnp.where(at < n // 2, 2 * at, 2 * (n - 1 - at) + 1)


def take(refs, *counts):
    out, at = [], 0
    for n in counts:
        out.append(refs[at : at + n])
        at += n
    return *out, refs[at:]


class Ring:
    def __init__(self, block, pieces):
        n = lax.axis_size("col")
        order = ring_order(n)
        self.n, self.hops = n, 0
        self.up = [(order[i], order[(i + 1) % n]) for i in range(n)]
        self.down = [(b, a) for a, b in self.up]
        self.rows = block.shape[0]
        self.found = [(lax.axis_index("col"), 0, block)]
        self.height = self.rows // pieces
        parts = [block[i * self.height : (i + 1) * self.height] for i in range(pieces)]
        self.last = [(p, p) for p in parts]

    def hop(self, beside=()):
        if self.hops == self.n // 2:
            return [], list(beside)
        c, half = self.found[0][0], self.rows // 2
        self.hops += 1
        found = []
        for i, (below, above) in enumerate(self.last):
            top = i * self.height
            firsts = [top, top]
            sends = [(below, self.up), (above, self.down)]
            if self.hops == self.n // 2:
                if len(self.last) == 1:
                    sends = [(below[:half], self.up), (above[half:], self.down)]
                    firsts = [0, half]
                else:
                    sends = [sends[0], None] if top < half else [None, sends[1]]
            got = [None if s is None else lax.ppermute(s[0], "col", s[1]) for s in sends]
            more = list(beside) if i == len(self.last) - 1 else []
            here = [g for g in got if g is not None]
            here, more = take(lax.optimization_barrier((*here, *more)), len(here))
            here = list(here)
            got = [None if g is None else here.pop(0) for g in got]
            self.last[i] = tuple(got)
            for way, piece in enumerate(got):
                if piece is not None:
                    hops = self.hops if way == 0 else -self.hops
                    found.append((ring_source(c, hops, self.n), firsts[way], piece))
        self.found += found
        return found, list(more)


def blank(shape):
    return pl.pallas_call(
        lambda o_ref: None,
        out_specs=pl.BlockSpec(memory_space=pl.ANY),
        out_shape=jax.ShapeDtypeStruct(shape, jnp.bfloat16),
    )()


def multiply(steps, a_buf, w_bufs, accs, a_sem, w_sem):
    for i, (left, rights) in enumerate(steps):
        pltpu.make_async_copy(left, a_buf.at[i], a_sem.at[i]).start()
        for g, chunks in enumerate(rights):
            at = 0
            for chunk in chunks:
                wide = chunk.shape[1]
                into = w_bufs[g].at[i, :, pl.ds(at, wide)]
                pltpu.make_async_copy(chunk, into, w_sem.at[g, i]).start()
                at += wide

    def body(i, carry):
        pltpu.make_async_copy(a_buf.at[i], a_buf.at[i], a_sem.at[i]).wait()
        for g, acc in enumerate(accs):
            pltpu.make_async_copy(w_bufs[g].at[i], w_bufs[g].at[i], w_sem.at[g, i]).wait()
            acc[...] += jnp.dot(a_buf[i], w_bufs[g][i], preferred_element_type=jnp.float32)
        return carry

    lax.fori_loop(0, len(steps), body, 0)


def project_kernel(near, far, chunks, first, heads, factor, panel_ref, *refs):
    near_refs, far_refs, (scale_ref, cos_ref, sin_ref), rest = take(refs, near, far * chunks, 3)
    o_ref, a_buf, w_buf, acc, a_sem, w_sem = rest
    slots, _, depth = panel_ref.shape
    per = slots // (near + far)
    cols = acc.shape[1]
    steps = []
    for k in range(slots):
        p, rows = k // per, pl.ds(k % per * depth, depth)
        if p < near:
            right = [near_refs[p].at[rows, pl.ds(first, cols)]]
        else:
            at = (p - near) * chunks
            right = [ref.at[rows, :] for ref in far_refs[at : at + chunks]]
        steps.append((panel_ref.at[k], [right]))
    acc[...] = jnp.zeros_like(acc)
    multiply(steps, a_buf, [w_buf], [acc], a_sem, w_sem)
    scale = scale_ref[...] * factor
    for h in range(cols // HD):
        at = pl.ds(h * HD, HD)
        x = acc[:, at] * scale
        if heads < 0 or h < heads:
            x = x * cos_ref[...] + pltpu.roll(x, HD // 2, 1) * sin_ref[...]
        o_ref[:, at] = x.astype(o_ref.dtype)


def project(panel, near, far, first, heads, factor, scale, cos, sin):
    slots, tok, depth = panel.shape
    chunks = len(far[0])
    cols = sum(w.shape[1] for w in far[0])
    hbm = pl.BlockSpec(memory_space=pl.ANY)
    vmem = pl.BlockSpec(memory_space=pltpu.VMEM)
    return pl.pallas_call(
        functools.partial(project_kernel, len(near), len(far), chunks, first, heads, factor),
        in_specs=[hbm] * (1 + len(near) + len(far) * chunks) + [vmem] * 3,
        out_specs=vmem,
        out_shape=jax.ShapeDtypeStruct((tok, cols), jnp.bfloat16),
        scratch_shapes=[
            pltpu.VMEM((slots, tok, depth), jnp.bfloat16),
            pltpu.VMEM((slots, depth, cols), jnp.bfloat16),
            pltpu.VMEM((tok, cols), jnp.float32),
            pltpu.SemaphoreType.DMA((slots,)),
            pltpu.SemaphoreType.DMA((1, slots)),
        ],
        compiler_params=pltpu.CompilerParams(vmem_limit_bytes=60 * MIB),
        cost_estimate=SHORT,
    )(panel, *near, *[w for pieces in far for w in pieces], scale, cos, sin)


def attend_kernel(parts, chunks, pair, r_ref, *refs):
    chunk_refs, pieces = refs[:chunks], refs[chunks : chunks + parts]
    o_ref, q_ref, turned, top, total, acc = refs[chunks + parts :]
    r = r_ref[0]
    tok = q_ref.shape[0]
    step = pl.program_id(0)
    per = pl.num_programs(0) // chunks
    for i in range(chunks):

        @pl.when(step // per == i)
        def _():
            q_ref[...] = chunk_refs[i][...]

    dims = (((1,), (1,)), ((), ()))

    @pl.when(step == 0)
    def _():
        for j in range(parts):
            turned[j] = pieces[j][:, HD:].T

    def scores(j, g):
        return lax.dot_general(
            pieces[j][:, :HD],
            q_ref[:, g * HD : (g + 1) * HD],
            dims,
            preferred_element_type=jnp.float32,
        )

    key = lax.broadcasted_iota(jnp.int32, (tok, tok), 0)
    query = lax.broadcasted_iota(jnp.int32, (tok, tok), 1)
    for g in range(pair):
        s = jnp.where(key <= query, scores(0, g), -jnp.inf)
        m = jnp.max(s, axis=0, keepdims=True)
        p = jnp.exp2(s - m)
        top[g] = m
        total[g] = jnp.sum(p, axis=0, keepdims=True)
        acc[g] = jnp.dot(turned[0], p.astype(jnp.bfloat16), preferred_element_type=jnp.float32)
    for j in range(1, parts):

        @pl.when(jnp.bitwise_xor(r, j) < r)
        def _():
            for g in range(pair):
                s = scores(j, g)
                m = jnp.maximum(top[g], jnp.max(s, axis=0, keepdims=True))
                keep = jnp.exp2(top[g] - m)
                p = jnp.exp2(s - m)
                top[g] = m
                total[g] = total[g] * keep + jnp.sum(p, axis=0, keepdims=True)
                acc[g] = acc[g] * keep + jnp.dot(
                    turned[j], p.astype(jnp.bfloat16), preferred_element_type=jnp.float32
                )

    for g in range(pair):
        o_ref[:, g * HD : (g + 1) * HD] = (acc[g] / total[g]).T.astype(o_ref.dtype)


def attend(r, queries, pieces):
    tok, cols = queries[0].shape
    chunks, parts = len(queries), len(pieces)
    pair = 2 if cols // HD % 2 == 0 else 1
    per = cols // (HD * pair)
    heads = chunks * cols // HD

    def query_spec(i):
        return pl.BlockSpec((tok, pair * HD), lambda h, r: (0, jnp.clip(h - i * per, 0, per - 1)))

    return pl.pallas_call(
        functools.partial(attend_kernel, parts, chunks, pair),
        grid_spec=pltpu.PrefetchScalarGridSpec(
            num_scalar_prefetch=1,
            grid=(chunks * per,),
            in_specs=[query_spec(i) for i in range(chunks)]
            + [pl.BlockSpec((tok, 2 * HD), lambda h, r: (0, 0)) for _ in pieces],
            out_specs=pl.BlockSpec((tok, pair * HD), lambda h, r: (0, h)),
            scratch_shapes=[
                pltpu.VMEM((tok, pair * HD), jnp.bfloat16),
                pltpu.VMEM((parts, HD, tok), jnp.bfloat16),
                pltpu.VMEM((pair, 1, tok), jnp.float32),
                pltpu.VMEM((pair, 1, tok), jnp.float32),
                pltpu.VMEM((pair, HD, tok), jnp.float32),
            ],
        ),
        out_shape=jax.ShapeDtypeStruct((tok, chunks * cols), jnp.bfloat16),
        compiler_params=pltpu.CompilerParams(
            dimension_semantics=("arbitrary",), vmem_limit_bytes=32 * MIB
        ),
        cost_estimate=SHORT,
    )(r.reshape(1), *queries, *pieces)


def finish_kernel(steps, per, rows, n_panels, near, others, r_ref, *refs):
    panels, near_refs, rest = take(refs, n_panels, near)
    gathered, (*old, o_ref, a_buf, w_buf, acc, a_sem, w_sem) = take(rest, others)
    depth = a_buf.shape[2]
    plan = []
    for g, k in steps:
        at = pl.ds(k % per * rows + g * depth, depth)
        if k // per < near:
            right = near_refs[k // per].at[at, :]
        else:
            right = gathered[0].at[jnp.bitwise_xor(r_ref[0], k // per), at, :]
        plan.append((panels[g].at[k], [[right]]))
    acc[...] = old[0][...] if old else jnp.zeros_like(acc)
    multiply(plan, a_buf, [w_buf], [acc], a_sem, w_sem)
    o_ref[...] = acc[...].astype(o_ref.dtype)


def finish(r, panels, steps, near, gathered, per, rows, dtype, total=None):
    _, tok, wide = panels[0].shape
    cols = near[0].shape[1]
    count = len(steps)
    others = [] if gathered is None else [gathered]
    old = [] if total is None else [total]
    hbm = pl.BlockSpec(memory_space=pl.ANY)
    vmem = pl.BlockSpec(memory_space=pltpu.VMEM)
    return pl.pallas_call(
        functools.partial(
            finish_kernel, steps, per, rows, len(panels), len(near), len(others)
        ),
        in_specs=[pl.BlockSpec(memory_space=pltpu.SMEM)]
        + [hbm] * (len(panels) + len(near) + len(others))
        + [vmem] * len(old),
        out_specs=vmem,
        out_shape=jax.ShapeDtypeStruct((tok, cols), dtype),
        scratch_shapes=[
            pltpu.VMEM((count, tok, wide), jnp.bfloat16),
            pltpu.VMEM((count, wide, cols), jnp.bfloat16),
            pltpu.VMEM((tok, cols), jnp.float32),
            pltpu.SemaphoreType.DMA((count,)),
            pltpu.SemaphoreType.DMA((1, count)),
        ],
        compiler_params=pltpu.CompilerParams(vmem_limit_bytes=60 * MIB),
        cost_estimate=SHORT,
    )(r.reshape(1), *panels, *near, *others, *old)


def per_device(hidden, norm_gain, wq, wk, wv, wo):
    tok, feat = hidden.shape
    n_row, n_col = lax.axis_size("row"), lax.axis_size("col")
    r, c = lax.axis_index("row"), lax.axis_index("col")
    depth = feat * n_col
    rows = wq.shape[0]
    cols = wq.shape[1]

    kv_cols = wk.shape[1]
    group = max(1, HD // kv_cols)
    stacked = jnp.stack((wk, wv), axis=1)
    for bit in range(group.bit_length() - 1):
        other = swap(stacked, "col", 1 << bit)
        stacked = order_pair(stacked, other, c, bit, 2)
    stacked = stacked.reshape(rows, 2 * HD)

    n_heads = cols // HD
    first_heads = n_heads // 2
    late_heads = n_heads - first_heads
    if n_heads >= 4:
        sizes = [first_heads // 2, first_heads - first_heads // 2]
        eighth = late_heads // 4
        sizes += [n for n in (eighth, late_heads - 2 * eighth, eighth) if n > 0]
    else:
        sizes = [first_heads, late_heads]
    early = 2 if n_heads >= 4 else 1
    wide, rest = first_heads * HD, late_heads * HD
    chunks = [
        wq[:, sum(sizes[:i]) * HD : sum(sizes[: i + 1]) * HD] for i in range(len(sizes))
    ]

    def by_block(far):
        return [list(pieces) for pieces in zip(*far)]

    half = HD // 2
    positions = r * tok + jnp.arange(tok)
    freqs = 10000.0 ** (-jnp.arange(half).astype(jnp.float32) / half)
    angles = positions.astype(jnp.float32)[:, None] * freqs[None, :]
    cosine, sine = jnp.cos(angles), jnp.sin(angles)
    cosine = jnp.concatenate([cosine, cosine], axis=1)
    sine = jnp.concatenate([-sine, sine], axis=1)
    factor = HD ** (-0.5) * math.log2(math.e)

    per = rows // feat

    def put(panel, found):
        for source, first, piece in found:
            slot = (source // per ^ r) * per + source % per
            panel = lax.dynamic_update_slice(panel, piece[None], (slot, first, 0))
        return panel

    def put_hidden(panel, squares, found):
        for source, first, piece in found:
            wider = piece.astype(jnp.float32)
            sums = jnp.sum(wider * wider, axis=1)
            for h in range(2):
                if first <= h * tok // 2 < first + piece.shape[0]:
                    at = h * tok // 2 - first
                    squares[h] += sums[at : at + tok // 2]
            gain = lax.dynamic_slice(norm_gain, (source * feat,), (feat,))
            panel = put(panel, [(source, first, (wider * gain).astype(jnp.bfloat16))])
        return panel, squares

    ring = Ring(hidden, 1)
    hops = n_col // 2
    x_sent = exchange(stacked)
    got_x = []
    zeros = [jnp.zeros((tok // 2,), jnp.float32)] * 2
    panel, squares = put_hidden(blank((n_col, tok, feat)), zeros, ring.found)
    for i in range(hops):
        last_hop = i == hops - 1
        tie = ring.last[0][1]
        sent = [] if x_sent is None else [x_sent]
        ahead = chunks[i : i + 1] if i < len(sizes) - 1 else []
        beside = [panel, *squares, cosine, sine, *sent, *ahead]
        if last_hop:
            near = gather_near(after(stacked, tie))
            kv_weights = [*near, *gather_near(after(got_x[0], tie))]
            beside += kv_weights
        found, beside = ring.hop(beside)
        (panel, *squares, cosine, sine), beside = take(beside, 5)
        panel, squares = put_hidden(panel, squares, found)
        sent, ahead, kv_weights = take(beside, len(sent), len(ahead))
        got_x += sent
        x_sent = exchange(ahead[0]) if ahead else None
    blocks_near = len(kv_weights) // 2
    kv_near, kv_far = take(kv_weights, blocks_near)
    scale = lax.rsqrt(jnp.concatenate(squares) / depth + 1e-05)[:, None]

    kv = project(panel, kv_near, by_block([kv_far]), 0, 1, 1.0, scale, cosine, sine)
    scale = after(scale, kv)
    q_far = [gather_near(after(x, *kv_weights)) for x in got_x[1 : 1 + early]]
    q_near = gather_near(after(wq, *kv_weights))
    queries = project(
        panel, q_near, by_block(q_far[:early]), 0, first_heads, factor, scale, cosine, sine
    )
    beside = [exchange(kv), queries, chunks[-1], *gather_near(kv)]
    if x_sent is not None:
        beside.append(x_sent)
    kv_other, queries, last_chunk, *beside = lax.optimization_barrier(tuple(beside))
    kv_pieces, arrived = take(beside, blocks_near)
    kv_pieces = [*kv_pieces, *gather_near(kv_other)]
    late_far = [list(gather_near(piece)) for piece in (*got_x[1 + early :], *arrived)]
    last_other = exchange(last_chunk)
    o_weights = lax.all_gather(after(wo, kv_other), "row")
    heads = attend(r, [queries], kv_pieces)

    ring = Ring(heads, 1)
    panels = [put(blank((n_col, tok, wide)), ring.found), blank((n_col, tok, rest))]
    tables = scale, cosine, sine
    late, first = [], wide
    if late_far:
        late.append(project(panel, q_near, by_block(late_far), first, -1, factor, *tables))
        first += late[0].shape[1]
    found, (last_other, *beside) = ring.hop([last_other, *panels, *late])
    panels, late = take(beside, 2)
    panels[0] = put(panels[0], found)
    last_far = by_block([gather_near(last_other)])
    late = [*late, project(panel, q_near, last_far, first, -1, factor, *tables)]
    late = jnp.concatenate(late, axis=1)
    found, (late, panels[0]) = ring.hop([late, panels[0]])
    panels[0] = put(panels[0], found)
    heads = attend(r, [late], kv_pieces)
    o_near = gather_near(after(wo, late))
    found, (heads, panels[0], *o_near) = ring.hop([heads, panels[0], *o_near])
    panels[0] = put(panels[0], found)
    second = Ring(heads, 1)
    panels[1] = put(panels[1], second.found)
    half = n_col // 2
    for i in range(hops):
        found, (panels[0],) = ring.hop([panels[0]])
        panels[0] = put(panels[0], found)
        beside = [panels[1]]
        if i == hops - 1:
            steps = [(0, k) for k in range(half)]
            beside.append(finish(r, panels[:1], steps, o_near, None, per, cols, jnp.float32))
        found, (panels[1], *beside) = second.hop(beside)
        panels[1] = put(panels[1], found)
    (total,) = beside

    steps = [(1, k) for k in range(half)] + [(g, k) for k in range(half, n_col) for g in (0, 1)]
    return finish(r, panels, steps, o_near, o_weights, per, cols, jnp.bfloat16, total)


def solution(mesh):
    in_specs = (
        P("row", "col"),
        P(),
        P("row", "col"),
        P("row", "col"),
        P("row", "col"),
        P("row", "col"),
    )
    out_specs = P("row", "col")
    return jax.shard_map(
        per_device, mesh=mesh, in_specs=in_specs, out_specs=out_specs, check_vma=False
    )
```

```python
import functools
import math

import jax
import jax.numpy as jnp
from jax import lax
from jax.experimental import pallas as pl
from jax.experimental.pallas import tpu as pltpu
from jax.sharding import PartitionSpec as P

HD = 128
MIB = 1 << 20
SHORT = pl.CostEstimate(flops=1, bytes_accessed=1, transcendentals=0)


def after(array, *earlier):
    if not earlier:
        return array
    return lax.optimization_barrier((array, *earlier))[0]


def swap(array, axis, mask):
    return lax.ppermute(array, axis, [(i, i ^ mask) for i in range(lax.axis_size(axis))])


def row_bits():
    return [1 << b for b in reversed(range((lax.axis_size("row")).bit_length() - 1))]


def exchange(array, *earlier):
    return swap(after(array, *earlier), "row", row_bits()[0])


def gather_near(array, *earlier):
    pieces = {0: after(array, *earlier)}
    for bit in row_bits()[1:]:
        pieces.update({j ^ bit: swap(p, "row", bit) for j, p in pieces.items()})
    return [pieces[j] for j in range(len(pieces))]


def order_pair(mine, other, col_index, bit, axis_dim):
    upper = col_index // 2**bit % 2 == 1
    lower_part = jnp.where(upper, other, mine)
    upper_part = jnp.where(upper, mine, other)
    return jnp.concatenate([lower_part, upper_part], axis=axis_dim)


def ring_order(n):
    return list(range(0, n, 2)) + list(range(1, n, 2))[::-1]


def ring_source(c, hops, n):
    at = jnp.where(c % 2 == 0, c // 2, n - 1 - c // 2)
    at = (at - hops) % n
    return jnp.where(at < n // 2, 2 * at, 2 * (n - 1 - at) + 1)


def take(refs, *counts):
    out, at = [], 0
    for n in counts:
        out.append(refs[at : at + n])
        at += n
    return *out, refs[at:]


class Ring:
    def __init__(self, block, pieces):
        n = lax.axis_size("col")
        order = ring_order(n)
        self.n, self.hops = n, 0
        self.up = [(order[i], order[(i + 1) % n]) for i in range(n)]
        self.down = [(b, a) for a, b in self.up]
        self.rows = block.shape[0]
        self.found = [(lax.axis_index("col"), 0, block)]
        self.height = self.rows // pieces
        parts = [block[i * self.height : (i + 1) * self.height] for i in range(pieces)]
        self.last = [(p, p) for p in parts]

    def hop(self, beside=()):
        if self.hops == self.n // 2:
            return [], list(beside)
        c, half = self.found[0][0], self.rows // 2
        self.hops += 1
        found = []
        for i, (below, above) in enumerate(self.last):
            top = i * self.height
            firsts = [top, top]
            sends = [(below, self.up), (above, self.down)]
            if self.hops == self.n // 2:
                if len(self.last) == 1:
                    sends = [(below[:half], self.up), (above[half:], self.down)]
                    firsts = [0, half]
                else:
                    sends = [sends[0], None] if top < half else [None, sends[1]]
            got = [None if s is None else lax.ppermute(s[0], "col", s[1]) for s in sends]
            more = list(beside) if i == len(self.last) - 1 else []
            here = [g for g in got if g is not None]
            here, more = take(lax.optimization_barrier((*here, *more)), len(here))
            here = list(here)
            got = [None if g is None else here.pop(0) for g in got]
            self.last[i] = tuple(got)
            for way, piece in enumerate(got):
                if piece is not None:
                    hops = self.hops if way == 0 else -self.hops
                    found.append((ring_source(c, hops, self.n), firsts[way], piece))
        self.found += found
        return found, list(more)


def blank(shape):
    return pl.pallas_call(
        lambda o_ref: None,
        out_specs=pl.BlockSpec(memory_space=pl.ANY),
        out_shape=jax.ShapeDtypeStruct(shape, jnp.bfloat16),
    )()


def multiply(steps, a_buf, w_bufs, accs, a_sem, w_sem):
    for i, (left, rights) in enumerate(steps):
        pltpu.make_async_copy(left, a_buf.at[i], a_sem.at[i]).start()
        for g, chunks in enumerate(rights):
            at = 0
            for chunk in chunks:
                wide = chunk.shape[1]
                into = w_bufs[g].at[i, :, pl.ds(at, wide)]
                pltpu.make_async_copy(chunk, into, w_sem.at[g, i]).start()
                at += wide

    def body(i, carry):
        pltpu.make_async_copy(a_buf.at[i], a_buf.at[i], a_sem.at[i]).wait()
        for g, acc in enumerate(accs):
            pltpu.make_async_copy(w_bufs[g].at[i], w_bufs[g].at[i], w_sem.at[g, i]).wait()
            acc[...] += jnp.dot(a_buf[i], w_bufs[g][i], preferred_element_type=jnp.float32)
        return carry

    lax.fori_loop(0, len(steps), body, 0)


def project_kernel(near, far, chunks, first, heads, factor, panel_ref, *refs):
    near_refs, far_refs, (scale_ref, cos_ref, sin_ref), rest = take(refs, near, far * chunks, 3)
    o_ref, a_buf, w_buf, acc, a_sem, w_sem = rest
    slots, _, depth = panel_ref.shape
    per = slots // (near + far)
    cols = acc.shape[1]
    steps = []
    for k in range(slots):
        p, rows = k // per, pl.ds(k % per * depth, depth)
        if p < near:
            right = [near_refs[p].at[rows, pl.ds(first, cols)]]
        else:
            at = (p - near) * chunks
            right = [ref.at[rows, :] for ref in far_refs[at : at + chunks]]
        steps.append((panel_ref.at[k], [right]))
    acc[...] = jnp.zeros_like(acc)
    multiply(steps, a_buf, [w_buf], [acc], a_sem, w_sem)
    scale = scale_ref[...] * factor
    for h in range(cols // HD):
        at = pl.ds(h * HD, HD)
        x = acc[:, at] * scale
        if heads < 0 or h < heads:
            x = x * cos_ref[...] + pltpu.roll(x, HD // 2, 1) * sin_ref[...]
        o_ref[:, at] = x.astype(o_ref.dtype)


def project(panel, near, far, first, heads, factor, scale, cos, sin):
    slots, tok, depth = panel.shape
    chunks = len(far[0])
    cols = sum(w.shape[1] for w in far[0])
    hbm = pl.BlockSpec(memory_space=pl.ANY)
    vmem = pl.BlockSpec(memory_space=pltpu.VMEM)
    return pl.pallas_call(
        functools.partial(project_kernel, len(near), len(far), chunks, first, heads, factor),
        in_specs=[hbm] * (1 + len(near) + len(far) * chunks) + [vmem] * 3,
        out_specs=vmem,
        out_shape=jax.ShapeDtypeStruct((tok, cols), jnp.bfloat16),
        scratch_shapes=[
            pltpu.VMEM((slots, tok, depth), jnp.bfloat16),
            pltpu.VMEM((slots, depth, cols), jnp.bfloat16),
            pltpu.VMEM((tok, cols), jnp.float32),
            pltpu.SemaphoreType.DMA((slots,)),
            pltpu.SemaphoreType.DMA((1, slots)),
        ],
        compiler_params=pltpu.CompilerParams(vmem_limit_bytes=60 * MIB),
        cost_estimate=SHORT,
    )(panel, *near, *[w for pieces in far for w in pieces], scale, cos, sin)


def attend_kernel(parts, chunks, pair, r_ref, *refs):
    chunk_refs, pieces = refs[:chunks], refs[chunks : chunks + parts]
    o_ref, q_ref, turned, top, total, acc = refs[chunks + parts :]
    r = r_ref[0]
    tok = q_ref.shape[0]
    step = pl.program_id(0)
    per = pl.num_programs(0) // chunks
    for i in range(chunks):

        @pl.when(step // per == i)
        def _():
            q_ref[...] = chunk_refs[i][...]

    dims = (((1,), (1,)), ((), ()))

    @pl.when(step == 0)
    def _():
        for j in range(parts):
            turned[j] = pieces[j][:, HD:].T

    def scores(j, g):
        return lax.dot_general(
            pieces[j][:, :HD],
            q_ref[:, g * HD : (g + 1) * HD],
            dims,
            preferred_element_type=jnp.float32,
        )

    key = lax.broadcasted_iota(jnp.int32, (tok, tok), 0)
    query = lax.broadcasted_iota(jnp.int32, (tok, tok), 1)
    for g in range(pair):
        s = jnp.where(key <= query, scores(0, g), -jnp.inf)
        m = jnp.max(s, axis=0, keepdims=True)
        p = jnp.exp2(s - m)
        top[g] = m
        total[g] = jnp.sum(p, axis=0, keepdims=True)
        acc[g] = jnp.dot(turned[0], p.astype(jnp.bfloat16), preferred_element_type=jnp.float32)
    for j in range(1, parts):

        @pl.when(jnp.bitwise_xor(r, j) < r)
        def _():
            for g in range(pair):
                s = scores(j, g)
                m = jnp.maximum(top[g], jnp.max(s, axis=0, keepdims=True))
                keep = jnp.exp2(top[g] - m)
                p = jnp.exp2(s - m)
                top[g] = m
                total[g] = total[g] * keep + jnp.sum(p, axis=0, keepdims=True)
                acc[g] = acc[g] * keep + jnp.dot(
                    turned[j], p.astype(jnp.bfloat16), preferred_element_type=jnp.float32
                )

    for g in range(pair):
        o_ref[:, g * HD : (g + 1) * HD] = (acc[g] / total[g]).T.astype(o_ref.dtype)


def attend(r, queries, pieces):
    tok, cols = queries[0].shape
    chunks, parts = len(queries), len(pieces)
    pair = 2 if cols // HD % 2 == 0 else 1
    per = cols // (HD * pair)
    heads = chunks * cols // HD

    def query_spec(i):
        return pl.BlockSpec((tok, pair * HD), lambda h, r: (0, jnp.clip(h - i * per, 0, per - 1)))

    return pl.pallas_call(
        functools.partial(attend_kernel, parts, chunks, pair),
        grid_spec=pltpu.PrefetchScalarGridSpec(
            num_scalar_prefetch=1,
            grid=(chunks * per,),
            in_specs=[query_spec(i) for i in range(chunks)]
            + [pl.BlockSpec((tok, 2 * HD), lambda h, r: (0, 0)) for _ in pieces],
            out_specs=pl.BlockSpec((tok, pair * HD), lambda h, r: (0, h)),
            scratch_shapes=[
                pltpu.VMEM((tok, pair * HD), jnp.bfloat16),
                pltpu.VMEM((parts, HD, tok), jnp.bfloat16),
                pltpu.VMEM((pair, 1, tok), jnp.float32),
                pltpu.VMEM((pair, 1, tok), jnp.float32),
                pltpu.VMEM((pair, HD, tok), jnp.float32),
            ],
        ),
        out_shape=jax.ShapeDtypeStruct((tok, chunks * cols), jnp.bfloat16),
        compiler_params=pltpu.CompilerParams(
            dimension_semantics=("arbitrary",), vmem_limit_bytes=32 * MIB
        ),
        cost_estimate=SHORT,
    )(r.reshape(1), *queries, *pieces)


def finish_kernel(steps, per, rows, n_panels, near, others, r_ref, *refs):
    panels, near_refs, rest = take(refs, n_panels, near)
    gathered, (*old, o_ref, a_buf, w_buf, acc, a_sem, w_sem) = take(rest, others)
    depth = a_buf.shape[2]
    plan = []
    for g, k in steps:
        at = pl.ds(k % per * rows + g * depth, depth)
        if k // per < near:
            right = near_refs[k // per].at[at, :]
        else:
            right = gathered[0].at[jnp.bitwise_xor(r_ref[0], k // per), at, :]
        plan.append((panels[g].at[k], [[right]]))
    acc[...] = old[0][...] if old else jnp.zeros_like(acc)
    multiply(plan, a_buf, [w_buf], [acc], a_sem, w_sem)
    o_ref[...] = acc[...].astype(o_ref.dtype)


def finish(r, panels, steps, near, gathered, per, rows, dtype, total=None):
    _, tok, wide = panels[0].shape
    cols = near[0].shape[1]
    count = len(steps)
    others = [] if gathered is None else [gathered]
    old = [] if total is None else [total]
    hbm = pl.BlockSpec(memory_space=pl.ANY)
    vmem = pl.BlockSpec(memory_space=pltpu.VMEM)
    return pl.pallas_call(
        functools.partial(
            finish_kernel, steps, per, rows, len(panels), len(near), len(others)
        ),
        in_specs=[pl.BlockSpec(memory_space=pltpu.SMEM)]
        + [hbm] * (len(panels) + len(near) + len(others))
        + [vmem] * len(old),
        out_specs=vmem,
        out_shape=jax.ShapeDtypeStruct((tok, cols), dtype),
        scratch_shapes=[
            pltpu.VMEM((count, tok, wide), jnp.bfloat16),
            pltpu.VMEM((count, wide, cols), jnp.bfloat16),
            pltpu.VMEM((tok, cols), jnp.float32),
            pltpu.SemaphoreType.DMA((count,)),
            pltpu.SemaphoreType.DMA((1, count)),
        ],
        compiler_params=pltpu.CompilerParams(vmem_limit_bytes=60 * MIB),
        cost_estimate=SHORT,
    )(r.reshape(1), *panels, *near, *others, *old)


def per_device(hidden, norm_gain, wq, wk, wv, wo):
    tok, feat = hidden.shape
    n_row, n_col = lax.axis_size("row"), lax.axis_size("col")
    r, c = lax.axis_index("row"), lax.axis_index("col")
    depth = feat * n_col
    rows = wq.shape[0]
    cols = wq.shape[1]

    kv_cols = wk.shape[1]
    group = max(1, HD // kv_cols)
    stacked = jnp.stack((wk, wv), axis=1)
    for bit in range(group.bit_length() - 1):
        other = swap(stacked, "col", 1 << bit)
        stacked = order_pair(stacked, other, c, bit, 2)
    stacked = stacked.reshape(rows, 2 * HD)

    n_heads = cols // HD
    first_heads = n_heads // 2
    late_heads = n_heads - first_heads
    if n_heads >= 4:
        sizes = [first_heads // 2, first_heads - first_heads // 2]
        eighth = late_heads // 4
        sizes += [n for n in (eighth, late_heads - 2 * eighth, eighth) if n > 0]
    else:
        sizes = [first_heads, late_heads]
    early = 2 if n_heads >= 4 else 1
    wide, rest = first_heads * HD, late_heads * HD
    chunks = [
        wq[:, sum(sizes[:i]) * HD : sum(sizes[: i + 1]) * HD] for i in range(len(sizes))
    ]

    def by_block(far):
        return [list(pieces) for pieces in zip(*far)]

    half = HD // 2
    positions = r * tok + jnp.arange(tok)
    freqs = 10000.0 ** (-jnp.arange(half).astype(jnp.float32) / half)
    angles = positions.astype(jnp.float32)[:, None] * freqs[None, :]
    cosine, sine = jnp.cos(angles), jnp.sin(angles)
    cosine = jnp.concatenate([cosine, cosine], axis=1)
    sine = jnp.concatenate([-sine, sine], axis=1)
    factor = HD ** (-0.5) * math.log2(math.e)

    per = rows // feat

    def put(panel, found):
        for source, first, piece in found:
            slot = (source // per ^ r) * per + source % per
            panel = lax.dynamic_update_slice(panel, piece[None], (slot, first, 0))
        return panel

    def put_hidden(panel, squares, found):
        for source, first, piece in found:
            wider = piece.astype(jnp.float32)
            sums = jnp.sum(wider * wider, axis=1)
            for h in range(2):
                if first <= h * tok // 2 < first + piece.shape[0]:
                    at = h * tok // 2 - first
                    squares[h] += sums[at : at + tok // 2]
            gain = lax.dynamic_slice(norm_gain, (source * feat,), (feat,))
            panel = put(panel, [(source, first, (wider * gain).astype(jnp.bfloat16))])
        return panel, squares

    ring = Ring(hidden, 1)
    hops = n_col // 2
    x_sent = exchange(stacked)
    got_x = []
    zeros = [jnp.zeros((tok // 2,), jnp.float32)] * 2
    panel, squares = put_hidden(blank((n_col, tok, feat)), zeros, ring.found)
    for i in range(hops):
        last_hop = i == hops - 1
        tie = ring.last[0][1]
        sent = [] if x_sent is None else [x_sent]
        ahead = chunks[i : i + 1] if i < len(sizes) - 1 else []
        beside = [panel, *squares, cosine, sine, *sent, *ahead]
        if last_hop:
            near = gather_near(after(stacked, tie))
            kv_weights = [*near, *gather_near(after(got_x[0], tie))]
            beside += kv_weights
        found, beside = ring.hop(beside)
        (panel, *squares, cosine, sine), beside = take(beside, 5)
        panel, squares = put_hidden(panel, squares, found)
        sent, ahead, kv_weights = take(beside, len(sent), len(ahead))
        got_x += sent
        x_sent = exchange(ahead[0]) if ahead else None
    blocks_near = len(kv_weights) // 2
    kv_near, kv_far = take(kv_weights, blocks_near)
    scale = lax.rsqrt(jnp.concatenate(squares) / depth + 1e-05)[:, None]

    kv = project(panel, kv_near, by_block([kv_far]), 0, 1, 1.0, scale, cosine, sine)
    scale = after(scale, kv)
    q_far = [gather_near(after(x, *kv_weights)) for x in got_x[1 : 1 + early]]
    q_near = gather_near(after(wq, *kv_weights))
    queries = project(
        panel, q_near, by_block(q_far[:early]), 0, first_heads, factor, scale, cosine, sine
    )
    beside = [exchange(kv), queries, chunks[-1], *gather_near(kv)]
    if x_sent is not None:
        beside.append(x_sent)
    kv_other, queries, last_chunk, *beside = lax.optimization_barrier(tuple(beside))
    kv_pieces, arrived = take(beside, blocks_near)
    kv_pieces = [*kv_pieces, *gather_near(kv_other)]
    late_far = [list(gather_near(piece)) for piece in (*got_x[1 + early :], *arrived)]
    last_other = exchange(last_chunk)
    o_weights = lax.all_gather(after(wo, kv_other), "row")
    heads = attend(r, [queries], kv_pieces)

    ring = Ring(heads, 1)
    panels = [put(blank((n_col, tok, wide)), ring.found), blank((n_col, tok, rest))]
    tables = scale, cosine, sine
    late, first = [], wide
    if late_far:
        late.append(project(panel, q_near, by_block(late_far), first, -1, factor, *tables))
        first += late[0].shape[1]
    pending, (last_other, *beside) = ring.hop([last_other, *panels, *late])
    panels, late = take(beside, 2)
    last_far = by_block([gather_near(last_other)])
    late = [*late, project(panel, q_near, last_far, first, -1, factor, *tables)]
    late = jnp.concatenate(late, axis=1)
    found, (late,) = ring.hop([late])
    pending += found
    heads = attend(r, [late], kv_pieces)
    o_near = gather_near(after(wo, late))
    found, (heads, *o_near) = ring.hop([heads, *o_near])
    pending += found
    second = Ring(heads, 1)
    panels[1] = put(panels[1], second.found)
    half = n_col // 2
    for i in range(hops):
        found, _ = ring.hop()
        if i > 0:
            panels[0] = put(panels[0], pending)
            pending = []
        pending += found
        beside = panels
        if i == hops - 2:
            steps = [(0, k) for k in range(half)]
            total = finish(r, panels[:1], steps, o_near, None, per, cols, jnp.float32)
            beside = [*panels, total]
        found, beside = second.hop(beside)
        panels, beside = take(beside, 2)
        panels[1] = put(panels[1], found)
        if beside:
            (total,) = beside

    steps = [(1, k) for k in range(half)]
    total = finish(r, panels, steps, o_near, None, per, cols, jnp.float32, total)
    steps = [(g, k) for k in range(half, n_col) for g in (0, 1)]
    return finish(r, panels, steps, o_near, o_weights, per, cols, jnp.bfloat16, total)


def solution(mesh):
    in_specs = (
        P("row", "col"),
        P(),
        P("row", "col"),
        P("row", "col"),
        P("row", "col"),
        P("row", "col"),
    )
    out_specs = P("row", "col")
    return jax.shard_map(
        per_device, mesh=mesh, in_specs=in_specs, out_specs=out_specs, check_vma=False
    )
```

```python
import functools
import math

import jax
import jax.numpy as jnp
from jax import lax
from jax.experimental import pallas as pl
from jax.experimental.pallas import tpu as pltpu
from jax.sharding import PartitionSpec as P

HD = 128
MIB = 1 << 20
SHORT = pl.CostEstimate(flops=1, bytes_accessed=1, transcendentals=0)


def after(array, *earlier):
    if not earlier:
        return array
    return lax.optimization_barrier((array, *earlier))[0]


def swap(array, axis, mask):
    return lax.ppermute(array, axis, [(i, i ^ mask) for i in range(lax.axis_size(axis))])


def row_bits():
    return [1 << b for b in reversed(range((lax.axis_size("row")).bit_length() - 1))]


def exchange(array, *earlier):
    return swap(after(array, *earlier), "row", row_bits()[0])


def gather_near(array, *earlier):
    pieces = {0: after(array, *earlier)}
    for bit in row_bits()[1:]:
        pieces.update({j ^ bit: swap(p, "row", bit) for j, p in pieces.items()})
    return [pieces[j] for j in range(len(pieces))]


def order_pair(mine, other, col_index, bit, axis_dim):
    upper = col_index // 2**bit % 2 == 1
    lower_part = jnp.where(upper, other, mine)
    upper_part = jnp.where(upper, mine, other)
    return jnp.concatenate([lower_part, upper_part], axis=axis_dim)


def ring_order(n):
    return list(range(0, n, 2)) + list(range(1, n, 2))[::-1]


def ring_source(c, hops, n):
    at = jnp.where(c % 2 == 0, c // 2, n - 1 - c // 2)
    at = (at - hops) % n
    return jnp.where(at < n // 2, 2 * at, 2 * (n - 1 - at) + 1)


def take(refs, *counts):
    out, at = [], 0
    for n in counts:
        out.append(refs[at : at + n])
        at += n
    return *out, refs[at:]


class Ring:
    def __init__(self, block, pieces):
        n = lax.axis_size("col")
        order = ring_order(n)
        self.n, self.hops = n, 0
        self.up = [(order[i], order[(i + 1) % n]) for i in range(n)]
        self.down = [(b, a) for a, b in self.up]
        self.rows = block.shape[0]
        self.found = [(lax.axis_index("col"), 0, block)]
        self.height = self.rows // pieces
        parts = [block[i * self.height : (i + 1) * self.height] for i in range(pieces)]
        self.last = [(p, p) for p in parts]

    def hop(self, beside=()):
        if self.hops == self.n // 2:
            return [], list(beside)
        c, half = self.found[0][0], self.rows // 2
        self.hops += 1
        found = []
        for i, (below, above) in enumerate(self.last):
            top = i * self.height
            firsts = [top, top]
            sends = [(below, self.up), (above, self.down)]
            if self.hops == self.n // 2:
                if len(self.last) == 1:
                    sends = [(below[:half], self.up), (above[half:], self.down)]
                    firsts = [0, half]
                else:
                    sends = [sends[0], None] if top < half else [None, sends[1]]
            got = [None if s is None else lax.ppermute(s[0], "col", s[1]) for s in sends]
            more = list(beside) if i == len(self.last) - 1 else []
            here = [g for g in got if g is not None]
            here, more = take(lax.optimization_barrier((*here, *more)), len(here))
            here = list(here)
            got = [None if g is None else here.pop(0) for g in got]
            self.last[i] = tuple(got)
            for way, piece in enumerate(got):
                if piece is not None:
                    hops = self.hops if way == 0 else -self.hops
                    found.append((ring_source(c, hops, self.n), firsts[way], piece))
        self.found += found
        return found, list(more)


def blank(shape):
    return pl.pallas_call(
        lambda o_ref: None,
        out_specs=pl.BlockSpec(memory_space=pl.ANY),
        out_shape=jax.ShapeDtypeStruct(shape, jnp.bfloat16),
    )()


def multiply(steps, a_buf, w_bufs, accs, a_sem, w_sem):
    for i, (left, rights) in enumerate(steps):
        pltpu.make_async_copy(left, a_buf.at[i], a_sem.at[i]).start()
        for g, chunks in enumerate(rights):
            at = 0
            for chunk in chunks:
                wide = chunk.shape[1]
                into = w_bufs[g].at[i, :, pl.ds(at, wide)]
                pltpu.make_async_copy(chunk, into, w_sem.at[g, i]).start()
                at += wide

    def body(i, carry):
        pltpu.make_async_copy(a_buf.at[i], a_buf.at[i], a_sem.at[i]).wait()
        for g, acc in enumerate(accs):
            pltpu.make_async_copy(w_bufs[g].at[i], w_bufs[g].at[i], w_sem.at[g, i]).wait()
            acc[...] += jnp.dot(a_buf[i], w_bufs[g][i], preferred_element_type=jnp.float32)
        return carry

    lax.fori_loop(0, len(steps), body, 0)


def project_kernel(near, far, chunks, first, heads, factor, panel_ref, *refs):
    near_refs, far_refs, (scale_ref, cos_ref, sin_ref), rest = take(refs, near, far * chunks, 3)
    o_ref, a_buf, w_buf, acc, a_sem, w_sem = rest
    slots, _, depth = panel_ref.shape
    per = slots // (near + far)
    cols = acc.shape[1]
    steps = []
    for k in range(slots):
        p, rows = k // per, pl.ds(k % per * depth, depth)
        if p < near:
            right = [near_refs[p].at[rows, pl.ds(first, cols)]]
        else:
            at = (p - near) * chunks
            right = [ref.at[rows, :] for ref in far_refs[at : at + chunks]]
        steps.append((panel_ref.at[k], [right]))
    acc[...] = jnp.zeros_like(acc)
    multiply(steps, a_buf, [w_buf], [acc], a_sem, w_sem)
    scale = scale_ref[...] * factor
    for h in range(cols // HD):
        at = pl.ds(h * HD, HD)
        x = acc[:, at] * scale
        if heads < 0 or h < heads:
            x = x * cos_ref[...] + pltpu.roll(x, HD // 2, 1) * sin_ref[...]
        o_ref[:, at] = x.astype(o_ref.dtype)


def project(panel, near, far, first, heads, factor, scale, cos, sin):
    slots, tok, depth = panel.shape
    chunks = len(far[0])
    cols = sum(w.shape[1] for w in far[0])
    hbm = pl.BlockSpec(memory_space=pl.ANY)
    vmem = pl.BlockSpec(memory_space=pltpu.VMEM)
    return pl.pallas_call(
        functools.partial(project_kernel, len(near), len(far), chunks, first, heads, factor),
        in_specs=[hbm] * (1 + len(near) + len(far) * chunks) + [vmem] * 3,
        out_specs=vmem,
        out_shape=jax.ShapeDtypeStruct((tok, cols), jnp.bfloat16),
        scratch_shapes=[
            pltpu.VMEM((slots, tok, depth), jnp.bfloat16),
            pltpu.VMEM((slots, depth, cols), jnp.bfloat16),
            pltpu.VMEM((tok, cols), jnp.float32),
            pltpu.SemaphoreType.DMA((slots,)),
            pltpu.SemaphoreType.DMA((1, slots)),
        ],
        compiler_params=pltpu.CompilerParams(vmem_limit_bytes=60 * MIB),
        cost_estimate=SHORT,
    )(panel, *near, *[w for pieces in far for w in pieces], scale, cos, sin)


def attend_kernel(parts, chunks, pair, r_ref, *refs):
    chunk_refs, pieces = refs[:chunks], refs[chunks : chunks + parts]
    o_ref, q_ref, turned, top, total, acc = refs[chunks + parts :]
    r = r_ref[0]
    tok = q_ref.shape[0]
    step = pl.program_id(0)
    per = pl.num_programs(0) // chunks
    for i in range(chunks):

        @pl.when(step // per == i)
        def _():
            q_ref[...] = chunk_refs[i][...]

    dims = (((1,), (1,)), ((), ()))

    @pl.when(step == 0)
    def _():
        for j in range(parts):
            turned[j] = pieces[j][:, HD:].T

    def scores(j, g):
        return lax.dot_general(
            pieces[j][:, :HD],
            q_ref[:, g * HD : (g + 1) * HD],
            dims,
            preferred_element_type=jnp.float32,
        )

    key = lax.broadcasted_iota(jnp.int32, (tok, tok), 0)
    query = lax.broadcasted_iota(jnp.int32, (tok, tok), 1)
    for g in range(pair):
        s = jnp.where(key <= query, scores(0, g), -jnp.inf)
        m = jnp.max(s, axis=0, keepdims=True)
        p = jnp.exp2(s - m)
        top[g] = m
        total[g] = jnp.sum(p, axis=0, keepdims=True)
        acc[g] = jnp.dot(turned[0], p.astype(jnp.bfloat16), preferred_element_type=jnp.float32)
    for j in range(1, parts):

        @pl.when(jnp.bitwise_xor(r, j) < r)
        def _():
            for g in range(pair):
                s = scores(j, g)
                m = jnp.maximum(top[g], jnp.max(s, axis=0, keepdims=True))
                keep = jnp.exp2(top[g] - m)
                p = jnp.exp2(s - m)
                top[g] = m
                total[g] = total[g] * keep + jnp.sum(p, axis=0, keepdims=True)
                acc[g] = acc[g] * keep + jnp.dot(
                    turned[j], p.astype(jnp.bfloat16), preferred_element_type=jnp.float32
                )

    for g in range(pair):
        o_ref[:, g * HD : (g + 1) * HD] = (acc[g] / total[g]).T.astype(o_ref.dtype)


def attend(r, queries, pieces):
    tok, cols = queries[0].shape
    chunks, parts = len(queries), len(pieces)
    pair = 2 if cols // HD % 2 == 0 else 1
    per = cols // (HD * pair)
    heads = chunks * cols // HD

    def query_spec(i):
        return pl.BlockSpec((tok, pair * HD), lambda h, r: (0, jnp.clip(h - i * per, 0, per - 1)))

    return pl.pallas_call(
        functools.partial(attend_kernel, parts, chunks, pair),
        grid_spec=pltpu.PrefetchScalarGridSpec(
            num_scalar_prefetch=1,
            grid=(chunks * per,),
            in_specs=[query_spec(i) for i in range(chunks)]
            + [pl.BlockSpec((tok, 2 * HD), lambda h, r: (0, 0)) for _ in pieces],
            out_specs=pl.BlockSpec((tok, pair * HD), lambda h, r: (0, h)),
            scratch_shapes=[
                pltpu.VMEM((tok, pair * HD), jnp.bfloat16),
                pltpu.VMEM((parts, HD, tok), jnp.bfloat16),
                pltpu.VMEM((pair, 1, tok), jnp.float32),
                pltpu.VMEM((pair, 1, tok), jnp.float32),
                pltpu.VMEM((pair, HD, tok), jnp.float32),
            ],
        ),
        out_shape=jax.ShapeDtypeStruct((tok, chunks * cols), jnp.bfloat16),
        compiler_params=pltpu.CompilerParams(
            dimension_semantics=("arbitrary",), vmem_limit_bytes=32 * MIB
        ),
        cost_estimate=SHORT,
    )(r.reshape(1), *queries, *pieces)


def finish_kernel(steps, per, rows, n_panels, near, others, r_ref, *refs):
    panels, near_refs, rest = take(refs, n_panels, near)
    gathered, (*old, o_ref, a_buf, w_buf, acc, a_sem, w_sem) = take(rest, others)
    depth = a_buf.shape[2]
    plan = []
    for g, k in steps:
        at = pl.ds(k % per * rows + g * depth, depth)
        if k // per < near:
            right = near_refs[k // per].at[at, :]
        else:
            right = gathered[0].at[jnp.bitwise_xor(r_ref[0], k // per), at, :]
        plan.append((panels[g].at[k], [[right]]))
    acc[...] = old[0][...] if old else jnp.zeros_like(acc)
    multiply(plan, a_buf, [w_buf], [acc], a_sem, w_sem)
    o_ref[...] = acc[...].astype(o_ref.dtype)


def finish(r, panels, steps, near, gathered, per, rows, dtype, total=None):
    _, tok, wide = panels[0].shape
    cols = near[0].shape[1]
    count = len(steps)
    others = [] if gathered is None else [gathered]
    old = [] if total is None else [total]
    hbm = pl.BlockSpec(memory_space=pl.ANY)
    vmem = pl.BlockSpec(memory_space=pltpu.VMEM)
    return pl.pallas_call(
        functools.partial(
            finish_kernel, steps, per, rows, len(panels), len(near), len(others)
        ),
        in_specs=[pl.BlockSpec(memory_space=pltpu.SMEM)]
        + [hbm] * (len(panels) + len(near) + len(others))
        + [vmem] * len(old),
        out_specs=vmem,
        out_shape=jax.ShapeDtypeStruct((tok, cols), dtype),
        scratch_shapes=[
            pltpu.VMEM((count, tok, wide), jnp.bfloat16),
            pltpu.VMEM((count, wide, cols), jnp.bfloat16),
            pltpu.VMEM((tok, cols), jnp.float32),
            pltpu.SemaphoreType.DMA((count,)),
            pltpu.SemaphoreType.DMA((1, count)),
        ],
        compiler_params=pltpu.CompilerParams(vmem_limit_bytes=40 * MIB),
        cost_estimate=SHORT,
    )(r.reshape(1), *panels, *near, *others, *old)


def per_device(hidden, norm_gain, wq, wk, wv, wo):
    tok, feat = hidden.shape
    n_row, n_col = lax.axis_size("row"), lax.axis_size("col")
    r, c = lax.axis_index("row"), lax.axis_index("col")
    depth = feat * n_col
    rows = wq.shape[0]
    cols = wq.shape[1]

    kv_cols = wk.shape[1]
    group = max(1, HD // kv_cols)
    stacked = jnp.stack((wk, wv), axis=1)
    for bit in range(group.bit_length() - 1):
        other = swap(stacked, "col", 1 << bit)
        stacked = order_pair(stacked, other, c, bit, 2)
    stacked = stacked.reshape(rows, 2 * HD)

    n_heads = cols // HD
    first_heads = n_heads // 2
    late_heads = n_heads - first_heads
    if n_heads >= 4:
        sizes = [first_heads // 2, first_heads - first_heads // 2]
        eighth = late_heads // 4
        sizes += [n for n in (eighth, late_heads - 2 * eighth, eighth) if n > 0]
    else:
        sizes = [first_heads, late_heads]
    early = 2 if n_heads >= 4 else 1
    wide, rest = first_heads * HD, late_heads * HD
    chunks = [
        wq[:, sum(sizes[:i]) * HD : sum(sizes[: i + 1]) * HD] for i in range(len(sizes))
    ]

    def by_block(far):
        return [list(pieces) for pieces in zip(*far)]

    half = HD // 2
    positions = r * tok + jnp.arange(tok)
    freqs = 10000.0 ** (-jnp.arange(half).astype(jnp.float32) / half)
    angles = positions.astype(jnp.float32)[:, None] * freqs[None, :]
    cosine, sine = jnp.cos(angles), jnp.sin(angles)
    cosine = jnp.concatenate([cosine, cosine], axis=1)
    sine = jnp.concatenate([-sine, sine], axis=1)
    factor = HD ** (-0.5) * math.log2(math.e)

    per = rows // feat

    def put(panel, found):
        for source, first, piece in found:
            slot = (source // per ^ r) * per + source % per
            panel = lax.dynamic_update_slice(panel, piece[None], (slot, first, 0))
        return panel

    def put_hidden(panel, squares, found):
        for source, first, piece in found:
            wider = piece.astype(jnp.float32)
            sums = jnp.sum(wider * wider, axis=1)
            for h in range(2):
                if first <= h * tok // 2 < first + piece.shape[0]:
                    at = h * tok // 2 - first
                    squares[h] += sums[at : at + tok // 2]
            gain = lax.dynamic_slice(norm_gain, (source * feat,), (feat,))
            panel = put(panel, [(source, first, (wider * gain).astype(jnp.bfloat16))])
        return panel, squares

    ring = Ring(hidden, 1)
    hops = n_col // 2
    x_sent = exchange(stacked)
    got_x = []
    zeros = [jnp.zeros((tok // 2,), jnp.float32)] * 2
    panel, squares = put_hidden(blank((n_col, tok, feat)), zeros, ring.found)
    for i in range(hops):
        last_hop = i == hops - 1
        tie = ring.last[0][1]
        sent = [] if x_sent is None else [x_sent]
        ahead = chunks[i : i + 1] if i < len(sizes) - 1 else []
        beside = [panel, *squares, cosine, sine, *sent, *ahead]
        if last_hop:
            near = gather_near(after(stacked, tie))
            kv_weights = [*near, *gather_near(after(got_x[0], tie))]
            beside += kv_weights
        found, beside = ring.hop(beside)
        (panel, *squares, cosine, sine), beside = take(beside, 5)
        panel, squares = put_hidden(panel, squares, found)
        sent, ahead, kv_weights = take(beside, len(sent), len(ahead))
        got_x += sent
        x_sent = exchange(ahead[0]) if ahead else None
    blocks_near = len(kv_weights) // 2
    kv_near, kv_far = take(kv_weights, blocks_near)
    scale = lax.rsqrt(jnp.concatenate(squares) / depth + 1e-05)[:, None]

    kv = project(panel, kv_near, by_block([kv_far]), 0, 1, 1.0, scale, cosine, sine)
    scale = after(scale, kv)
    q_far = [gather_near(after(x, *kv_weights)) for x in got_x[1 : 1 + early]]
    q_near = gather_near(after(wq, *kv_weights))
    queries = project(
        panel, q_near, by_block(q_far[:early]), 0, first_heads, factor, scale, cosine, sine
    )
    beside = [exchange(kv), queries, chunks[-1], *gather_near(kv)]
    if x_sent is not None:
        beside.append(x_sent)
    kv_other, queries, last_chunk, *beside = lax.optimization_barrier(tuple(beside))
    kv_pieces, arrived = take(beside, blocks_near)
    kv_pieces = [*kv_pieces, *gather_near(kv_other)]
    late_far = [list(gather_near(piece)) for piece in (*got_x[1 + early :], *arrived)]
    last_other = exchange(last_chunk)
    o_weights = lax.all_gather(after(wo, kv_other), "row")
    heads = attend(r, [queries], kv_pieces)

    ring = Ring(heads, 1)
    panels = [put(blank((n_col, tok, wide)), ring.found), blank((n_col, tok, rest))]
    tables = scale, cosine, sine
    late, first = [], wide
    if late_far:
        late.append(project(panel, q_near, by_block(late_far), first, -1, factor, *tables))
        first += late[0].shape[1]
    found, (last_other, *beside) = ring.hop([last_other, *panels, *late])
    panels, late = take(beside, 2)
    panels[0] = put(panels[0], found)
    last_far = by_block([gather_near(last_other)])
    late = [*late, project(panel, q_near, last_far, first, -1, factor, *tables)]
    late = jnp.concatenate(late, axis=1)
    found, (late, panels[0]) = ring.hop([late, panels[0]])
    panels[0] = put(panels[0], found)
    heads = attend(r, [late], kv_pieces)
    o_near = gather_near(after(wo, late))
    found, (heads, panels[0], *o_near) = ring.hop([heads, panels[0], *o_near])
    panels[0] = put(panels[0], found)
    second = Ring(heads, 1)
    panels[1] = put(panels[1], second.found)
    half = n_col // 2
    for i in range(hops):
        found, (panels[0],) = ring.hop([panels[0]])
        panels[0] = put(panels[0], found)
        beside = [panels[1]]
        if i == hops - 1:
            steps = [(0, k) for k in range(half)]
            beside.append(finish(r, panels[:1], steps, o_near, None, per, cols, jnp.float32))
        found, (panels[1], *beside) = second.hop(beside)
        panels[1] = put(panels[1], found)
    (total,) = beside

    steps = [(1, k) for k in range(half)] + [(g, k) for k in range(half, n_col) for g in (0, 1)]
    return finish(r, panels, steps, o_near, o_weights, per, cols, jnp.bfloat16, total)


def solution(mesh):
    in_specs = (
        P("row", "col"),
        P(),
        P("row", "col"),
        P("row", "col"),
        P("row", "col"),
        P("row", "col"),
    )
    out_specs = P("row", "col")
    return jax.shard_map(
        per_device, mesh=mesh, in_specs=in_specs, out_specs=out_specs, check_vma=False
    )
```
